128 devices in a mesh: bucket: 4 (over x), dp: 32 (over y, z, core).
Axes of the slice: x: 4, y: 4, z: 4, core: 2. Of those that a mesh axis runs over, the one named last changes fastest.
Arguments:
- queries: bfloat16 [4, 32, 1024, 1024], P('bucket', 'dp'), may hold values from -10 to 10
- bucket_ids: int32 [4, 32, 1024], P('bucket', 'dp'), may hold values from 0 to 3, as said below
- raw_passages: bfloat16 [4, 32, 192, 1024], P('bucket', 'dp'), may hold values from -8 to 8
- counts: int32 [4, 32], P('bucket', 'dp'), may hold values from 1 to 192, 2048 in all within a row
- teacher: bfloat16 [4, 32, 1024, 2048], P('bucket', 'dp'), may hold values from -16 to 320
Outputs:
- grad_queries: bfloat16 [4, 32, 1024, 1024], P('bucket', 'dp')
- grad_passages: bfloat16 [4, 2048, 1024], P('bucket', 'dp')
- kl_rows: float32 [4, 32, 1024], P('bucket', 'dp')
The draws below stay inside these ranges and needn't reach their ends.
Inputs may be any that keep to these rules, and one draw needn't show every extreme that they name: `bucket_ids`: each device holds exactly 256 queries of each language. The counts of one language sum to 2048, and in every language one device holds exactly 192.
All inputs are finite; a program needn't handle non-finite values.
Results may differ from the reference program's by a relative error of at most 0.0075.
Values may be sent and summed in bfloat16 or wider, within the bound.
No kernel may reach another device: no remote copies, remote signals or barrier semaphores. Data moves between devices by JAX's collectives and lax.ppermute only.
A program may use at most 128 MiB of HBM per device.

```python
import math
import jax
import jax.numpy as jnp
import numpy as np
from jax import lax

D = 1024
Q_DEV = 1024
BUCKETS = 4
HOLDERS = 32
QB = 256
CAP = 192
NP = 2048


def language_ids(key):
    key = jax.random.fold_in(key, 101)
    scores = jax.random.randint(key, (BUCKETS, HOLDERS, Q_DEV), 0, 1 << 19, dtype=jnp.int32) * Q_DEV + jnp.arange(Q_DEV, dtype=jnp.int32)
    ordering = jnp.argsort(scores, axis=-1)
    return (ordering // QB).astype(jnp.int32)


def passage_parts(key):
    key = jax.random.fold_in(key, 102)
    first = jax.random.fold_in(key, 0)
    shape = (BUCKETS, HOLDERS, CAP, D)
    normal_rows = jax.random.truncated_normal(first, -6.0, 6.0, shape, jnp.float32)
    return normal_rows


def draw_raw_passages(key, part):
    normal_rows = passage_parts(key)
    result = normal_rows
    return result.astype(jnp.bfloat16)


def draw_bucket_ids(key, part):
    identity = language_ids(key)
    return identity


def draw_queries(key, part):
    key = jax.random.fold_in(key, 4)
    shape = (BUCKETS, HOLDERS, Q_DEV, D)
    result = jax.random.truncated_normal(key, -6.0, 6.0, shape, jnp.float32)
    return result.astype(jnp.bfloat16)


def draw_teacher(key, part):
    key = jax.random.fold_in(key, 5)
    shape = (BUCKETS, HOLDERS, Q_DEV, NP)
    result = 3.0 * jax.random.truncated_normal(key, -5.0, 5.0, shape, jnp.float32)
    return result.astype(jnp.bfloat16)


def profile(amount, total, reach, skew):
    portions = [(1 << 20) // math.isqrt(rank ** skew) + 1 for rank in range(2, amount + 1)]
    surplus, given = total - reach - (amount - 1), [1] * (amount - 1)
    while surplus > 0:
        candidates = [i for i in range(amount - 1) if given[i] < reach]
        pool, budget = sum([portions[i] for i in candidates]), surplus
        for i in candidates:
            extra = min(reach - given[i], max(1, budget * portions[i] // pool), surplus)
            given[i] = given[i] + extra
            surplus = surplus - extra
    return np.array([reach] + given)


def ragged(own_key, number_of, total, limit, lean):
    if number_of == 2:
        one = jax.random.randint(own_key, (), max(1, total - limit), min(limit, total - 1) + 1)
        return jnp.stack([one, total - one])
    tallies = jnp.asarray(profile(number_of, total, limit, lean), jnp.int32)
    couples = (number_of - 1) // 2
    donor, taker = tallies[1:1 + 2 * couples:2], tallies[2:2 + 2 * couples:2]
    room = jnp.minimum(donor - 1, limit - taker)
    shifted = jax.random.randint(jax.random.fold_in(own_key, 1), (couples,), 0, 1 << 20) % (room + 1)
    tallies = tallies.at[1:1 + 2 * couples:2].set(donor - shifted).at[2:2 + 2 * couples:2].set(taker + shifted)
    return tallies[jax.random.permutation(jax.random.fold_in(own_key, 2), number_of)]


def setup_inputs(seed: int = 0) -> dict:
    arg_keys = jax.random.split(jax.random.key(seed), 6)
    return {
        "queries": draw_queries(jax.random.fold_in(arg_keys[5], 71), 0),
        "bucket_ids": draw_bucket_ids(jax.random.fold_in(arg_keys[5], 71), 0),
        "raw_passages": draw_raw_passages(jax.random.fold_in(arg_keys[5], 71), 0),
        "counts": jax.vmap(lambda own: ragged(own, HOLDERS, NP, CAP, 2))(jax.random.split(arg_keys[3], BUCKETS)).reshape((BUCKETS, HOLDERS)).astype(jnp.int32),
        "teacher": draw_teacher(jax.random.fold_in(arg_keys[5], 71), 0),
    }


student_scale = 0.1


def arrange(raw_rows, counts_row):
    counts_row = counts_row.astype(jnp.int32)
    offsets = (jnp.cumsum(counts_row) - counts_row).astype(jnp.int32)
    places = jnp.arange(NP, dtype=jnp.int32)
    started = offsets[None, :] <= places[:, None]
    holder = (jnp.sum(started.astype(jnp.int32), axis=1) - 1).astype(jnp.int32)
    opening = jnp.max(jnp.where(started, offsets[None, :], jnp.int32(0)), axis=1).astype(jnp.int32)
    flat_rows = raw_rows.reshape(HOLDERS * CAP, D)
    return flat_rows[holder * CAP + places - opening]


def row_terms(query_block, teacher_block, passages):
    scores = lax.dot_general(query_block, passages, (((1,), (1,)), ((), ())), preferred_element_type=jnp.float32) * student_scale
    row_top = jnp.max(scores, axis=1, keepdims=True)
    log_total = row_top + jnp.log(jnp.sum(jnp.exp(scores - row_top), axis=1, keepdims=True))
    teacher_float = teacher_block.astype(jnp.float32)
    teacher_top = jnp.max(teacher_float, axis=1, keepdims=True)
    teacher_log = teacher_float - teacher_top - jnp.log(jnp.sum(jnp.exp(teacher_float - teacher_top), axis=1, keepdims=True))
    teacher_prob = jnp.exp(teacher_log)
    diverge = jnp.sum(teacher_prob * teacher_log, axis=1) - jnp.sum(teacher_prob * scores, axis=1) + log_total[:, 0]
    weights = (student_scale * (jnp.exp(scores - log_total) - teacher_prob)).astype(jnp.bfloat16)
    return diverge, weights


def reference(queries, bucket_ids, raw_passages, counts, teacher):
    identity = bucket_ids.astype(jnp.int32)
    languages = jnp.arange(BUCKETS, dtype=jnp.int32)
    one_hot = (identity[..., None] == languages).astype(jnp.int32)
    ranking = (jnp.sum(jnp.cumsum(one_hot, axis=2) * one_hot, axis=3) - 1).astype(jnp.int32)
    slot_index = (identity * QB + ranking).astype(jnp.int32)
    ordering = jnp.argsort(slot_index, axis=2).astype(jnp.int32)
    sorted_queries = jnp.take_along_axis(queries, ordering[..., None], axis=2)
    sorted_teacher = jnp.take_along_axis(teacher, ordering[..., None], axis=2)
    diverge_parts = []
    grad_parts = []
    passage_grads = []
    for language in range(BUCKETS):
        lang_queries = sorted_queries[:, :, language * QB:(language + 1) * QB].reshape(HOLDERS, Q_DEV, D)
        lang_teacher = sorted_teacher[:, :, language * QB:(language + 1) * QB].reshape(HOLDERS, Q_DEV, NP)
        passages = arrange(raw_passages[language], counts[language])

        def step_fn(running, blocks):
            diverge, weights = row_terms(blocks[0], blocks[1], passages)
            query_grad = jnp.dot(weights, passages, preferred_element_type=jnp.float32)
            passage_term = lax.dot_general(weights, blocks[0], (((0,), (0,)), ((), ())), preferred_element_type=jnp.float32)
            return running + passage_term, (diverge, query_grad)

        running, outputs = lax.scan(step_fn, jnp.zeros((NP, D), jnp.float32), (lang_queries, lang_teacher))
        diverge_parts.append(outputs[0].reshape(BUCKETS, HOLDERS, QB))
        grad_parts.append(outputs[1].reshape(BUCKETS, HOLDERS, QB, D))
        passage_grads.append(running.astype(jnp.bfloat16))
    diverge_sorted = jnp.stack(diverge_parts, axis=2).reshape(BUCKETS, HOLDERS, Q_DEV)
    grad_sorted = jnp.stack(grad_parts, axis=2).reshape(BUCKETS, HOLDERS, Q_DEV, D)
    kl_rows = jnp.take_along_axis(diverge_sorted, slot_index, axis=2)
    grad_queries = jnp.take_along_axis(grad_sorted, slot_index[..., None], axis=2).astype(jnp.bfloat16)
    grad_passages = jnp.stack(passage_grads, axis=0)
    return grad_queries, grad_passages, kl_rows
```

```python
import jax
import jax.numpy as jnp
from jax import lax
from jax.experimental import pallas as pl
from jax.experimental.pallas import tpu as pltpu
from jax.sharding import Mesh
from jax.sharding import PartitionSpec as P

student_scale = 0.1
languages = 4
holders = 32
capacity = 192
count_rows = 8
width = 1024
per_device = 1024
per_language = 256
passages_all = 2048
both = width + passages_all
window = 208
extra = 128
mib = 1024 * 1024


def slots_of(ids, here):
    turned = lax.rem(ids - here + languages, languages)
    hot = turned == lax.broadcasted_iota(jnp.int32, (8, per_device), 0)
    earlier = lax.broadcasted_iota(jnp.int32, (per_device, per_device), 0)
    later = lax.broadcasted_iota(jnp.int32, (per_device, per_device), 1)
    upper = (earlier <= later).astype(jnp.float32).astype(jnp.bfloat16)
    hot = hot.astype(jnp.float32)
    ranks = jnp.dot(hot.astype(jnp.bfloat16), upper, preferred_element_type=jnp.float32)
    first = lax.broadcasted_iota(jnp.int32, (8, per_device), 0).astype(jnp.float32) * per_language
    return jnp.sum(hot * (ranks - 1.0 + first), axis=0, keepdims=True).astype(jnp.int32)


def sort_kernel(here, ids, queries, teacher, out0, out1, out2, out3, slot, select):
    step = pl.program_id(0)

    @pl.when(step == 0)
    def _():
        slots = slots_of(ids[...], here[0])
        slot[...] = jnp.broadcast_to(slots, (8, per_device))
        rows = lax.broadcasted_iota(jnp.int32, (per_device, per_device), 0)
        select[...] = (rows == slots).astype(jnp.float32).astype(jnp.bfloat16)

    def move(block):
        for number, out in enumerate((out0, out1, out2, out3)):
            chosen = select[number * per_language : (number + 1) * per_language, :]
            out[...] = jnp.dot(chosen, block, preferred_element_type=jnp.float32).astype(
                jnp.bfloat16
            )

    @pl.when(step < 2)
    def _():
        move(queries[...])

    @pl.when(step >= 2)
    def _():
        move(teacher[...])


def sort_rows(here, ids, queries, teacher):
    tile = 512
    block = jax.ShapeDtypeStruct((per_language, both), jnp.bfloat16)
    out_block = pl.BlockSpec((per_language, tile), lambda j, here: (0, j))
    return pl.pallas_call(
        sort_kernel,
        grid_spec=pltpu.PrefetchScalarGridSpec(
            num_scalar_prefetch=1,
            grid=(both // tile,),
            in_specs=[
                pl.BlockSpec((1, per_device), lambda j, here: (0, 0)),
                pl.BlockSpec((per_device, tile), lambda j, here: (0, jnp.minimum(j, 1))),
                pl.BlockSpec((per_device, tile), lambda j, here: (0, jnp.maximum(j - 2, 0))),
            ],
            out_specs=[out_block] * 4
            + [pl.BlockSpec((8, per_device), lambda j, here: (0, 0))],
            scratch_shapes=[pltpu.VMEM((per_device, per_device), jnp.bfloat16)],
        ),
        out_shape=[block] * 4 + [jax.ShapeDtypeStruct((8, per_device), jnp.int32)],
        compiler_params=pltpu.CompilerParams(vmem_limit_bytes=40 * mib),
        cost_estimate=pl.CostEstimate(
            flops=2 * per_device * per_device * both, bytes_accessed=12 * mib, transcendentals=0
        ),
        name="sort_rows",
    )(here, ids, queries, teacher)


def weigh_kernel(
    offsets, counts, core, raw, in0, in1, in2, in3, send, keep, weights_out, passages_out, kl,
    raw_v, passages, queries, teacher, scores, weights, raw_sem, in_sem, out_sem,
):
    def raw_copy(h):
        return pltpu.make_async_copy(
            raw.at[h, pl.ds(0, capacity)], raw_v.at[h], raw_sem.at[h]
        )

    def start_raw(h, carry):
        raw_copy(h).start()
        return carry

    lax.fori_loop(0, holders, start_raw, 0)
    copies = []
    for number, block in enumerate((in0, in1, in2, in3)):
        rows = pl.ds(number * per_language, per_language)
        copies.append(
            pltpu.make_async_copy(
                block.at[:, pl.ds(0, width)], queries.at[rows], in_sem.at[2 * number]
            )
        )
        copies.append(
            pltpu.make_async_copy(
                block.at[:, pl.ds(width, passages_all)], teacher.at[rows], in_sem.at[2 * number + 1]
            )
        )
    for copy in copies:
        copy.start()

    passages[pl.ds(0, 16), :] = jnp.zeros((16, width), jnp.bfloat16)

    def place(h, carry):
        raw_copy(h).wait()
        offset = offsets[h]
        start = pl.multiple_of((offset // 16) * 16, 16)
        target = lax.broadcasted_iota(jnp.int32, (window, capacity), 0)
        source = lax.broadcasted_iota(jnp.int32, (window, capacity), 1)
        hit = (target == source + (offset - start)) & (source < counts[h])
        chosen = hit.astype(jnp.float32).astype(jnp.bfloat16)
        moved = jnp.dot(chosen, raw_v[h], preferred_element_type=jnp.float32).astype(jnp.bfloat16)
        head = passages[pl.ds(start, 16), :]
        passages[pl.ds(start, 16), :] = head + moved[:16]
        passages[pl.ds(start + 16, window - 16), :] = moved[16:]
        return carry

    lax.fori_loop(0, holders, place, 0)
    passage_copy = pltpu.make_async_copy(
        passages.at[pl.ds(0, passages_all)], passages_out, out_sem.at[4]
    )
    passage_copy.start()

    out_copies = []
    for number in range(languages):
        base = number * per_language
        copies[2 * number].wait()
        copies[2 * number + 1].wait()
        block_queries = queries[base : base + per_language, :]

        def score(j, carry):
            columns = pl.ds(pl.multiple_of(j * 512, 512), 512)
            scores[:, columns] = lax.dot_general(
                block_queries,
                passages[columns, :],
                (((1,), (1,)), ((), ())),
                preferred_element_type=jnp.float32,
            ) * student_scale
            return carry

        lax.fori_loop(0, passages_all // 512, score, 0)

        def rows_of(i, carry):
            local = pl.ds(pl.multiple_of(i * 16, 16), 16)
            placed = pl.ds(pl.multiple_of(base + i * 16, 16), 16)
            own = scores[local, :]
            taught = teacher[placed, :].astype(jnp.float32)
            top = jnp.max(own, axis=1, keepdims=True)
            taught_top = jnp.max(taught, axis=1, keepdims=True)
            grown = jnp.exp(own - top)
            total = jnp.sum(grown, axis=1, keepdims=True)
            shifted = taught - taught_top
            taught_grown = jnp.exp(shifted)
            taught_total = jnp.sum(taught_grown, axis=1, keepdims=True)
            cross = jnp.sum(taught_grown * (shifted - own), axis=1, keepdims=True)
            diverge = cross / taught_total - jnp.log(taught_total) + top + jnp.log(total)
            weights[placed, :] = (
                grown * (student_scale / total) - taught_grown * (student_scale / taught_total)
            ).astype(jnp.bfloat16)
            kl[placed, :] = jnp.broadcast_to(diverge, (16, 128))
            return carry

        lax.fori_loop(0, per_language // 16, rows_of, 0)
        rows = pl.ds(base, per_language)
        copy = pltpu.make_async_copy(weights.at[rows], weights_out.at[rows], out_sem.at[number])
        copy.start()
        out_copies.append(copy)

    even = core[0] == 0

    def reduce(j, carry):
        columns = pl.ds(pl.multiple_of(j * 256, 256), 256)
        grad = lax.dot_general(
            weights[:, columns],
            queries[...],
            (((0,), (0,)), ((), ())),
            preferred_element_type=jnp.float32,
        ).astype(jnp.bfloat16)
        for part in range(2):
            upper = grad[part * 128 : part * 128 + 64]
            lower = grad[part * 128 + 64 : part * 128 + 128]
            rows = pl.ds(pl.multiple_of(j * 128 + part * 64, 64), 64)
            keep[rows, :] = jnp.where(even, upper, lower)
            send[rows, :] = jnp.where(even, lower, upper)
        return carry

    lax.fori_loop(0, passages_all // 256, reduce, 0)
    passage_copy.wait()
    for copy in out_copies:
        copy.wait()


def weigh(offsets, counts, core, raw, blocks):
    smem = pl.BlockSpec(memory_space=pltpu.SMEM)
    anywhere = pl.BlockSpec(memory_space=pl.ANY)
    vmem = pl.BlockSpec(memory_space=pltpu.VMEM)
    half = jax.ShapeDtypeStruct((passages_all // 2, width), jnp.bfloat16)
    return pl.pallas_call(
        weigh_kernel,
        in_specs=[smem] * 3 + [anywhere] * 5,
        out_specs=[vmem, vmem, anywhere, anywhere, vmem],
        out_shape=[
            half,
            half,
            jax.ShapeDtypeStruct((per_device, passages_all), jnp.bfloat16),
            jax.ShapeDtypeStruct((passages_all, width), jnp.bfloat16),
            jax.ShapeDtypeStruct((per_device, 128), jnp.float32),
        ],
        scratch_shapes=[
            pltpu.VMEM((holders, capacity, width), jnp.bfloat16),
            pltpu.VMEM((passages_all + 256, width), jnp.bfloat16),
            pltpu.VMEM((per_device, width), jnp.bfloat16),
            pltpu.VMEM((per_device, passages_all), jnp.bfloat16),
            pltpu.VMEM((per_language, passages_all), jnp.float32),
            pltpu.VMEM((per_device, passages_all), jnp.bfloat16),
            pltpu.SemaphoreType.DMA((holders,)),
            pltpu.SemaphoreType.DMA((8,)),
            pltpu.SemaphoreType.DMA((5,)),
        ],
        compiler_params=pltpu.CompilerParams(vmem_limit_bytes=56 * mib),
        cost_estimate=pl.CostEstimate(
            flops=12 * 1024**3, bytes_accessed=32 * mib, transcendentals=4 * mib
        ),
        name="weigh",
    )(offsets, counts, core, raw, *blocks)


def query_kernel(weights, passages, kl, out0, out1, out2, out3):
    step = pl.program_id(0)
    grad = jnp.dot(weights[...], passages[...], preferred_element_type=jnp.float32)
    value = kl[...]
    high = value.astype(jnp.bfloat16).astype(jnp.float32)
    middle = (value - high).astype(jnp.bfloat16).astype(jnp.float32)
    low = value - high - middle
    lane = lax.broadcasted_iota(jnp.int32, (per_language, extra), 1)
    parts = jnp.where(
        lane == 0, high, jnp.where(lane == 1, middle, jnp.where(lane == 2, low, 0.0))
    )
    for number, out in enumerate((out0, out1, out2, out3)):

        @pl.when(step == number)
        def _(out=out):
            out[:, :width] = grad.astype(jnp.bfloat16)
            out[:, width:] = parts.astype(jnp.bfloat16)


def query_grads(weights, passages, kl):
    block = jax.ShapeDtypeStruct((per_language, width + extra), jnp.bfloat16)
    return pl.pallas_call(
        query_kernel,
        grid=(languages,),
        in_specs=[
            pl.BlockSpec((per_language, passages_all), lambda i: (i, 0)),
            pl.BlockSpec((passages_all, width), lambda i: (0, 0)),
            pl.BlockSpec((per_language, 128), lambda i: (i, 0)),
        ],
        out_specs=[pl.BlockSpec((per_language, width + extra), lambda i: (0, 0))] * 4,
        out_shape=[block] * 4,
        compiler_params=pltpu.CompilerParams(vmem_limit_bytes=40 * mib),
        cost_estimate=pl.CostEstimate(
            flops=4 * 1024**3, bytes_accessed=12 * mib, transcendentals=0
        ),
        name="query_grads",
    )(weights, passages, kl)


def restore_kernel(slot, in0, in1, in2, in3, grads, kl, select):
    rows = lax.broadcasted_iota(jnp.int32, (per_device, per_device), 0)
    slots = slot[0:1, :]
    select[...] = (rows == slots).astype(jnp.float32).astype(jnp.bfloat16)
    total = jnp.zeros((per_device, 128), jnp.float32)
    contract = (((0,), (0,)), ((), ()))
    for j in range(4):
        columns = slice(j * 256, (j + 1) * 256)
        part = jnp.zeros((per_device, 256), jnp.float32)
        for number, block in enumerate((in0, in1, in2, in3)):
            chosen = select[number * per_language : (number + 1) * per_language, :]
            part += lax.dot_general(
                chosen, block[:, columns], contract, preferred_element_type=jnp.float32
            )
        grads[:, columns] = part.astype(jnp.bfloat16)
    for number, block in enumerate((in0, in1, in2, in3)):
        chosen = select[number * per_language : (number + 1) * per_language, :]
        total += lax.dot_general(
            chosen, block[:, width:], contract, preferred_element_type=jnp.float32
        )
    column = jnp.sum(total, axis=1, keepdims=True)
    kl[...] = jnp.transpose(jnp.broadcast_to(column, (per_device, 128)))[:8]


def restore(slot, blocks):
    vmem = pl.BlockSpec(memory_space=pltpu.VMEM)
    return pl.pallas_call(
        restore_kernel,
        in_specs=[vmem] * 5,
        out_specs=[vmem, vmem],
        out_shape=[
            jax.ShapeDtypeStruct((per_device, width), jnp.bfloat16),
            jax.ShapeDtypeStruct((8, per_device), jnp.float32),
        ],
        scratch_shapes=[pltpu.VMEM((per_device, per_device), jnp.bfloat16)],
        compiler_params=pltpu.CompilerParams(vmem_limit_bytes=40 * mib),
        cost_estimate=pl.CostEstimate(
            flops=2 * 1024**3, bytes_accessed=6 * mib, transcendentals=0
        ),
        name="restore",
    )(slot, *blocks)


def shift(array, by):
    pairs = [(i, (i + by) % languages) for i in range(languages)]
    return lax.ppermute(array, "x", pairs)


def on_device(queries, bucket_ids, raw_passages, counts, teacher):
    group = ("y", "z", "c")
    here = lax.axis_index("x").astype(jnp.int32).reshape(1)
    core = lax.axis_index("c").astype(jnp.int32).reshape(1)
    count_block = jnp.broadcast_to(counts[0, 0].astype(jnp.bfloat16), (1, count_rows, width))
    labelled = jnp.concatenate([raw_passages[0], count_block], axis=1)
    all_raw = lax.all_gather(labelled, group, axis=0, tiled=True)
    *outgoing, slot = sort_rows(here, bucket_ids[0], queries[0, 0], teacher[0, 0])
    blocks = [outgoing[0]] + [shift(outgoing[d], d) for d in range(1, languages)]
    holder_counts = all_raw[:, capacity, 0].astype(jnp.int32)
    earlier = jnp.arange(holders)[None, :] < jnp.arange(holders)[:, None]
    offsets = jnp.sum(jnp.where(earlier, holder_counts[None, :], 0), axis=1).astype(jnp.int32)
    send, keep, weights, passages, kl = weigh(offsets, holder_counts, core, all_raw, blocks)
    other = lax.ppermute(send, "c", [(0, 1), (1, 0)])
    paired = (keep.astype(jnp.float32) + other.astype(jnp.float32)).astype(jnp.bfloat16)
    spread = lax.all_to_all(
        paired.reshape(16, 64, width), ("y", "z"), split_axis=0, concat_axis=0, tiled=True
    )
    grad_passages = jnp.sum(spread.astype(jnp.float32), axis=0).astype(jnp.bfloat16)
    returning = query_grads(weights, passages, kl)
    back = [returning[0]] + [shift(returning[d], -d) for d in range(1, languages)]
    grad_queries, kl_rows = restore(slot, back)
    return (grad_queries[None, None], grad_passages[None], kl_rows[0][None, None])


def solution(mesh):
    split = Mesh(mesh.devices.reshape(4, 4, 4, 2), ("x", "y", "z", "c"))
    group = ("y", "z", "c")
    in_specs = (
        P("x", group, None, None),
        P("x", group, None),
        P("x", group, None, None),
        P("x", group),
        P("x", group, None, None),
    )
    out_specs = (P("x", group, None, None), P("x", group, None), P("x", group, None))
    return jax.shard_map(
        on_device, mesh=split, in_specs=in_specs, out_specs=out_specs, check_vma=False
    )
```

```python
import functools

import jax
import jax.numpy as jnp
from jax import lax
from jax.experimental import pallas as pl
from jax.experimental.pallas import tpu as pltpu
from jax.sharding import Mesh
from jax.sharding import PartitionSpec as P

student_scale = 0.1
languages = 4
holders = 32
capacity = 192
width = 1024
per_device = 1024
per_language = 256
passages_all = 2048
both = width + passages_all
window = 208
extra = 128
mib = 1024 * 1024


def slots_of(ids, here):
    turned = lax.rem(ids - here + languages, languages)
    hot = turned == lax.broadcasted_iota(jnp.int32, (8, per_device), 0)
    earlier = lax.broadcasted_iota(jnp.int32, (per_device, per_device), 0)
    later = lax.broadcasted_iota(jnp.int32, (per_device, per_device), 1)
    upper = (earlier <= later).astype(jnp.float32).astype(jnp.bfloat16)
    hot = hot.astype(jnp.float32)
    ranks = jnp.dot(hot.astype(jnp.bfloat16), upper, preferred_element_type=jnp.float32)
    first = lax.broadcasted_iota(jnp.int32, (8, per_device), 0).astype(jnp.float32) * per_language
    return jnp.sum(hot * (ranks - 1.0 + first), axis=0, keepdims=True).astype(jnp.int32)


def sort_kernel(first, number, here, ids, slot_in, queries, teacher, out, slot, select):
    step = pl.program_id(0)

    @pl.when(step == 0)
    def _():
        if first:
            slots = slots_of(ids[...], here[0])
            slot[...] = jnp.broadcast_to(slots, (8, per_device))
        else:
            slots = slot_in[0:1, :]
            slot[...] = jnp.zeros((8, 128), jnp.int32)
        rows = lax.broadcasted_iota(jnp.int32, (per_language, per_device), 0)
        hit = rows + number * per_language == slots
        select[...] = hit.astype(jnp.float32).astype(jnp.bfloat16)

    @pl.when(step == 0)
    def _():
        out[...] = jnp.dot(
            select[...], queries[...], preferred_element_type=jnp.float32
        ).astype(jnp.bfloat16)

    @pl.when(step > 0)
    def _():
        out[...] = jnp.dot(
            select[...], teacher[...], preferred_element_type=jnp.float32
        ).astype(jnp.bfloat16)


def sort_rows(number, here, ids, slot, queries, teacher):
    first = slot is None
    whole = lambda j, here: (0, 0)
    slot_shape = (8, per_device) if first else (8, 128)
    return pl.pallas_call(
        functools.partial(sort_kernel, first, number),
        grid_spec=pltpu.PrefetchScalarGridSpec(
            num_scalar_prefetch=1,
            grid=(3,),
            in_specs=[
                pl.BlockSpec((1, per_device), whole),
                pl.BlockSpec((8, per_device) if not first else (1, per_device), whole),
                pl.BlockSpec((per_device, width), whole),
                pl.BlockSpec((per_device, width), lambda j, here: (0, jnp.maximum(j - 1, 0))),
            ],
            out_specs=[
                pl.BlockSpec((per_language, width), lambda j, here: (0, j)),
                pl.BlockSpec(slot_shape, whole),
            ],
            scratch_shapes=[pltpu.VMEM((per_language, per_device), jnp.bfloat16)],
        ),
        out_shape=[
            jax.ShapeDtypeStruct((per_language, both), jnp.bfloat16),
            jax.ShapeDtypeStruct(slot_shape, jnp.int32),
        ],
        compiler_params=pltpu.CompilerParams(vmem_limit_bytes=60 * mib),
        cost_estimate=pl.CostEstimate(
            flops=2 * per_language * per_device * both, bytes_accessed=8 * mib, transcendentals=0
        ),
        name=f"sort_rows_{number}",
    )(here, ids, ids if first else slot, queries, teacher)


def row_pass(base, quarter, scores, teacher, weights, kl):
    for i in range(4):
        local = pl.ds(pl.multiple_of(quarter * 64 + i * 16, 16), 16)
        placed = pl.ds(pl.multiple_of(base + quarter * 64 + i * 16, 16), 16)
        own = scores[local, :]
        taught = teacher[placed, :].astype(jnp.float32)
        top = jnp.max(own, axis=1, keepdims=True)
        taught_top = jnp.max(taught, axis=1, keepdims=True)
        grown = jnp.exp(own - top)
        total = jnp.sum(grown, axis=1, keepdims=True)
        shifted = taught - taught_top
        taught_grown = jnp.exp(shifted)
        taught_total = jnp.sum(taught_grown, axis=1, keepdims=True)
        cross = jnp.sum(taught_grown * (shifted - own), axis=1, keepdims=True)
        diverge = cross / taught_total - jnp.log(taught_total) + top + jnp.log(total)
        weights[placed, :] = (
            grown * (student_scale / total) - taught_grown * (student_scale / taught_total)
        ).astype(jnp.bfloat16)
        kl[placed, :] = jnp.broadcast_to(diverge, (16, 128))


def score_quarter(base, quarter, queries, passages, scores):
    columns = pl.ds(pl.multiple_of(quarter * 512, 512), 512)
    scores[:, columns] = (
        lax.dot_general(
            queries[base : base + per_language, :],
            passages[columns, :],
            (((1,), (1,)), ((), ())),
            preferred_element_type=jnp.float32,
        )
        * student_scale
    )


def first_kernel(
    offsets, counts, raw, in0, in1, in2, weights_out, passages_out, kl,
    raw_v, passages, queries, teacher, scores, other_scores, weights, raw_sem, in_sem, out_sem,
):
    def raw_copy(h):
        return pltpu.make_async_copy(raw.at[h], raw_v.at[h], raw_sem.at[h])

    def start_raw(h, carry):
        raw_copy(h).start()
        return carry

    lax.fori_loop(0, holders, start_raw, 0)
    copies = []
    for number, block in enumerate((in0, in1, in2)):
        rows = pl.ds(number * per_language, per_language)
        copies.append(
            pltpu.make_async_copy(
                block.at[:, pl.ds(0, width)], queries.at[rows], in_sem.at[2 * number]
            )
        )
        copies.append(
            pltpu.make_async_copy(
                block.at[:, pl.ds(width, passages_all)], teacher.at[rows], in_sem.at[2 * number + 1]
            )
        )
    for copy in copies:
        copy.start()

    passages[pl.ds(0, 16), :] = jnp.zeros((16, width), jnp.bfloat16)

    def place(h, carry):
        raw_copy(h).wait()
        offset = offsets[h]
        start = pl.multiple_of((offset // 16) * 16, 16)
        target = lax.broadcasted_iota(jnp.int32, (window, capacity), 0)
        source = lax.broadcasted_iota(jnp.int32, (window, capacity), 1)
        hit = (target == source + (offset - start)) & (source < counts[h])
        chosen = hit.astype(jnp.float32).astype(jnp.bfloat16)
        moved = jnp.dot(chosen, raw_v[h], preferred_element_type=jnp.float32).astype(jnp.bfloat16)
        head = passages[pl.ds(start, 16), :]
        passages[pl.ds(start, 16), :] = head + moved[:16]
        passages[pl.ds(start + 16, window - 16), :] = moved[16:]
        return carry

    lax.fori_loop(0, holders, place, 0)
    passage_copy = pltpu.make_async_copy(
        passages.at[pl.ds(0, passages_all)], passages_out, out_sem.at[3]
    )
    passage_copy.start()
    for copy in copies:
        copy.wait()

    def score_only(quarter, carry):
        score_quarter(0, quarter, queries, passages, scores)
        return carry

    lax.fori_loop(0, 4, score_only, 0)
    out_copies = []
    held, free = scores, other_scores
    for number in range(3):
        base = number * per_language

        def together(quarter, carry, base=base, held=held, free=free, last=number == 2):
            if not last:
                score_quarter(base + per_language, quarter, queries, passages, free)
            row_pass(base, quarter, held, teacher, weights, kl)
            return carry

        lax.fori_loop(0, 4, together, 0)
        rows = pl.ds(base, per_language)
        copy = pltpu.make_async_copy(weights.at[rows], weights_out.at[rows], out_sem.at[number])
        copy.start()
        out_copies.append(copy)
        held, free = free, held
    passage_copy.wait()
    for copy in out_copies:
        copy.wait()


def first_blocks(offsets, counts, raw, blocks):
    smem = pl.BlockSpec(memory_space=pltpu.SMEM)
    anywhere = pl.BlockSpec(memory_space=pl.ANY)
    rows = 3 * per_language
    return pl.pallas_call(
        first_kernel,
        in_specs=[smem] * 2 + [anywhere] * 4,
        out_specs=[anywhere, anywhere, pl.BlockSpec(memory_space=pltpu.VMEM)],
        out_shape=[
            jax.ShapeDtypeStruct((rows, passages_all), jnp.bfloat16),
            jax.ShapeDtypeStruct((passages_all, width), jnp.bfloat16),
            jax.ShapeDtypeStruct((rows, 128), jnp.float32),
        ],
        scratch_shapes=[
            pltpu.VMEM((holders, capacity, width), jnp.bfloat16),
            pltpu.VMEM((passages_all + 256, width), jnp.bfloat16),
            pltpu.VMEM((rows, width), jnp.bfloat16),
            pltpu.VMEM((rows, passages_all), jnp.bfloat16),
            pltpu.VMEM((per_language, passages_all), jnp.float32),
            pltpu.VMEM((per_language, passages_all), jnp.float32),
            pltpu.VMEM((rows, passages_all), jnp.bfloat16),
            pltpu.SemaphoreType.DMA((holders,)),
            pltpu.SemaphoreType.DMA((6,)),
            pltpu.SemaphoreType.DMA((4,)),
        ],
        compiler_params=pltpu.CompilerParams(vmem_limit_bytes=60 * mib),
        cost_estimate=pl.CostEstimate(
            flops=5 * 1024**3, bytes_accessed=28 * mib, transcendentals=3 * mib
        ),
        name="first_blocks",
    )(offsets, counts, raw, *blocks)


def last_kernel(
    core, passages_in, weights_in, in0, in1, in2, in3, weights_out, send_out, keep_out, kl,
    passages, queries, teacher, scores, weights, send, keep, in_sem, out_sem,
):
    base = 3 * per_language
    own = pl.ds(base, per_language)
    ready = [
        pltpu.make_async_copy(in3.at[:, pl.ds(0, width)], queries.at[own], in_sem.at[0]),
        pltpu.make_async_copy(passages_in, passages, in_sem.at[1]),
        pltpu.make_async_copy(in3.at[:, pl.ds(width, passages_all)], teacher, in_sem.at[2]),
    ]
    later = [pltpu.make_async_copy(weights_in, weights.at[pl.ds(0, base)], in_sem.at[3])]
    for number, block in enumerate((in0, in1, in2)):
        later.append(
            pltpu.make_async_copy(
                block.at[:, pl.ds(0, width)],
                queries.at[pl.ds(number * per_language, per_language)],
                in_sem.at[4 + number],
            )
        )
    for copy in ready + later:
        copy.start()
    for copy in ready:
        copy.wait()

    def score_only(quarter, carry):
        score_quarter(base, quarter, queries, passages, scores)
        return carry

    lax.fori_loop(0, 4, score_only, 0)

    def rows_only(quarter, carry):
        row_pass(0, quarter, scores, teacher, weights.at[own], kl)
        return carry

    lax.fori_loop(0, 4, rows_only, 0)
    weight_copy = pltpu.make_async_copy(weights.at[own], weights_out, out_sem.at[0])
    weight_copy.start()
    for copy in later:
        copy.wait()
    even = core[0] == 0

    def sent(j):
        rows = pl.ds(pl.multiple_of(j * 128, 128), 128)
        return [
            pltpu.make_async_copy(send.at[rows], send_out.at[rows], out_sem.at[1 + j]),
            pltpu.make_async_copy(keep.at[rows], keep_out.at[rows], out_sem.at[9 + j]),
        ]

    def reduce(j, carry):
        columns = pl.ds(pl.multiple_of(j * 256, 256), 256)
        grad = lax.dot_general(
            weights[:, columns],
            queries[...],
            (((0,), (0,)), ((), ())),
            preferred_element_type=jnp.float32,
        ).astype(jnp.bfloat16)
        for part in range(2):
            upper = grad[part * 128 : part * 128 + 64]
            lower = grad[part * 128 + 64 : part * 128 + 128]
            rows = pl.ds(pl.multiple_of(j * 128 + part * 64, 64), 64)
            keep[rows, :] = jnp.where(even, upper, lower)
            send[rows, :] = jnp.where(even, lower, upper)
        for copy in sent(j):
            copy.start()
        return carry

    lax.fori_loop(0, passages_all // 256, reduce, 0)
    weight_copy.wait()
    for j in range(passages_all // 256):
        for copy in sent(j):
            copy.wait()


def last_block(core, passages, weights, blocks):
    smem = pl.BlockSpec(memory_space=pltpu.SMEM)
    anywhere = pl.BlockSpec(memory_space=pl.ANY)
    half = (passages_all // 2, width)
    return pl.pallas_call(
        last_kernel,
        in_specs=[smem] + [anywhere] * 6,
        out_specs=[anywhere] * 3 + [pl.BlockSpec(memory_space=pltpu.VMEM)],
        out_shape=[
            jax.ShapeDtypeStruct((per_language, passages_all), jnp.bfloat16),
            jax.ShapeDtypeStruct(half, jnp.bfloat16),
            jax.ShapeDtypeStruct(half, jnp.bfloat16),
            jax.ShapeDtypeStruct((per_language, 128), jnp.float32),
        ],
        scratch_shapes=[
            pltpu.VMEM((passages_all, width), jnp.bfloat16),
            pltpu.VMEM((per_device, width), jnp.bfloat16),
            pltpu.VMEM((per_language, passages_all), jnp.bfloat16),
            pltpu.VMEM((per_language, passages_all), jnp.float32),
            pltpu.VMEM((per_device, passages_all), jnp.bfloat16),
            pltpu.VMEM(half, jnp.bfloat16),
            pltpu.VMEM(half, jnp.bfloat16),
            pltpu.SemaphoreType.DMA((7,)),
            pltpu.SemaphoreType.DMA((17,)),
        ],
        compiler_params=pltpu.CompilerParams(vmem_limit_bytes=60 * mib),
        cost_estimate=pl.CostEstimate(
            flops=6 * 1024**3, bytes_accessed=16 * mib, transcendentals=mib
        ),
        name="last_block",
    )(core, passages, weights, *blocks)


def query_kernel(weights, last_weights, passages, kl, last_kl, *outs):
    step = pl.program_id(0)
    last = step == languages - 1
    chosen = jnp.where(last, last_weights[...], weights[...])
    grad = jnp.dot(chosen, passages[...], preferred_element_type=jnp.float32)
    value = jnp.where(last, last_kl[...], kl[...])
    high = value.astype(jnp.bfloat16).astype(jnp.float32)
    middle = (value - high).astype(jnp.bfloat16).astype(jnp.float32)
    low = value - high - middle
    lane = lax.broadcasted_iota(jnp.int32, (per_language, extra), 1)
    parts = jnp.where(
        lane == 0, high, jnp.where(lane == 1, middle, jnp.where(lane == 2, low, 0.0))
    )
    for number, out in enumerate(outs):

        @pl.when(step == number)
        def _(out=out):
            out[:, :width] = grad.astype(jnp.bfloat16)
            out[:, width:] = parts.astype(jnp.bfloat16)


def query_grads(weights, last_weights, passages, kl, last_kl):
    block = jax.ShapeDtypeStruct((per_language, width + extra), jnp.bfloat16)
    whole = lambda i: (0, 0)
    return pl.pallas_call(
        query_kernel,
        grid=(languages,),
        in_specs=[
            pl.BlockSpec((per_language, passages_all), lambda i: (jnp.minimum(i, 2), 0)),
            pl.BlockSpec((per_language, passages_all), whole),
            pl.BlockSpec((passages_all, width), whole),
            pl.BlockSpec((per_language, 128), lambda i: (jnp.minimum(i, 2), 0)),
            pl.BlockSpec((per_language, 128), whole),
        ],
        out_specs=[pl.BlockSpec((per_language, width + extra), whole)] * 4,
        out_shape=[block] * 4,
        compiler_params=pltpu.CompilerParams(vmem_limit_bytes=60 * mib),
        cost_estimate=pl.CostEstimate(
            flops=4 * 1024**3, bytes_accessed=12 * mib, transcendentals=0
        ),
        name="query_grads",
    )(weights, last_weights, passages, kl, last_kl)


def pair_kernel(keep, other, out):
    out[...] = (keep[...].astype(jnp.float32) + other[...].astype(jnp.float32)).astype(jnp.bfloat16)


def pair_sum(keep, other):
    spec = pl.BlockSpec((256, width), lambda i: (i, 0))
    return pl.pallas_call(
        pair_kernel,
        grid=(4,),
        in_specs=[spec, spec],
        out_specs=spec,
        out_shape=jax.ShapeDtypeStruct(keep.shape, jnp.bfloat16),
        compiler_params=pltpu.CompilerParams(vmem_limit_bytes=60 * mib),
        cost_estimate=pl.CostEstimate(flops=mib, bytes_accessed=6 * mib, transcendentals=0),
        name="pair_sum",
    )(keep, other)


def restore_kernel(slot, in0, in1, in2, in3, grads, kl, select):
    rows = lax.broadcasted_iota(jnp.int32, (per_device, per_device), 0)
    slots = slot[0:1, :]
    select[...] = (rows == slots).astype(jnp.float32).astype(jnp.bfloat16)
    total = jnp.zeros((per_device, 128), jnp.float32)
    contract = (((0,), (0,)), ((), ()))
    for j in range(4):
        columns = slice(j * 256, (j + 1) * 256)
        part = jnp.zeros((per_device, 256), jnp.float32)
        for number, block in enumerate((in0, in1, in2, in3)):
            chosen = select[number * per_language : (number + 1) * per_language, :]
            part += lax.dot_general(
                chosen, block[:, columns], contract, preferred_element_type=jnp.float32
            )
        grads[:, columns] = part.astype(jnp.bfloat16)
    for number, block in enumerate((in0, in1, in2, in3)):
        chosen = select[number * per_language : (number + 1) * per_language, :]
        total += lax.dot_general(
            chosen, block[:, width:], contract, preferred_element_type=jnp.float32
        )
    column = jnp.sum(total, axis=1, keepdims=True)
    kl[...] = jnp.transpose(jnp.broadcast_to(column, (per_device, 128)))[:8]


def restore(slot, blocks):
    vmem = pl.BlockSpec(memory_space=pltpu.VMEM)
    return pl.pallas_call(
        restore_kernel,
        in_specs=[vmem] * 5,
        out_specs=[vmem, vmem],
        out_shape=[
            jax.ShapeDtypeStruct((per_device, width), jnp.bfloat16),
            jax.ShapeDtypeStruct((8, per_device), jnp.float32),
        ],
        scratch_shapes=[pltpu.VMEM((per_device, per_device), jnp.bfloat16)],
        compiler_params=pltpu.CompilerParams(vmem_limit_bytes=60 * mib),
        cost_estimate=pl.CostEstimate(
            flops=2 * 1024**3, bytes_accessed=6 * mib, transcendentals=0
        ),
        name="restore",
    )(slot, *blocks)


def shift(array, by):
    pairs = [(i, (i + by) % languages) for i in range(languages)]
    return lax.ppermute(array, "x", pairs)


def on_device(queries, bucket_ids, raw_passages, counts, teacher):
    group = ("y", "z", "c")
    here = lax.axis_index("x").astype(jnp.int32).reshape(1)
    core = lax.axis_index("c").astype(jnp.int32).reshape(1)
    all_raw = lax.all_gather(raw_passages[0], group, axis=0, tiled=True)
    ids = bucket_ids[0]
    out1, slot = sort_rows(1, here, ids, None, queries[0, 0], teacher[0, 0])
    in1 = shift(out1, 1)
    out3, _ = sort_rows(3, here, ids, slot, queries[0, 0], teacher[0, 0])
    in3 = shift(out3, 3)
    out2, _ = sort_rows(2, here, ids, slot, queries[0, 0], teacher[0, 0])
    in2 = shift(out2, 2)
    in0, _ = sort_rows(0, here, ids, slot, queries[0, 0], teacher[0, 0])
    held_counts, in0 = lax.optimization_barrier((counts, in0))
    holder_counts = lax.all_gather(held_counts[0], group, axis=0, tiled=True)
    earlier = jnp.arange(holders)[None, :] < jnp.arange(holders)[:, None]
    offsets = jnp.sum(jnp.where(earlier, holder_counts[None, :], 0), axis=1).astype(jnp.int32)
    weights, passages, kl = first_blocks(offsets, holder_counts, all_raw, (in0, in1, in3))
    last_weights, send, keep, last_kl = last_block(core, passages, weights, (in0, in1, in3, in2))
    other = lax.ppermute(send, "c", [(0, 1), (1, 0)])
    back0, back1, back3, back2 = query_grads(weights, last_weights, passages, kl, last_kl)
    other, back1, back2, back3 = lax.optimization_barrier((other, back1, back2, back3))
    back = [back0, shift(back1, -1), shift(back2, -2), shift(back3, -3)]
    paired = pair_sum(keep, other)
    spread = lax.all_to_all(
        paired.reshape(16, 64, width), ("y", "z"), split_axis=0, concat_axis=0, tiled=True
    )
    grad_passages = jnp.sum(spread.astype(jnp.float32), axis=0).astype(jnp.bfloat16)
    grad_queries, kl_rows = restore(slot, back)
    return (grad_queries[None, None], grad_passages[None], kl_rows[0][None, None])


def solution(mesh):
    split = Mesh(mesh.devices.reshape(4, 4, 4, 2), ("x", "y", "z", "c"))
    group = ("y", "z", "c")
    in_specs = (
        P("x", group, None, None),
        P("x", group, None),
        P("x", group, None, None),
        P("x", group),
        P("x", group, None, None),
    )
    out_specs = (P("x", group, None, None), P("x", group, None), P("x", group, None))
    return jax.shard_map(
        on_device, mesh=split, in_specs=in_specs, out_specs=out_specs, check_vma=False
    )
```

```python
import functools

import jax
import jax.numpy as jnp
from jax import lax
from jax.experimental import pallas as pl
from jax.experimental.pallas import tpu as pltpu
from jax.sharding import Mesh
from jax.sharding import PartitionSpec as P

student_scale = 0.1
languages = 4
holders = 32
capacity = 192
width = 1024
per_device = 1024
per_language = 256
passages_all = 2048
both = width + passages_all
window = 208
extra = 128
mib = 1024 * 1024


def slots_of(ids, here):
    turned = lax.rem(ids - here + languages, languages)
    hot = turned == lax.broadcasted_iota(jnp.int32, (8, per_device), 0)
    earlier = lax.broadcasted_iota(jnp.int32, (per_device, per_device), 0)
    later = lax.broadcasted_iota(jnp.int32, (per_device, per_device), 1)
    upper = (earlier <= later).astype(jnp.float32).astype(jnp.bfloat16)
    hot = hot.astype(jnp.float32)
    ranks = jnp.dot(hot.astype(jnp.bfloat16), upper, preferred_element_type=jnp.float32)
    first = lax.broadcasted_iota(jnp.int32, (8, per_device), 0).astype(jnp.float32) * per_language
    return jnp.sum(hot * (ranks - 1.0 + first), axis=0, keepdims=True).astype(jnp.int32)


def sort_kernel(first, here, ids, slot_in, queries, teacher, out_a, out_b, slot, select):
    step = pl.program_id(0)

    @pl.when(step == 0)
    def _():
        if first is not None:
            slots = slots_of(ids[...], here[0])
            slot[...] = jnp.broadcast_to(slots, (8, per_device))
        else:
            slots = slot_in[0:1, :]
            slot[...] = jnp.zeros((8, 128), jnp.int32)
        rows = lax.broadcasted_iota(jnp.int32, (2 * per_language, per_device), 0)
        numbers = (1, 3) if first is not None else (2, 0)
        begin = jnp.where(
            rows < per_language,
            rows + numbers[0] * per_language,
            rows + (numbers[1] - 1) * per_language,
        )
        select[...] = (begin == slots).astype(jnp.float32).astype(jnp.bfloat16)

    def move(block):
        out_a[...] = jnp.dot(
            select[:per_language, :], block, preferred_element_type=jnp.float32
        ).astype(jnp.bfloat16)
        out_b[...] = jnp.dot(
            select[per_language:, :], block, preferred_element_type=jnp.float32
        ).astype(jnp.bfloat16)

    @pl.when(step < 2)
    def _():
        move(queries[...])

    @pl.when(step >= 2)
    def _():
        move(teacher[...])


def sort_rows(here, ids, slot, queries, teacher):
    first = True if slot is None else None
    whole = lambda j, here: (0, 0)
    slot_shape = (8, per_device) if first else (8, 128)
    tile = 512
    block = jax.ShapeDtypeStruct((per_language, both), jnp.bfloat16)
    out_block = pl.BlockSpec((per_language, tile), lambda j, here: (0, j))
    return pl.pallas_call(
        functools.partial(sort_kernel, first),
        grid_spec=pltpu.PrefetchScalarGridSpec(
            num_scalar_prefetch=1,
            grid=(both // tile,),
            in_specs=[
                pl.BlockSpec((1, per_device), whole),
                pl.BlockSpec((8, per_device) if not first else (1, per_device), whole),
                pl.BlockSpec((per_device, tile), lambda j, here: (0, jnp.minimum(j, 1))),
                pl.BlockSpec((per_device, tile), lambda j, here: (0, jnp.maximum(j - 2, 0))),
            ],
            out_specs=[out_block, out_block, pl.BlockSpec(slot_shape, whole)],
            scratch_shapes=[pltpu.VMEM((2 * per_language, per_device), jnp.bfloat16)],
        ),
        out_shape=[block, block, jax.ShapeDtypeStruct(slot_shape, jnp.int32)],
        compiler_params=pltpu.CompilerParams(vmem_limit_bytes=60 * mib),
        cost_estimate=pl.CostEstimate(
            flops=4 * per_language * per_device * both, bytes_accessed=9 * mib, transcendentals=0
        ),
        name="sort_first" if first else "sort_rest",
    )(here, ids, ids if first else slot, queries, teacher)


def grad_half(rows, columns, weights, passages, out):
    out[rows, columns] = jnp.dot(
        weights[rows, :], passages[pl.ds(0, passages_all), columns],
        preferred_element_type=jnp.float32,
    ).astype(jnp.bfloat16)


def kl_parts(value):
    high = value.astype(jnp.bfloat16).astype(jnp.float32)
    middle = (value - high).astype(jnp.bfloat16).astype(jnp.float32)
    low = value - high - middle
    lane = lax.broadcasted_iota(jnp.int32, value.shape, 1)
    parts = jnp.where(
        lane == 0, high, jnp.where(lane == 1, middle, jnp.where(lane == 2, low, 0.0))
    )
    return parts.astype(jnp.bfloat16)


def row_pass(base, quarter, scores, teacher, weights, kl):
    for i in range(4):
        local = pl.ds(pl.multiple_of(quarter * 64 + i * 16, 16), 16)
        placed = pl.ds(pl.multiple_of(base + quarter * 64 + i * 16, 16), 16)
        own = scores[local, :]
        taught = teacher[placed, :].astype(jnp.float32)
        top = jnp.max(own, axis=1, keepdims=True)
        taught_top = jnp.max(taught, axis=1, keepdims=True)
        grown = jnp.exp(own - top)
        total = jnp.sum(grown, axis=1, keepdims=True)
        shifted = taught - taught_top
        taught_grown = jnp.exp(shifted)
        taught_total = jnp.sum(taught_grown, axis=1, keepdims=True)
        cross = jnp.sum(taught_grown * (shifted - own), axis=1, keepdims=True)
        diverge = cross / taught_total - jnp.log(taught_total) + top + jnp.log(total)
        weights[placed, :] = (
            grown * (student_scale / total) - taught_grown * (student_scale / taught_total)
        ).astype(jnp.bfloat16)
        kl[placed, :] = jnp.broadcast_to(diverge, (16, 128))


def score_quarter(base, quarter, queries, passages, scores):
    columns = pl.ds(pl.multiple_of(quarter * 512, 512), 512)
    scores[:, columns] = (
        lax.dot_general(
            queries[base : base + per_language, :],
            passages[columns, :],
            (((1,), (1,)), ((), ())),
            preferred_element_type=jnp.float32,
        )
        * student_scale
    )


def first_kernel(
    offsets, counts, raw, in0, in1, in2, weights_out, passages_out, grad0, grad1, grad2,
    raw_v, passages, queries, teacher, scores, other_scores, weights, grads, kl,
    raw_sem, in_sem, out_sem,
):
    def raw_copy(h):
        return pltpu.make_async_copy(raw.at[h], raw_v.at[h], raw_sem.at[h])

    def start_raw(h, carry):
        raw_copy(h).start()
        return carry

    lax.fori_loop(0, holders, start_raw, 0)
    copies = []
    for number, block in enumerate((in0, in1, in2)):
        rows = pl.ds(number * per_language, per_language)
        copies.append(
            pltpu.make_async_copy(
                block.at[:, pl.ds(0, width)], queries.at[rows], in_sem.at[2 * number]
            )
        )
        copies.append(
            pltpu.make_async_copy(
                block.at[:, pl.ds(width, passages_all)], teacher.at[rows], in_sem.at[2 * number + 1]
            )
        )
    for copy in copies:
        copy.start()

    passages[pl.ds(0, 16), :] = jnp.zeros((16, width), jnp.bfloat16)

    def place(h, carry):
        raw_copy(h).wait()
        offset = offsets[h]
        start = pl.multiple_of((offset // 16) * 16, 16)
        target = lax.broadcasted_iota(jnp.int32, (window, capacity), 0)
        source = lax.broadcasted_iota(jnp.int32, (window, capacity), 1)
        hit = (target == source + (offset - start)) & (source < counts[h])
        chosen = hit.astype(jnp.float32).astype(jnp.bfloat16)
        moved = jnp.dot(chosen, raw_v[h], preferred_element_type=jnp.float32).astype(jnp.bfloat16)
        head = passages[pl.ds(start, 16), :]
        passages[pl.ds(start, 16), :] = head + moved[:16]
        passages[pl.ds(start + 16, window - 16), :] = moved[16:]
        return carry

    lax.fori_loop(0, holders, place, 0)
    passage_copy = pltpu.make_async_copy(
        passages.at[pl.ds(0, passages_all)], passages_out, out_sem.at[3]
    )
    passage_copy.start()
    for copy in copies:
        copy.wait()

    def score_only(quarter, carry):
        score_quarter(0, quarter, queries, passages, scores)
        return carry

    lax.fori_loop(0, 4, score_only, 0)
    out_copies = []
    held, free = scores, other_scores
    for number in range(3):
        base = number * per_language

        def together(quarter, carry, base=base, held=held, free=free, last=number == 2):
            if last:
                done = pl.ds(pl.multiple_of((quarter // 2) * per_language, 256), per_language)
                columns = pl.ds(pl.multiple_of((quarter % 2) * 512, 512), 512)
                grad_half(done, columns, weights, passages, grads)
            else:
                score_quarter(base + per_language, quarter, queries, passages, free)
            row_pass(base, quarter, held, teacher, weights, kl)
            return carry

        lax.fori_loop(0, 4, together, 0)
        rows = pl.ds(base, per_language)
        copy = pltpu.make_async_copy(weights.at[rows], weights_out.at[rows], out_sem.at[number])
        copy.start()
        out_copies.append(copy)
        held, free = free, held
    for number, out in enumerate((grad0, grad1, grad2)):
        rows = pl.ds(number * per_language, per_language)
        if number == 2:
            for half in range(2):
                grad_half(rows, slice(half * 512, (half + 1) * 512), weights, passages, grads)
        grads[rows, width:] = kl_parts(kl[rows, :])
        copy = pltpu.make_async_copy(grads.at[rows], out, out_sem.at[4 + number])
        copy.start()
        out_copies.append(copy)
    passage_copy.wait()
    for copy in out_copies:
        copy.wait()


def first_blocks(offsets, counts, raw, blocks):
    smem = pl.BlockSpec(memory_space=pltpu.SMEM)
    anywhere = pl.BlockSpec(memory_space=pltpu.HBM)
    rows = 3 * per_language
    return pl.pallas_call(
        first_kernel,
        in_specs=[smem] * 2 + [anywhere] * 4,
        out_specs=[anywhere] * 5,
        out_shape=[
            jax.ShapeDtypeStruct((rows, passages_all), jnp.bfloat16),
            jax.ShapeDtypeStruct((passages_all, width), jnp.bfloat16),
        ]
        + [jax.ShapeDtypeStruct((per_language, width + extra), jnp.bfloat16)] * 3,
        scratch_shapes=[
            pltpu.VMEM((holders, capacity, width), jnp.bfloat16),
            pltpu.VMEM((passages_all + 256, width), jnp.bfloat16),
            pltpu.VMEM((rows, width), jnp.bfloat16),
            pltpu.VMEM((rows, passages_all), jnp.bfloat16),
            pltpu.VMEM((per_language, passages_all), jnp.float32),
            pltpu.VMEM((per_language, passages_all), jnp.float32),
            pltpu.VMEM((rows, passages_all), jnp.bfloat16),
            pltpu.VMEM((rows, width + extra), jnp.bfloat16),
            pltpu.VMEM((rows, 128), jnp.float32),
            pltpu.SemaphoreType.DMA((holders,)),
            pltpu.SemaphoreType.DMA((6,)),
            pltpu.SemaphoreType.DMA((7,)),
        ],
        compiler_params=pltpu.CompilerParams(vmem_limit_bytes=60 * mib),
        cost_estimate=pl.CostEstimate(
            flops=8 * 1024**3, bytes_accessed=30 * mib, transcendentals=3 * mib
        ),
        name="first_blocks",
    )(offsets, counts, raw, *blocks)


def last_kernel(
    core, passages_in, weights_in, in0, in1, in2, in3, weights_out, send_out, keep_out, kl,
    passages, queries, teacher, scores, weights, total, send, keep, in_sem, out_sem,
):
    base = 3 * per_language
    own = pl.ds(base, per_language)

    def passage_copy(quarter):
        rows = pl.ds(pl.multiple_of(quarter * 512, 512), 512)
        return pltpu.make_async_copy(
            passages_in.at[rows], passages.at[rows], in_sem.at[6 + quarter]
        )

    own_queries = pltpu.make_async_copy(
        in3.at[:, pl.ds(0, width)], queries.at[own], in_sem.at[0]
    )
    own_queries.start()
    for quarter in range(4):
        passage_copy(quarter).start()
    later = [
        pltpu.make_async_copy(in3.at[:, pl.ds(width, passages_all)], teacher, in_sem.at[1]),
        pltpu.make_async_copy(weights_in, weights.at[pl.ds(0, base)], in_sem.at[2]),
    ]
    for number, block in enumerate((in0, in1, in2)):
        later.append(
            pltpu.make_async_copy(
                block.at[:, pl.ds(0, width)],
                queries.at[pl.ds(number * per_language, per_language)],
                in_sem.at[3 + number],
            )
        )
    for copy in later:
        copy.start()
    own_queries.wait()

    def score_only(quarter, carry):
        passage_copy(quarter).wait()
        score_quarter(base, quarter, queries, passages, scores)
        return carry

    lax.fori_loop(0, 4, score_only, 0)
    for copy in later:
        copy.wait()
    before = pl.ds(0, base)

    def together(quarter, carry):
        row_pass(0, quarter, scores, teacher, weights.at[own], kl)
        columns = pl.ds(pl.multiple_of(quarter * 512, 512), 512)
        total[columns, :] = lax.dot_general(
            weights[before, columns],
            queries[before, :],
            (((0,), (0,)), ((), ())),
            preferred_element_type=jnp.float32,
        )
        return carry

    lax.fori_loop(0, 4, together, 0)
    weight_copy = pltpu.make_async_copy(weights.at[own], weights_out, out_sem.at[0])
    weight_copy.start()
    even = core[0] == 0

    def sent(j):
        rows = pl.ds(pl.multiple_of(j * 128, 128), 128)
        return [
            pltpu.make_async_copy(send.at[rows], send_out.at[rows], out_sem.at[1 + j]),
            pltpu.make_async_copy(keep.at[rows], keep_out.at[rows], out_sem.at[9 + j]),
        ]

    def reduce(j, carry):
        columns = pl.ds(pl.multiple_of(j * 256, 256), 256)
        grad = lax.dot_general(
            weights[own, columns],
            queries[own, :],
            (((0,), (0,)), ((), ())),
            preferred_element_type=jnp.float32,
        )
        grad = (grad + total[columns, :]).astype(jnp.bfloat16)
        for part in range(2):
            upper = grad[part * 128 : part * 128 + 64]
            lower = grad[part * 128 + 64 : part * 128 + 128]
            rows = pl.ds(pl.multiple_of(j * 128 + part * 64, 64), 64)
            keep[rows, :] = jnp.where(even, upper, lower)
            send[rows, :] = jnp.where(even, lower, upper)
        for copy in sent(j):
            copy.start()
        return carry

    lax.fori_loop(0, passages_all // 256, reduce, 0)
    weight_copy.wait()
    for j in range(passages_all // 256):
        for copy in sent(j):
            copy.wait()


def last_block(core, passages, weights, blocks):
    smem = pl.BlockSpec(memory_space=pltpu.SMEM)
    anywhere = pl.BlockSpec(memory_space=pltpu.HBM)
    half = (passages_all // 2, width)
    return pl.pallas_call(
        last_kernel,
        in_specs=[smem] + [anywhere] * 6,
        out_specs=[anywhere] * 3 + [pl.BlockSpec(memory_space=pltpu.VMEM)],
        out_shape=[
            jax.ShapeDtypeStruct((per_language, passages_all), jnp.bfloat16),
            jax.ShapeDtypeStruct(half, jnp.bfloat16),
            jax.ShapeDtypeStruct(half, jnp.bfloat16),
            jax.ShapeDtypeStruct((per_language, 128), jnp.float32),
        ],
        scratch_shapes=[
            pltpu.VMEM((passages_all, width), jnp.bfloat16),
            pltpu.VMEM((per_device, width), jnp.bfloat16),
            pltpu.VMEM((per_language, passages_all), jnp.bfloat16),
            pltpu.VMEM((per_language, passages_all), jnp.float32),
            pltpu.VMEM((per_device, passages_all), jnp.bfloat16),
            pltpu.VMEM((passages_all, width), jnp.float32),
            pltpu.VMEM(half, jnp.bfloat16),
            pltpu.VMEM(half, jnp.bfloat16),
            pltpu.SemaphoreType.DMA((10,)),
            pltpu.SemaphoreType.DMA((17,)),
        ],
        compiler_params=pltpu.CompilerParams(vmem_limit_bytes=60 * mib),
        cost_estimate=pl.CostEstimate(
            flops=6 * 1024**3, bytes_accessed=16 * mib, transcendentals=mib
        ),
        name="last_block",
    )(core, passages, weights, *blocks)


def query_kernel(weights, passages, kl, out):
    half = pl.program_id(0)
    grad = jnp.dot(weights[...], passages[...], preferred_element_type=jnp.float32)
    for number in range(2):

        @pl.when(half == number)
        def _(number=number):
            out[:, number * 512 : (number + 1) * 512] = grad.astype(jnp.bfloat16)

    @pl.when(half == 0)
    def _():
        out[:, width:] = kl_parts(kl[...])


def query_grads(weights, passages, kl):
    whole = lambda i: (0, 0)
    return pl.pallas_call(
        query_kernel,
        grid=(2,),
        in_specs=[
            pl.BlockSpec((per_language, passages_all), whole),
            pl.BlockSpec((passages_all, 512), lambda i: (0, i)),
            pl.BlockSpec((per_language, 128), whole),
        ],
        out_specs=pl.BlockSpec((per_language, width + extra), whole),
        out_shape=jax.ShapeDtypeStruct((per_language, width + extra), jnp.bfloat16),
        compiler_params=pltpu.CompilerParams(vmem_limit_bytes=60 * mib),
        cost_estimate=pl.CostEstimate(
            flops=1024**3, bytes_accessed=6 * mib, transcendentals=0
        ),
        name="query_grads",
    )(weights, passages, kl)


def pair_kernel(keep_in, other_in, out, keep, other, paired, sems):
    chunk = 256

    def read(i):
        rows = pl.ds(pl.multiple_of(i * chunk, chunk), chunk)
        return (
            pltpu.make_async_copy(keep_in.at[rows], keep.at[rows], sems.at[i]),
            pltpu.make_async_copy(other_in.at[rows], other.at[rows], sems.at[4 + i]),
        )

    def written(i):
        rows = pl.ds(pl.multiple_of(i * chunk, chunk), chunk)
        return pltpu.make_async_copy(paired.at[rows], out.at[rows], sems.at[8 + i])

    for i in range(4):
        for copy in read(i):
            copy.start()

    def step(i, carry):
        for copy in read(i):
            copy.wait()
        rows = pl.ds(pl.multiple_of(i * chunk, chunk), chunk)
        paired[rows, :] = (
            keep[rows, :].astype(jnp.float32) + other[rows, :].astype(jnp.float32)
        ).astype(jnp.bfloat16)
        written(i).start()
        return carry

    lax.fori_loop(0, 4, step, 0)
    for i in range(4):
        written(i).wait()


def pair_sum(keep, other):
    anywhere = pl.BlockSpec(memory_space=pltpu.HBM)
    return pl.pallas_call(
        pair_kernel,
        in_specs=[anywhere, anywhere],
        out_specs=anywhere,
        out_shape=jax.ShapeDtypeStruct(keep.shape, jnp.bfloat16),
        scratch_shapes=[pltpu.VMEM(keep.shape, jnp.bfloat16)] * 3
        + [pltpu.SemaphoreType.DMA((12,))],
        compiler_params=pltpu.CompilerParams(vmem_limit_bytes=60 * mib),
        cost_estimate=pl.CostEstimate(flops=mib, bytes_accessed=6 * mib, transcendentals=0),
        name="pair_sum",
    )(keep, other)


def restore_kernel(slot, in0, in1, in2, in3, grads, kl, select):
    rows = lax.broadcasted_iota(jnp.int32, (per_device, per_device), 0)
    slots = slot[0:1, :]
    select[...] = (rows == slots).astype(jnp.float32).astype(jnp.bfloat16)
    total = jnp.zeros((per_device, 128), jnp.float32)
    contract = (((0,), (0,)), ((), ()))
    for j in range(4):
        columns = slice(j * 256, (j + 1) * 256)
        part = jnp.zeros((per_device, 256), jnp.float32)
        for number, block in enumerate((in0, in1, in2, in3)):
            chosen = select[number * per_language : (number + 1) * per_language, :]
            part += lax.dot_general(
                chosen, block[:, columns], contract, preferred_element_type=jnp.float32
            )
        grads[:, columns] = part.astype(jnp.bfloat16)
    for number, block in enumerate((in0, in1, in2, in3)):
        chosen = select[number * per_language : (number + 1) * per_language, :]
        total += lax.dot_general(
            chosen, block[:, width:], contract, preferred_element_type=jnp.float32
        )
    column = jnp.sum(total, axis=1, keepdims=True)
    kl[...] = jnp.transpose(jnp.broadcast_to(column, (per_device, 128)))[:8]


def restore(slot, blocks):
    vmem = pl.BlockSpec(memory_space=pltpu.VMEM)
    return pl.pallas_call(
        restore_kernel,
        in_specs=[vmem] * 5,
        out_specs=[vmem, vmem],
        out_shape=[
            jax.ShapeDtypeStruct((per_device, width), jnp.bfloat16),
            jax.ShapeDtypeStruct((8, per_device), jnp.float32),
        ],
        scratch_shapes=[pltpu.VMEM((per_device, per_device), jnp.bfloat16)],
        compiler_params=pltpu.CompilerParams(vmem_limit_bytes=60 * mib),
        cost_estimate=pl.CostEstimate(
            flops=2 * 1024**3, bytes_accessed=6 * mib, transcendentals=0
        ),
        name="restore",
    )(slot, *blocks)


def shift(array, by):
    pairs = [(i, (i + by) % languages) for i in range(languages)]
    return lax.ppermute(array, "x", pairs)


def on_device(queries, bucket_ids, raw_passages, counts, teacher):
    group = ("y", "z", "c")
    here = lax.axis_index("x").astype(jnp.int32).reshape(1)
    core = lax.axis_index("c").astype(jnp.int32).reshape(1)
    all_raw = lax.all_gather(raw_passages[0], group, axis=0, tiled=True)
    ids = bucket_ids[0]
    out1, out3, slot = sort_rows(here, ids, None, queries[0, 0], teacher[0, 0])
    in1, in3 = shift(out1, 1), shift(out3, 3)
    out2, in0, _ = sort_rows(here, ids, slot, queries[0, 0], teacher[0, 0])
    held_counts, in0, out2 = lax.optimization_barrier((counts, in0, out2))
    holder_counts = lax.all_gather(held_counts[0], group, axis=0, tiled=True)
    earlier = jnp.arange(holders)[None, :] < jnp.arange(holders)[:, None]
    offsets = jnp.sum(jnp.where(earlier, holder_counts[None, :], 0), axis=1).astype(jnp.int32)
    out2, in1, in3, offsets = lax.optimization_barrier((out2, in1, in3, offsets))
    in2 = shift(out2, 2)
    weights, passages, back0, back1, back3 = first_blocks(
        offsets, holder_counts, all_raw, (in0, in1, in3)
    )
    home1, home3 = shift(back1, -1), shift(back3, -3)
    last_weights, send, keep, last_kl = last_block(core, passages, weights, (in0, in1, in3, in2))
    other = lax.ppermute(send, "c", [(0, 1), (1, 0)])
    back2 = query_grads(last_weights, passages, last_kl)
    other, back2 = lax.optimization_barrier((other, back2))
    back = [back0, home1, shift(back2, -2), home3]
    paired = pair_sum(keep, other)
    spread = lax.all_to_all(
        paired.reshape(16, 64, width), ("y", "z"), split_axis=0, concat_axis=0, tiled=True
    )
    grad_passages = jnp.sum(spread.astype(jnp.float32), axis=0).astype(jnp.bfloat16)
    grad_queries, kl_rows = restore(slot, back)
    return (grad_queries[None, None], grad_passages[None], kl_rows[0][None, None])


def solution(mesh):
    split = Mesh(mesh.devices.reshape(4, 4, 4, 2), ("x", "y", "z", "c"))
    group = ("y", "z", "c")
    in_specs = (
        P("x", group, None, None),
        P("x", group, None),
        P("x", group, None, None),
        P("x", group),
        P("x", group, None, None),
    )
    out_specs = (P("x", group, None, None), P("x", group, None), P("x", group, None))
    return jax.shard_map(
        on_device, mesh=split, in_specs=in_specs, out_specs=out_specs, check_vma=False
    )
```

```python
import functools

import jax
import jax.numpy as jnp
from jax import lax
from jax.experimental import pallas as pl
from jax.experimental.pallas import tpu as pltpu
from jax.sharding import Mesh
from jax.sharding import PartitionSpec as P

student_scale = 0.1
languages = 4
holders = 32
capacity = 192
width = 1024
per_device = 1024
per_language = 256
passages_all = 2048
both = width + passages_all
window = 80
extra = 128
chunk_rows = 64
mib = 1024 * 1024


def slots_of(ids, here):
    turned = lax.rem(ids - here + languages, languages)
    hot = turned == lax.broadcasted_iota(jnp.int32, (8, per_device), 0)
    earlier = lax.broadcasted_iota(jnp.int32, (per_device, per_device), 0)
    later = lax.broadcasted_iota(jnp.int32, (per_device, per_device), 1)
    upper = (earlier <= later).astype(jnp.float32).astype(jnp.bfloat16)
    hot = hot.astype(jnp.float32)
    ranks = jnp.dot(hot.astype(jnp.bfloat16), upper, preferred_element_type=jnp.float32)
    first = lax.broadcasted_iota(jnp.int32, (8, per_device), 0).astype(jnp.float32) * per_language
    return jnp.sum(hot * (ranks - 1.0 + first), axis=0, keepdims=True).astype(jnp.int32)


vmem = pl.BlockSpec(memory_space=pltpu.VMEM)
smem = pl.BlockSpec(memory_space=pltpu.SMEM)
hbm = pl.BlockSpec(memory_space=pltpu.HBM)


def call(kernel, name, in_specs, outs, scratch, limit, flops, transcendentals=0):
    return pl.pallas_call(
        kernel,
        in_specs=in_specs,
        out_specs=[spec for spec, _, _ in outs],
        out_shape=[jax.ShapeDtypeStruct(shape, dtype) for _, shape, dtype in outs],
        scratch_shapes=scratch,
        compiler_params=pltpu.CompilerParams(vmem_limit_bytes=limit * mib),
        cost_estimate=pl.CostEstimate(
            flops=flops, bytes_accessed=8 * mib, transcendentals=transcendentals
        ),
        name=name,
    )


def sort_kernel(
    first, here, ids, slot_in, queries, teacher, out_a, out_b, slot,
    select, block, moved_a, moved_b, in_sem, out_sem,
):
    tile = 512
    tiles = both // tile

    def read(j):
        source = queries if j < width // tile else teacher
        column = j * tile if j < width // tile else j * tile - width
        return pltpu.make_async_copy(
            source.at[:, pl.ds(column, tile)], block.at[j], in_sem.at[j]
        )

    def written(j):
        columns = pl.ds(j * tile, tile)
        return [
            pltpu.make_async_copy(moved_a.at[j], out_a.at[:, columns], out_sem.at[2 * j]),
            pltpu.make_async_copy(moved_b.at[j], out_b.at[:, columns], out_sem.at[2 * j + 1]),
        ]

    for j in range(tiles):
        read(j).start()
    if first:
        slots = slots_of(ids[...], here[0])
        slot[...] = jnp.broadcast_to(slots, (8, per_device))
    else:
        slots = slot_in[0:1, :]
        slot[...] = jnp.zeros((8, 128), jnp.int32)
    rows = lax.broadcasted_iota(jnp.int32, (per_language, per_device), 0)
    for half, number in enumerate((1, 3) if first else (2, 0)):
        hit = rows + number * per_language == slots
        select[pl.ds(half * per_language, per_language), :] = hit.astype(jnp.float32).astype(
            jnp.bfloat16
        )
    for j in range(tiles):
        read(j).wait()
        moved = jnp.dot(select[...], block[j], preferred_element_type=jnp.float32)
        moved_a[j] = moved[:per_language].astype(jnp.bfloat16)
        moved_b[j] = moved[per_language:].astype(jnp.bfloat16)
        for copy in written(j):
            copy.start()
    for j in range(tiles):
        for copy in written(j):
            copy.wait()


def sort_rows(here, ids, slot, queries, teacher):
    first = slot is None
    tiles = both // 512
    moved = pltpu.VMEM((tiles, per_language, 512), jnp.bfloat16)
    out = (hbm, (per_language, both), jnp.bfloat16)
    return call(
        functools.partial(sort_kernel, first),
        "sort_first" if first else "sort_rest",
        [smem, vmem, vmem, hbm, hbm],
        [out, out, (vmem, (8, per_device) if first else (8, 128), jnp.int32)],
        [
            pltpu.VMEM((2 * per_language, per_device), jnp.bfloat16),
            pltpu.VMEM((tiles, per_device, 512), jnp.bfloat16),
            moved,
            moved,
            pltpu.SemaphoreType.DMA((tiles,)),
            pltpu.SemaphoreType.DMA((2 * tiles,)),
        ],
        60 if first else 28,
        4 * per_language * per_device * both,
    )(here, ids, ids if first else slot, queries, teacher)


def kl_parts(value):
    high = value.astype(jnp.bfloat16).astype(jnp.float32)
    middle = (value - high).astype(jnp.bfloat16).astype(jnp.float32)
    low = value - high - middle
    lane = lax.broadcasted_iota(jnp.int32, value.shape, 1)
    parts = jnp.where(
        lane == 0, high, jnp.where(lane == 1, middle, jnp.where(lane == 2, low, 0.0))
    )
    return parts.astype(jnp.bfloat16)


def row_pass(quarter, scores, block, weights, kl):
    for i in range(4):
        local = pl.ds(pl.multiple_of(quarter * 64 + i * 16, 16), 16)
        own = scores[local, :]
        taught = block[local, pl.ds(width, passages_all)].astype(jnp.float32)
        top = jnp.max(own, axis=1, keepdims=True)
        taught_top = jnp.max(taught, axis=1, keepdims=True)
        grown = jnp.exp(own - top)
        total = jnp.sum(grown, axis=1, keepdims=True)
        shifted = taught - taught_top
        taught_grown = jnp.exp(shifted)
        taught_total = jnp.sum(taught_grown, axis=1, keepdims=True)
        cross = jnp.sum(taught_grown * (shifted - (own - top)), axis=1, keepdims=True)
        diverge = cross / taught_total - jnp.log(taught_total) + jnp.log(total)
        weights[local, :] = (
            grown * (student_scale / total) - taught_grown * (student_scale / taught_total)
        ).astype(jnp.bfloat16)
        kl[local, :] = jnp.broadcast_to(diverge, (16, 128))


def score_quarter(block, quarter, passages, scores):
    columns = pl.ds(pl.multiple_of(quarter * 512, 512), 512)
    scores[:, columns] = (
        lax.dot_general(
            block[:, pl.ds(0, width)],
            passages[columns, :],
            (((1,), (1,)), ((), ())),
            preferred_element_type=jnp.float32,
        )
        * student_scale
    )


def teacher_kernel(in0, in1, in2, taught_out, kl):
    for number, block in enumerate((in0, in1, in2)):

        def rows_of(i, carry, number=number, block=block):
            for part in range(4):
                local = pl.ds(pl.multiple_of(i * 64 + part * 16, 16), 16)
                placed = pl.ds(
                    pl.multiple_of(number * per_language + i * 64 + part * 16, 16), 16
                )
                taught = block[local, pl.ds(width, passages_all)].astype(jnp.float32)
                shifted = taught - jnp.max(taught, axis=1, keepdims=True)
                grown = jnp.exp(shifted)
                total = jnp.sum(grown, axis=1, keepdims=True)
                cross = jnp.sum(grown * shifted, axis=1, keepdims=True)
                taught_out[placed, :] = (grown * (student_scale / total)).astype(jnp.bfloat16)
                kl[placed, :] = jnp.broadcast_to(cross / total - jnp.log(total), (16, 128))
            return carry

        lax.fori_loop(0, 4, rows_of, 0)


def teacher_rows(blocks):
    rows = 3 * per_language
    return call(
        teacher_kernel,
        "teacher_rows",
        [vmem] * 3,
        [(vmem, (rows, passages_all), jnp.bfloat16), (vmem, (rows, 128), jnp.float32)],
        [],
        16,
        mib,
        2 * mib,
    )(*blocks)


def student_pass(base, quarter, scores, taught_ref, entropy, weights, kl):
    for i in range(4):
        local = pl.ds(pl.multiple_of(quarter * 64 + i * 16, 16), 16)
        placed = pl.ds(pl.multiple_of(base + quarter * 64 + i * 16, 16), 16)
        own = scores[local, :]
        taught = taught_ref[placed, :].astype(jnp.float32)
        shifted = own - jnp.max(own, axis=1, keepdims=True)
        grown = jnp.exp(shifted)
        total = jnp.sum(grown, axis=1, keepdims=True)
        cross = jnp.sum(taught * shifted, axis=1, keepdims=True)
        diverge = entropy[placed, :] - cross * (1.0 / student_scale) + jnp.log(total)
        weights[placed, :] = (grown * (student_scale / total) - taught).astype(jnp.bfloat16)
        kl[placed, :] = diverge


def first_kernel(
    offsets, counts, raw, in0, in1, in2, taught, entropy, weights, passages, kl,
    raw_v, scores, other_scores, raw_sem,
):
    chunks = capacity // chunk_rows

    def raw_copy(h, c):
        rows = pl.ds(pl.multiple_of(c * chunk_rows, chunk_rows), chunk_rows)
        return pltpu.make_async_copy(
            raw.at[h, rows], raw_v.at[h, rows], raw_sem.at[h * chunks + c]
        )

    def used(h):
        return (counts[h] + chunk_rows - 1) // chunk_rows

    def start_raw(h, carry):
        def start_chunk(c, carry):
            raw_copy(h, c).start()
            return carry

        return lax.fori_loop(0, used(h), start_chunk, carry)

    lax.fori_loop(0, holders, start_raw, 0)
    passages[pl.ds(0, 16), :] = jnp.zeros((16, width), jnp.bfloat16)

    def place(h, carry):
        def place_chunk(c, carry):
            raw_copy(h, c).wait()
            offset = offsets[h] + c * chunk_rows
            start = pl.multiple_of((offset // 16) * 16, 16)
            target = lax.broadcasted_iota(jnp.int32, (window, chunk_rows), 0)
            source = lax.broadcasted_iota(jnp.int32, (window, chunk_rows), 1)
            hit = (target == source + (offset - start)) & (source < counts[h] - c * chunk_rows)
            chosen = hit.astype(jnp.float32).astype(jnp.bfloat16)
            rows = pl.ds(pl.multiple_of(c * chunk_rows, chunk_rows), chunk_rows)
            moved = jnp.dot(
                chosen, raw_v[h, rows, :], preferred_element_type=jnp.float32
            ).astype(jnp.bfloat16)
            head = passages[pl.ds(start, 16), :]
            passages[pl.ds(start, 16), :] = head + moved[:16]
            passages[pl.ds(start + 16, window - 16), :] = moved[16:]
            return carry

        return lax.fori_loop(0, used(h), place_chunk, carry)

    lax.fori_loop(0, holders, place, 0)

    def score_only(quarter, carry):
        score_quarter(in0, quarter, passages, scores)
        return carry

    lax.fori_loop(0, 4, score_only, 0)
    held, free = scores, other_scores
    for number in range(3):

        def together(quarter, carry, number=number, held=held, free=free):
            if number < 2:
                score_quarter((in1, in2)[number], quarter, passages, free)
            student_pass(
                number * per_language, quarter, held, taught, entropy, weights, kl
            )
            return carry

        lax.fori_loop(0, 4, together, 0)
        held, free = free, held


def first_blocks(offsets, counts, raw, blocks, taught, entropy):
    rows = 3 * per_language
    scores = pltpu.VMEM((per_language, passages_all), jnp.float32)
    return call(
        first_kernel,
        "first_blocks",
        [smem] * 2 + [hbm] + [vmem] * 5,
        [
            (vmem, (rows, passages_all), jnp.bfloat16),
            (vmem, (passages_all + 256, width), jnp.bfloat16),
            (vmem, (rows, 128), jnp.float32),
        ],
        [
            pltpu.VMEM((holders, capacity, width), jnp.bfloat16),
            scores,
            scores,
            pltpu.SemaphoreType.DMA((holders * (capacity // chunk_rows),)),
        ],
        38,
        6 * 1024**3,
        2 * mib,
    )(offsets, counts, raw, *blocks, taught, entropy)


def last_kernel(
    core, passages, before, in0, in1, in2, in3, weights, send, keep, kl, scores, total
):
    def score_only(quarter, carry):
        score_quarter(in3, quarter, passages, scores)
        return carry

    lax.fori_loop(0, 4, score_only, 0)
    contract = (((0,), (0,)), ((), ()))

    def together(quarter, carry):
        row_pass(quarter, scores, in3, weights, kl)
        columns = pl.ds(pl.multiple_of(quarter * 512, 512), 512)
        part = None
        for number, block in enumerate((in0, in1, in2)):
            rows = pl.ds(number * per_language, per_language)
            term = lax.dot_general(
                before[rows, columns],
                block[:, pl.ds(0, width)],
                contract,
                preferred_element_type=jnp.float32,
            )
            part = term if part is None else part + term
        total[columns, :] = part
        return carry

    lax.fori_loop(0, 4, together, 0)
    even = core[0] == 0

    def reduce(j, carry):
        columns = pl.ds(pl.multiple_of(j * 256, 256), 256)
        grad = lax.dot_general(
            weights[:, columns],
            in3[:, pl.ds(0, width)],
            contract,
            preferred_element_type=jnp.float32,
        )
        grad = (grad + total[columns, :]).astype(jnp.bfloat16)
        for part in range(2):
            upper = grad[part * 128 : part * 128 + 64]
            lower = grad[part * 128 + 64 : part * 128 + 128]
            rows = pl.ds(pl.multiple_of(j * 128 + part * 64, 64), 64)
            keep[rows, :] = jnp.where(even, upper, lower)
            send[rows, :] = jnp.where(even, lower, upper)
        return carry

    lax.fori_loop(0, passages_all // 256, reduce, 0)


def last_block(core, passages, weights, blocks):
    half = (vmem, (passages_all // 2, width), jnp.bfloat16)
    return call(
        last_kernel,
        "last_block",
        [smem] + [vmem] * 6,
        [
            (vmem, (per_language, passages_all), jnp.bfloat16),
            half,
            half,
            (vmem, (per_language, 128), jnp.float32),
        ],
        [
            pltpu.VMEM((per_language, passages_all), jnp.float32),
            pltpu.VMEM((passages_all, width), jnp.float32),
        ],
        20,
        6 * 1024**3,
        mib,
    )(core, passages, weights, *blocks)


def query_kernel(places, *refs):
    count = len(places)
    weights, kls = refs[:count], refs[count : 2 * count]
    passages, outs = refs[2 * count], refs[2 * count + 1 :]
    for place, block, kl, out in zip(places, weights, kls, outs):
        rows = pl.ds(place * per_language, per_language)

        def step(half, carry, rows=rows, block=block, out=out):
            columns = pl.ds(pl.multiple_of(half * 512, 512), 512)
            out[:, columns] = jnp.dot(
                block[rows, :],
                passages[pl.ds(0, passages_all), columns],
                preferred_element_type=jnp.float32,
            ).astype(jnp.bfloat16)
            return carry

        lax.fori_loop(0, 2, step, 0)
        out[:, pl.ds(width, extra)] = kl_parts(kl[rows, :])


def query_grads(places, weights, kls, passages):
    return call(
        functools.partial(query_kernel, places),
        "query_grads",
        [vmem] * (2 * len(places) + 1),
        [(vmem, (per_language, width + extra), jnp.bfloat16)] * len(places),
        [],
        8,
        len(places) * 1024**3,
    )(*weights, *kls, passages)


def pair_kernel(keep, other, out):
    def step(i, carry):
        rows = pl.ds(pl.multiple_of(i * 64, 64), 64)
        out[rows, :] = (
            keep[rows, :].astype(jnp.float32) + other[rows, :].astype(jnp.float32)
        ).astype(jnp.bfloat16)
        return carry

    lax.fori_loop(0, passages_all // 128, step, 0)


def pair_sum(keep, other):
    return call(
        pair_kernel, "pair_sum", [vmem] * 2, [(vmem, keep.shape, jnp.bfloat16)], [], 8, mib
    )(keep, other)[0]


def restore_kernel(slot, in0, in1, in2, in3, grads, kl, select):
    rows = lax.broadcasted_iota(jnp.int32, (per_device, per_device), 0)
    select[...] = (rows == slot[0:1, :]).astype(jnp.float32).astype(jnp.bfloat16)
    contract = (((0,), (0,)), ((), ()))

    def joined(columns):
        part = None
        for number, block in enumerate((in0, in1, in2, in3)):
            chosen = select[number * per_language : (number + 1) * per_language, :]
            term = lax.dot_general(
                chosen, block[:, columns], contract, preferred_element_type=jnp.float32
            )
            part = term if part is None else part + term
        return part

    def step(j, carry):
        columns = pl.ds(pl.multiple_of(j * 256, 256), 256)
        grads[:, columns] = joined(columns).astype(jnp.bfloat16)
        return carry

    lax.fori_loop(0, width // 256, step, 0)
    column = jnp.sum(joined(pl.ds(width, extra)), axis=1, keepdims=True)
    kl[...] = jnp.transpose(jnp.broadcast_to(column, (per_device, 128)))[:8]


def restore(slot, blocks):
    return call(
        restore_kernel,
        "restore",
        [vmem] * 5,
        [
            (vmem, (per_device, width), jnp.bfloat16),
            (vmem, (8, per_device), jnp.float32),
        ],
        [pltpu.VMEM((per_device, per_device), jnp.bfloat16)],
        24,
        2 * 1024**3,
    )(slot, *blocks)


def shift(array, by):
    pairs = [(i, (i + by) % languages) for i in range(languages)]
    return lax.ppermute(array, "x", pairs)


def on_device(queries, bucket_ids, raw_passages, counts, teacher):
    group = ("y", "z", "c")
    here = lax.axis_index("x").astype(jnp.int32).reshape(1)
    core = lax.axis_index("c").astype(jnp.int32).reshape(1)
    all_raw = lax.all_gather(raw_passages[0], group, axis=0, tiled=True)
    ids = bucket_ids[0]
    out1, out3, slot = sort_rows(here, ids, None, queries[0, 0], teacher[0, 0])
    in1, in3 = shift(out1, 1), shift(out3, 3)
    out2, in0, _ = sort_rows(here, ids, slot, queries[0, 0], teacher[0, 0])
    held_counts, in0, out2 = lax.optimization_barrier((counts, in0, out2))
    holder_counts = lax.all_gather(held_counts[0], group, axis=0, tiled=True)
    earlier = jnp.arange(holders)[None, :] < jnp.arange(holders)[:, None]
    offsets = jnp.sum(jnp.where(earlier, holder_counts[None, :], 0), axis=1).astype(jnp.int32)
    out2, in1, in3, offsets = lax.optimization_barrier((out2, in1, in3, offsets))
    in2 = shift(out2, 2)
    taught, entropy = teacher_rows((in0, in1, in3))
    all_raw, taught, entropy = lax.optimization_barrier((all_raw, taught, entropy))
    weights, passages, kl = first_blocks(
        offsets, holder_counts, all_raw, (in0, in1, in3), taught, entropy
    )
    back1, back3 = query_grads((1, 2), (weights, weights), (kl, kl), passages)
    in2, back1, back3 = lax.optimization_barrier((in2, back1, back3))
    home1, home3 = shift(back1, -1), shift(back3, -3)
    last_weights, send, keep, last_kl = last_block(core, passages, weights, (in0, in1, in3, in2))
    other = lax.ppermute(send, "c", [(0, 1), (1, 0)])
    paired = pair_sum(keep, other)
    spread = lax.all_to_all(
        paired.reshape(16, 64, width), ("y", "z"), split_axis=0, concat_axis=0, tiled=True
    )
    paired, last_weights, home1, home3 = lax.optimization_barrier(
        (paired, last_weights, home1, home3)
    )
    back2, back0 = query_grads((0, 0), (last_weights, weights), (last_kl, kl), passages)
    home2 = shift(back2, -2)
    grad_passages = jnp.sum(spread.astype(jnp.float32), axis=0).astype(jnp.bfloat16)
    grad_queries, kl_rows = restore(slot, (back0, home1, home2, home3))
    return (grad_queries[None, None], grad_passages[None], kl_rows[0][None, None])


def solution(mesh):
    split = Mesh(mesh.devices.reshape(4, 4, 4, 2), ("x", "y", "z", "c"))
    group = ("y", "z", "c")
    in_specs = (
        P("x", group, None, None),
        P("x", group, None),
        P("x", group, None, None),
        P("x", group),
        P("x", group, None, None),
    )
    out_specs = (P("x", group, None, None), P("x", group, None), P("x", group, None))
    return jax.shard_map(
        on_device, mesh=split, in_specs=in_specs, out_specs=out_specs, check_vma=False
    )
```

```python
import functools

import jax
import jax.numpy as jnp
from jax import lax
from jax.experimental import pallas as pl
from jax.experimental.pallas import tpu as pltpu
from jax.sharding import Mesh
from jax.sharding import PartitionSpec as P

student_scale = 0.1
languages = 4
holders = 32
capacity = 192
width = 1024
per_device = 1024
per_language = 256
passages_all = 2048
both = width + passages_all
group_chunks = 4
group_rows = 256
window = 272
extra = 128
chunk_rows = 64
chunk_count = 64
mib = 1024 * 1024


def slots_of(ids, here):
    turned = lax.rem(ids - here + languages, languages)
    hot = turned == lax.broadcasted_iota(jnp.int32, (8, per_device), 0)
    earlier = lax.broadcasted_iota(jnp.int32, (per_device, per_device), 0)
    later = lax.broadcasted_iota(jnp.int32, (per_device, per_device), 1)
    upper = (earlier <= later).astype(jnp.float32).astype(jnp.bfloat16)
    hot = hot.astype(jnp.float32)
    ranks = jnp.dot(hot.astype(jnp.bfloat16), upper, preferred_element_type=jnp.float32)
    first = lax.broadcasted_iota(jnp.int32, (8, per_device), 0).astype(jnp.float32) * per_language
    return jnp.sum(hot * (ranks - 1.0 + first), axis=0, keepdims=True).astype(jnp.int32)


vmem = pl.BlockSpec(memory_space=pltpu.VMEM)
smem = pl.BlockSpec(memory_space=pltpu.SMEM)
hbm = pl.BlockSpec(memory_space=pltpu.HBM)


def call(kernel, name, in_specs, outs, scratch, limit, flops, transcendentals=0):
    return pl.pallas_call(
        kernel,
        in_specs=in_specs,
        out_specs=[spec for spec, _, _ in outs],
        out_shape=[jax.ShapeDtypeStruct(shape, dtype) for _, shape, dtype in outs],
        scratch_shapes=scratch,
        compiler_params=pltpu.CompilerParams(vmem_limit_bytes=limit * mib),
        cost_estimate=pl.CostEstimate(
            flops=flops, bytes_accessed=8 * mib, transcendentals=transcendentals
        ),
        name=name,
    )


def sort_kernel(
    first, here, ids, slot_in, queries, teacher, out_a, out_b, slot,
    select, block, moved_a, moved_b, in_sem, out_sem,
):
    tile = 512
    tiles = both // tile

    def read(j):
        source = queries if j < width // tile else teacher
        column = j * tile if j < width // tile else j * tile - width
        return pltpu.make_async_copy(
            source.at[:, pl.ds(column, tile)], block.at[j], in_sem.at[j]
        )

    def written(j):
        columns = pl.ds(j * tile, tile)
        return [
            pltpu.make_async_copy(moved_a.at[j], out_a.at[:, columns], out_sem.at[2 * j]),
            pltpu.make_async_copy(moved_b.at[j], out_b.at[:, columns], out_sem.at[2 * j + 1]),
        ]

    for j in range(tiles):
        read(j).start()
    if first:
        slots = slots_of(ids[...], here[0])
        slot[...] = jnp.broadcast_to(slots, (8, per_device))
    else:
        slots = slot_in[0:1, :]
        slot[...] = jnp.zeros((8, 128), jnp.int32)
    rows = lax.broadcasted_iota(jnp.int32, (per_language, per_device), 0)
    for half, number in enumerate((1, 3) if first else (2, 0)):
        hit = rows + number * per_language == slots
        select[pl.ds(half * per_language, per_language), :] = hit.astype(jnp.float32).astype(
            jnp.bfloat16
        )
    for j in range(tiles):
        read(j).wait()
        moved = jnp.dot(select[...], block[j], preferred_element_type=jnp.float32)
        moved_a[j] = moved[:per_language].astype(jnp.bfloat16)
        moved_b[j] = moved[per_language:].astype(jnp.bfloat16)
        for copy in written(j):
            copy.start()
    for j in range(tiles):
        for copy in written(j):
            copy.wait()


def sort_rows(here, ids, slot, queries, teacher):
    first = slot is None
    tiles = both // 512
    moved = pltpu.VMEM((tiles, per_language, 512), jnp.bfloat16)
    out = (hbm, (per_language, both), jnp.bfloat16)
    return call(
        functools.partial(sort_kernel, first),
        "sort_first" if first else "sort_rest",
        [smem, vmem, vmem, hbm, hbm],
        [out, out, (vmem, (8, per_device) if first else (8, 128), jnp.int32)],
        [
            pltpu.VMEM((2 * per_language, per_device), jnp.bfloat16),
            pltpu.VMEM((tiles, per_device, 512), jnp.bfloat16),
            moved,
            moved,
            pltpu.SemaphoreType.DMA((tiles,)),
            pltpu.SemaphoreType.DMA((2 * tiles,)),
        ],
        60 if first else 28,
        4 * per_language * per_device * both,
    )(here, ids, ids if first else slot, queries, teacher)


def kl_parts(value):
    high = value.astype(jnp.bfloat16).astype(jnp.float32)
    middle = (value - high).astype(jnp.bfloat16).astype(jnp.float32)
    low = value - high - middle
    lane = lax.broadcasted_iota(jnp.int32, value.shape, 1)
    parts = jnp.where(
        lane == 0, high, jnp.where(lane == 1, middle, jnp.where(lane == 2, low, 0.0))
    )
    return parts.astype(jnp.bfloat16)


def row_pass(quarter, scores, block, weights, kl):
    for i in range(4):
        local = pl.ds(pl.multiple_of(quarter * 64 + i * 16, 16), 16)
        own = scores[local, :]
        taught = block[local, :].astype(jnp.float32)
        top = jnp.max(own, axis=1, keepdims=True)
        taught_top = jnp.max(taught, axis=1, keepdims=True)
        grown = jnp.exp(own - top)
        total = jnp.sum(grown, axis=1, keepdims=True)
        shifted = taught - taught_top
        taught_grown = jnp.exp(shifted)
        taught_total = jnp.sum(taught_grown, axis=1, keepdims=True)
        cross = jnp.sum(taught_grown * (shifted - (own - top)), axis=1, keepdims=True)
        diverge = cross / taught_total - jnp.log(taught_total) + jnp.log(total)
        weights[local, :] = (
            grown * (student_scale / total) - taught_grown * (student_scale / taught_total)
        ).astype(jnp.bfloat16)
        kl[local, :] = jnp.broadcast_to(diverge, (16, 128))


def score_quarter(queries, base, quarter, passages, scores):
    columns = pl.ds(pl.multiple_of(quarter * 512, 512), 512)
    scores[:, columns] = (
        lax.dot_general(
            queries[pl.ds(base, per_language), :],
            passages[columns, :],
            (((1,), (1,)), ((), ())),
            preferred_element_type=jnp.float32,
        )
        * student_scale
    )


def teacher_kernel(in0, in1, in2, taught_out, queries, kl):
    for number, block in enumerate((in0, in1, in2)):

        def rows_of(i, carry, number=number, block=block):
            for part in range(4):
                local = pl.ds(pl.multiple_of(i * 64 + part * 16, 16), 16)
                placed = pl.ds(
                    pl.multiple_of(number * per_language + i * 64 + part * 16, 16), 16
                )
                queries[placed, :] = block[local, pl.ds(0, width)]
                taught = block[local, pl.ds(width, passages_all)].astype(jnp.float32)
                shifted = taught - jnp.max(taught, axis=1, keepdims=True)
                grown = jnp.exp(shifted)
                total = jnp.sum(grown, axis=1, keepdims=True)
                cross = jnp.sum(grown * shifted, axis=1, keepdims=True)
                taught_out[placed, :] = (grown * (student_scale / total)).astype(jnp.bfloat16)
                kl[placed, :] = jnp.broadcast_to(cross / total - jnp.log(total), (16, 128))
            return carry

        lax.fori_loop(0, 4, rows_of, 0)


def teacher_rows(blocks):
    rows = 3 * per_language
    return call(
        teacher_kernel,
        "teacher_rows",
        [vmem] * 3,
        [
            (vmem, (rows, passages_all), jnp.bfloat16),
            (vmem, (rows, width), jnp.bfloat16),
            (vmem, (rows, 128), jnp.float32),
        ],
        [],
        16,
        mib,
        2 * mib,
    )(*blocks)


def student_pass(base, quarter, scores, taught_ref, weights, kl):
    for i in range(4):
        local = pl.ds(pl.multiple_of(quarter * 64 + i * 16, 16), 16)
        placed = pl.ds(pl.multiple_of(base + quarter * 64 + i * 16, 16), 16)
        own = scores[local, :]
        taught = taught_ref[placed, :].astype(jnp.float32)
        shifted = own - jnp.max(own, axis=1, keepdims=True)
        grown = jnp.exp(shifted)
        total = jnp.sum(grown, axis=1, keepdims=True)
        cross = jnp.sum(taught * shifted, axis=1, keepdims=True)
        diverge = jnp.log(total) - cross * (1.0 / student_scale)
        weights[placed, :] = (grown * (student_scale / total) - taught).astype(jnp.bfloat16)
        kl[placed, :] = jnp.broadcast_to(diverge, (16, 128))


def first_kernel(
    holder_of, row_of, place_of, target_of, raw, queries, taught,
    weights, passages, kl, raw_v, scores, other_scores, raw_sem,
):
    def raw_copy(k):
        rows = pl.ds(pl.multiple_of(row_of[k], chunk_rows), chunk_rows)
        return pltpu.make_async_copy(raw.at[holder_of[k], rows], raw_v.at[k], raw_sem.at[k])

    def start_raw(k, carry):
        raw_copy(k).start()
        return carry

    lax.fori_loop(0, chunk_count, start_raw, 0, unroll=4)
    passages[pl.ds(0, 16), :] = jnp.zeros((16, width), jnp.bfloat16)

    def place(g, carry):
        for c in range(group_chunks):
            raw_copy(g * group_chunks + c).wait()
        start = pl.multiple_of((place_of[g * group_chunks] // 16) * 16, 16)
        target = lax.broadcasted_iota(jnp.int32, (window, group_rows), 0)
        hit = target == target_of[pl.ds(g, 1), :] - start
        chosen = hit.astype(jnp.float32).astype(jnp.bfloat16)
        chunks = raw_v[pl.ds(g * group_chunks, group_chunks)].reshape(group_rows, width)
        moved = jnp.dot(chosen, chunks, preferred_element_type=jnp.float32).astype(jnp.bfloat16)
        head = passages[pl.ds(start, 16), :]
        passages[pl.ds(start, 16), :] = head + moved[:16]
        passages[pl.ds(start + 16, window - 16), :] = moved[16:]
        return carry

    lax.fori_loop(0, chunk_count // group_chunks, place, 0)

    def score_only(quarter, carry):
        score_quarter(queries, 0, quarter, passages, scores)
        return carry

    lax.fori_loop(0, 4, score_only, 0)
    held, free = scores, other_scores
    for number in range(3):
        base = number * per_language

        def together(quarter, carry, base=base, held=held, free=free, last=number == 2):
            if not last:
                score_quarter(queries, base + per_language, quarter, passages, free)
            student_pass(base, quarter, held, taught, weights, kl)
            return carry

        lax.fori_loop(0, 4, together, 0)
        held, free = free, held


def first_blocks(chunk_list, raw, queries, taught):
    rows = 3 * per_language
    scores = pltpu.VMEM((per_language, passages_all), jnp.float32)
    return call(
        first_kernel,
        "first_blocks",
        [smem] * 3 + [vmem, hbm] + [vmem] * 2,
        [
            (vmem, (rows, passages_all), jnp.bfloat16),
            (vmem, (passages_all + window, width), jnp.bfloat16),
            (vmem, (rows, 128), jnp.float32),
        ],
        [
            pltpu.VMEM((chunk_count, chunk_rows, width), jnp.bfloat16),
            scores,
            scores,
            pltpu.SemaphoreType.DMA((chunk_count,)),
        ],
        40,
        6 * 1024**3,
        2 * mib,
    )(*chunk_list, raw, queries, taught)


def chunks_of(counts):
    number = (counts + chunk_rows - 1) // chunk_rows
    upto = jnp.arange(holders)[None, :] < jnp.arange(holders)[:, None]
    offsets = jnp.sum(jnp.where(upto, counts[None, :], 0), axis=1)
    firsts = jnp.sum(jnp.where(upto, number[None, :], 0), axis=1)
    index = jnp.arange(chunk_count)[:, None]
    mine = (index >= firsts[None, :]) & (index < (firsts + number)[None, :])
    row = (index - firsts[None, :]) * chunk_rows

    def pick(values):
        return jnp.sum(jnp.where(mine, values, 0), axis=1)

    holder = pick(jnp.arange(holders)[None, :] + 0 * row)
    used = pick(jnp.minimum(counts[None, :] - row, chunk_rows))
    place = jnp.where(used > 0, pick(offsets[None, :] + row), passages_all)
    slots = jnp.arange(chunk_rows)[None, :]
    targets = jnp.where(slots < used[:, None], place[:, None] + slots, -1)
    return (
        holder.astype(jnp.int32),
        pick(row).astype(jnp.int32),
        place.astype(jnp.int32),
        targets.astype(jnp.int32).reshape(chunk_count // group_chunks, group_rows),
    )


def last_kernel(
    core, passages, before, queries, block, weights, send, keep, kl, scores, total
):
    own = block.at[:, pl.ds(0, width)]
    teacher = block.at[:, pl.ds(width, passages_all)]

    def score_only(quarter, carry):
        score_quarter(own, 0, quarter, passages, scores)
        return carry

    lax.fori_loop(0, 4, score_only, 0)
    contract = (((0,), (0,)), ((), ()))

    def together(quarter, carry):
        row_pass(quarter, scores, teacher, weights, kl)
        columns = pl.ds(pl.multiple_of(quarter * 512, 512), 512)
        total[columns, :] = lax.dot_general(
            before[:, columns],
            queries[...],
            contract,
            preferred_element_type=jnp.float32,
        )
        return carry

    lax.fori_loop(0, 4, together, 0)
    even = core[0] == 0

    def reduce(j, carry):
        columns = pl.ds(pl.multiple_of(j * 256, 256), 256)
        grad = lax.dot_general(
            weights[:, columns],
            own[...],
            contract,
            preferred_element_type=jnp.float32,
        )
        grad = (grad + total[columns, :]).astype(jnp.bfloat16)
        for part in range(2):
            upper = grad[part * 128 : part * 128 + 64]
            lower = grad[part * 128 + 64 : part * 128 + 128]
            rows = pl.ds(pl.multiple_of(j * 128 + part * 64, 64), 64)
            keep[rows, :] = jnp.where(even, upper, lower)
            send[rows, :] = jnp.where(even, lower, upper)
        return carry

    lax.fori_loop(0, passages_all // 256, reduce, 0)


def last_block(core, passages, weights, queries, block):
    half = (vmem, (passages_all // 2, width), jnp.bfloat16)
    return call(
        last_kernel,
        "last_block",
        [smem] + [vmem] * 4,
        [
            (vmem, (per_language, passages_all), jnp.bfloat16),
            half,
            half,
            (vmem, (per_language, 128), jnp.float32),
        ],
        [
            pltpu.VMEM((per_language, passages_all), jnp.float32),
            pltpu.VMEM((passages_all, width), jnp.float32),
        ],
        20,
        6 * 1024**3,
        mib,
    )(core, passages, weights, queries, block)


def query_kernel(weights, last_weights, kl, entropy, last_kl, passages, *outs):
    for number, out in enumerate(outs):
        rows = pl.ds((number % 3) * per_language, per_language)
        block = weights if number < 3 else last_weights

        def step(half, carry, rows=rows, block=block, out=out):
            columns = pl.ds(pl.multiple_of(half * 512, 512), 512)
            out[:, columns] = jnp.dot(
                block[rows, :],
                passages[pl.ds(0, passages_all), columns],
                preferred_element_type=jnp.float32,
            ).astype(jnp.bfloat16)
            return carry

        lax.fori_loop(0, 2, step, 0)
        value = kl[rows, :] + entropy[rows, :] if number < 3 else last_kl[...]
        out[:, pl.ds(width, extra)] = kl_parts(value)


def query_grads(weights, last_weights, kl, entropy, last_kl, passages):
    return call(
        query_kernel,
        "query_grads",
        [vmem] * 6,
        [(vmem, (per_language, width + extra), jnp.bfloat16)] * languages,
        [],
        8,
        4 * 1024**3,
    )(weights, last_weights, kl, entropy, last_kl, passages)


def pair_kernel(keep, other, out, paired, sems):
    chunk = 256

    def written(i):
        rows = pl.ds(pl.multiple_of(i * chunk, chunk), chunk)
        return pltpu.make_async_copy(paired.at[rows], out.at[rows], sems.at[i])

    def step(i, carry):
        for j in range(4):
            rows = pl.ds(pl.multiple_of(i * chunk + j * 64, 64), 64)
            paired[rows, :] = (
                keep[rows, :].astype(jnp.float32) + other[rows, :].astype(jnp.float32)
            ).astype(jnp.bfloat16)
        written(i).start()
        return carry

    lax.fori_loop(0, 4, step, 0)
    for i in range(4):
        written(i).wait()


def pair_sum(keep, other):
    return call(
        pair_kernel,
        "pair_sum",
        [vmem] * 2,
        [(hbm, keep.shape, jnp.bfloat16)],
        [pltpu.VMEM(keep.shape, jnp.bfloat16), pltpu.SemaphoreType.DMA((4,))],
        8,
        mib,
    )(keep, other)[0]


def restore_kernel(slot, in0, in1, in2, in3, grads, kl, select):
    rows = lax.broadcasted_iota(jnp.int32, (per_device, per_device), 0)
    select[...] = (rows == slot[0:1, :]).astype(jnp.float32).astype(jnp.bfloat16)
    contract = (((0,), (0,)), ((), ()))

    def joined(columns):
        part = None
        for number, block in enumerate((in0, in1, in2, in3)):
            chosen = select[number * per_language : (number + 1) * per_language, :]
            term = lax.dot_general(
                chosen, block[:, columns], contract, preferred_element_type=jnp.float32
            )
            part = term if part is None else part + term
        return part

    def step(j, carry):
        columns = pl.ds(pl.multiple_of(j * 256, 256), 256)
        grads[:, columns] = joined(columns).astype(jnp.bfloat16)
        return carry

    lax.fori_loop(0, width // 256, step, 0)
    column = jnp.sum(joined(pl.ds(width, extra)), axis=1, keepdims=True)
    kl[...] = jnp.transpose(jnp.broadcast_to(column, (per_device, 128)))[:8]


def restore(slot, blocks):
    return call(
        restore_kernel,
        "restore",
        [vmem] * 5,
        [
            (vmem, (per_device, width), jnp.bfloat16),
            (vmem, (8, per_device), jnp.float32),
        ],
        [pltpu.VMEM((per_device, per_device), jnp.bfloat16)],
        24,
        2 * 1024**3,
    )(slot, *blocks)


def shift(array, by):
    pairs = [(i, (i + by) % languages) for i in range(languages)]
    return lax.ppermute(array, "x", pairs)


def on_device(queries, bucket_ids, raw_passages, counts, teacher):
    group = ("y", "z", "c")
    here = lax.axis_index("x").astype(jnp.int32).reshape(1)
    core = lax.axis_index("c").astype(jnp.int32).reshape(1)
    all_raw = lax.all_gather(raw_passages[0], group, axis=0, tiled=True)
    ids = bucket_ids[0]
    out1, out3, slot = sort_rows(here, ids, None, queries[0, 0], teacher[0, 0])
    in1, in3 = shift(out1, 1), shift(out3, 3)
    out2, in0, _ = sort_rows(here, ids, slot, queries[0, 0], teacher[0, 0])
    held_counts, in0, out2 = lax.optimization_barrier((counts, in0, out2))
    holder_counts = lax.all_gather(held_counts[0], group, axis=0, tiled=True)
    chunk_list = chunks_of(holder_counts)
    out2, in1, in3, chunk_list = lax.optimization_barrier((out2, in1, in3, chunk_list))
    in2 = shift(out2, 2)
    taught, moved, entropy = teacher_rows((in0, in1, in3))
    all_raw, taught, moved, entropy = lax.optimization_barrier((all_raw, taught, moved, entropy))
    weights, passages, kl = first_blocks(chunk_list, all_raw, moved, taught)
    last_weights, send, keep, last_kl = last_block(core, passages, weights, moved, in2)
    other = lax.ppermute(send, "c", [(0, 1), (1, 0)])
    back0, back1, back3, back2 = query_grads(
        weights, last_weights, kl, entropy, last_kl, passages
    )
    other, back1, back2, back3 = lax.optimization_barrier((other, back1, back2, back3))
    home1, home3, home2 = shift(back1, -1), shift(back3, -3), shift(back2, -2)
    paired = pair_sum(keep, other)
    spread = lax.all_to_all(
        paired.reshape(16, 64, width), ("y", "z"), split_axis=0, concat_axis=0, tiled=True
    )
    grad_passages = jnp.sum(spread.astype(jnp.float32), axis=0).astype(jnp.bfloat16)
    grad_queries, kl_rows = restore(slot, (back0, home1, home2, home3))
    return (grad_queries[None, None], grad_passages[None], kl_rows[0][None, None])


def solution(mesh):
    split = Mesh(mesh.devices.reshape(4, 4, 4, 2), ("x", "y", "z", "c"))
    group = ("y", "z", "c")
    in_specs = (
        P("x", group, None, None),
        P("x", group, None),
        P("x", group, None, None),
        P("x", group),
        P("x", group, None, None),
    )
    out_specs = (P("x", group, None, None), P("x", group, None), P("x", group, None))
    return jax.shard_map(
        on_device, mesh=split, in_specs=in_specs, out_specs=out_specs, check_vma=False
    )
```

```python
import functools

import jax
import jax.numpy as jnp
from jax import lax
from jax.experimental import pallas as pl
from jax.experimental.pallas import tpu as pltpu
from jax.sharding import Mesh
from jax.sharding import PartitionSpec as P

student_scale = 0.1
languages = 4
holders = 32
capacity = 192
width = 1024
per_device = 1024
per_language = 256
passages_all = 2048
both = width + passages_all
group_chunks = 4
group_rows = 256
window = 272
extra = 128
chunk_rows = 64
chunk_count = 64
store_rows = 6144
mib = 1024 * 1024


def slots_of(ids, here):
    turned = lax.rem(ids - here + languages, languages)
    hot = turned == lax.broadcasted_iota(jnp.int32, (8, per_device), 0)
    earlier = lax.broadcasted_iota(jnp.int32, (per_device, per_device), 0)
    later = lax.broadcasted_iota(jnp.int32, (per_device, per_device), 1)
    upper = (earlier <= later).astype(jnp.float32).astype(jnp.bfloat16)
    hot = hot.astype(jnp.float32)
    ranks = jnp.dot(hot.astype(jnp.bfloat16), upper, preferred_element_type=jnp.float32)
    first = lax.broadcasted_iota(jnp.int32, (8, per_device), 0).astype(jnp.float32) * per_language
    return jnp.sum(hot * (ranks - 1.0 + first), axis=0, keepdims=True).astype(jnp.int32)


vmem = pl.BlockSpec(memory_space=pltpu.VMEM)
smem = pl.BlockSpec(memory_space=pltpu.SMEM)
hbm = pl.BlockSpec(memory_space=pltpu.HBM)


def call(kernel, name, in_specs, outs, scratch, limit, flops, transcendentals=0):
    return pl.pallas_call(
        kernel,
        in_specs=in_specs,
        out_specs=[spec for spec, _, _ in outs],
        out_shape=[jax.ShapeDtypeStruct(shape, dtype) for _, shape, dtype in outs],
        scratch_shapes=scratch,
        compiler_params=pltpu.CompilerParams(vmem_limit_bytes=limit * mib),
        cost_estimate=pl.CostEstimate(
            flops=flops, bytes_accessed=8 * mib, transcendentals=transcendentals
        ),
        name=name,
    )


def sort_kernel(
    first, here, ids, slot_in, queries, teacher, out_a, out_b, slot,
    select, block, moved_a, moved_b, in_sem, out_sem,
):
    tile = 512
    tiles = both // tile

    def read(j):
        source = queries if j < width // tile else teacher
        column = j * tile if j < width // tile else j * tile - width
        return pltpu.make_async_copy(
            source.at[:, pl.ds(column, tile)], block.at[j], in_sem.at[j]
        )

    def written(j):
        columns = pl.ds(j * tile, tile)
        return [
            pltpu.make_async_copy(moved_a.at[j], out_a.at[:, columns], out_sem.at[2 * j]),
            pltpu.make_async_copy(moved_b.at[j], out_b.at[:, columns], out_sem.at[2 * j + 1]),
        ]

    for j in range(tiles):
        read(j).start()
    if first:
        slots = slots_of(ids[...], here[0])
        slot[...] = jnp.broadcast_to(slots, (8, per_device))
    else:
        slots = slot_in[0:1, :]
        slot[...] = jnp.zeros((8, 128), jnp.int32)
    rows = lax.broadcasted_iota(jnp.int32, (per_language, per_device), 0)
    for half, number in enumerate((1, 3) if first else (2, 0)):
        hit = rows + number * per_language == slots
        select[pl.ds(half * per_language, per_language), :] = hit.astype(jnp.float32).astype(
            jnp.bfloat16
        )
    for j in range(tiles):
        read(j).wait()
        moved = jnp.dot(select[...], block[j], preferred_element_type=jnp.float32)
        moved_a[j] = moved[:per_language].astype(jnp.bfloat16)
        moved_b[j] = moved[per_language:].astype(jnp.bfloat16)
        for copy in written(j):
            copy.start()
    for j in range(tiles):
        for copy in written(j):
            copy.wait()


def sort_rows(here, ids, slot, queries, teacher):
    first = slot is None
    tiles = both // 512
    moved = pltpu.VMEM((tiles, per_language, 512), jnp.bfloat16)
    out = (hbm, (per_language, both), jnp.bfloat16)
    return call(
        functools.partial(sort_kernel, first),
        "sort_first" if first else "sort_rest",
        [smem, vmem, vmem, hbm, hbm],
        [out, out, (vmem, (8, per_device) if first else (8, 128), jnp.int32)],
        [
            pltpu.VMEM((2 * per_language, per_device), jnp.bfloat16),
            pltpu.VMEM((tiles, per_device, 512), jnp.bfloat16),
            moved,
            moved,
            pltpu.SemaphoreType.DMA((tiles,)),
            pltpu.SemaphoreType.DMA((2 * tiles,)),
        ],
        60 if first else 28,
        4 * per_language * per_device * both,
    )(here, ids, ids if first else slot, queries, teacher)


def kl_parts(value):
    high = value.astype(jnp.bfloat16).astype(jnp.float32)
    middle = (value - high).astype(jnp.bfloat16).astype(jnp.float32)
    low = value - high - middle
    lane = lax.broadcasted_iota(jnp.int32, value.shape, 1)
    parts = jnp.where(
        lane == 0, high, jnp.where(lane == 1, middle, jnp.where(lane == 2, low, 0.0))
    )
    return parts.astype(jnp.bfloat16)


def row_pass(quarter, scores, block, weights, kl):
    for i in range(4):
        local = pl.ds(pl.multiple_of(quarter * 64 + i * 16, 16), 16)
        own = scores[local, :]
        taught = block[local, :].astype(jnp.float32)
        top = jnp.max(own, axis=1, keepdims=True)
        taught_top = jnp.max(taught, axis=1, keepdims=True)
        grown = jnp.exp(own - top)
        total = jnp.sum(grown, axis=1, keepdims=True)
        shifted = taught - taught_top
        taught_grown = jnp.exp(shifted)
        taught_total = jnp.sum(taught_grown, axis=1, keepdims=True)
        cross = jnp.sum(taught_grown * (shifted - (own - top)), axis=1, keepdims=True)
        diverge = cross / taught_total - jnp.log(taught_total) + jnp.log(total)
        weights[local, :] = (
            grown * (student_scale / total) - taught_grown * (student_scale / taught_total)
        ).astype(jnp.bfloat16)
        kl[local, :] = jnp.broadcast_to(diverge, (16, 128))


def score_quarter(queries, base, quarter, passages, scores):
    columns = pl.ds(pl.multiple_of(quarter * 512, 512), 512)
    scores[:, columns] = (
        lax.dot_general(
            queries[pl.ds(base, per_language), :],
            passages[columns, :],
            (((1,), (1,)), ((), ())),
            preferred_element_type=jnp.float32,
        )
        * student_scale
    )


def teacher_kernel(in0, in1, in2, store, queries, kl, taught_out, sems):
    rows = 3 * per_language

    def saved(number):
        block = pl.ds(number * per_language, per_language)
        behind = pl.ds(rows + number * per_language, per_language)
        return [
            pltpu.make_async_copy(taught_out.at[block], store.at[block], sems.at[2 * number]),
            pltpu.make_async_copy(
                queries.at[block], store.at[behind, pl.ds(0, width)], sems.at[2 * number + 1]
            ),
        ]

    for number, block in enumerate((in0, in1, in2)):

        def rows_of(i, carry, number=number, block=block):
            for part in range(4):
                local = pl.ds(pl.multiple_of(i * 64 + part * 16, 16), 16)
                placed = pl.ds(
                    pl.multiple_of(number * per_language + i * 64 + part * 16, 16), 16
                )
                queries[placed, :] = block[local, pl.ds(0, width)]
                taught = block[local, pl.ds(width, passages_all)].astype(jnp.float32)
                shifted = taught - jnp.max(taught, axis=1, keepdims=True)
                grown = jnp.exp(shifted)
                total = jnp.sum(grown, axis=1, keepdims=True)
                cross = jnp.sum(grown * shifted, axis=1, keepdims=True)
                taught_out[placed, :] = (grown * (student_scale / total)).astype(jnp.bfloat16)
                kl[placed, :] = jnp.broadcast_to(cross / total - jnp.log(total), (16, 128))
            return carry

        lax.fori_loop(0, 4, rows_of, 0)
        for copy in saved(number):
            copy.start()
    for number in range(3):
        for copy in saved(number):
            copy.wait()


def teacher_rows(blocks):
    rows = 3 * per_language
    return call(
        teacher_kernel,
        "teacher_rows",
        [vmem] * 3,
        [
            (hbm, (store_rows, passages_all), jnp.bfloat16),
            (vmem, (rows, width), jnp.bfloat16),
            (vmem, (rows, 128), jnp.float32),
        ],
        [pltpu.VMEM((rows, passages_all), jnp.bfloat16), pltpu.SemaphoreType.DMA((6,))],
        40,
        mib,
        2 * mib,
    )(*blocks)


def student_pass(base, quarter, scores, taught_ref, weights, kl):
    for i in range(4):
        local = pl.ds(pl.multiple_of(quarter * 64 + i * 16, 16), 16)
        placed = pl.ds(pl.multiple_of(base + quarter * 64 + i * 16, 16), 16)
        own = scores[local, :]
        taught = taught_ref[placed, :].astype(jnp.float32)
        shifted = own - jnp.max(own, axis=1, keepdims=True)
        grown = jnp.exp(shifted)
        total = jnp.sum(grown, axis=1, keepdims=True)
        cross = jnp.sum(taught * shifted, axis=1, keepdims=True)
        diverge = jnp.log(total) - cross * (1.0 / student_scale)
        weights[placed, :] = (grown * (student_scale / total) - taught).astype(jnp.bfloat16)
        kl[placed, :] = jnp.broadcast_to(diverge, (16, 128))


def first_kernel(
    chunk_list, target_of, raw, store,
    weights, passages, kl, raw_v, queries, taught, scores, other_scores, raw_sem, in_sem,
):
    def raw_copy(k):
        rows = pl.ds(pl.multiple_of(chunk_list[chunk_count + k], chunk_rows), chunk_rows)
        return pltpu.make_async_copy(raw.at[chunk_list[k], rows], raw_v.at[k], raw_sem.at[k])

    def start_raw(k, carry):
        raw_copy(k).start()
        return carry

    lax.fori_loop(0, chunk_count, start_raw, 0, unroll=4)
    copies = [
        pltpu.make_async_copy(
            store.at[pl.ds(3 * per_language, 3 * per_language), pl.ds(0, width)],
            queries,
            in_sem.at[0],
        ),
        pltpu.make_async_copy(store.at[pl.ds(0, 3 * per_language)], taught, in_sem.at[1]),
    ]
    for copy in copies:
        copy.start()
    passages[pl.ds(0, 16), :] = jnp.zeros((16, width), jnp.bfloat16)

    def place(g, carry):
        for c in range(group_chunks):
            raw_copy(g * group_chunks + c).wait()
        start = pl.multiple_of((chunk_list[2 * chunk_count + g * group_chunks] // 16) * 16, 16)
        target = lax.broadcasted_iota(jnp.int32, (window, group_rows), 0)
        hit = target == target_of[pl.ds(g, 1), :] - start
        chosen = hit.astype(jnp.float32).astype(jnp.bfloat16)
        chunks = raw_v[pl.ds(g * group_chunks, group_chunks)].reshape(group_rows, width)
        moved = jnp.dot(chosen, chunks, preferred_element_type=jnp.float32).astype(jnp.bfloat16)
        head = passages[pl.ds(start, 16), :]
        passages[pl.ds(start, 16), :] = head + moved[:16]
        passages[pl.ds(start + 16, window - 16), :] = moved[16:]
        return carry

    lax.fori_loop(0, chunk_count // group_chunks, place, 0)
    for copy in copies:
        copy.wait()

    def score_only(quarter, carry):
        score_quarter(queries, 0, quarter, passages, scores)
        return carry

    lax.fori_loop(0, 4, score_only, 0)
    held, free = scores, other_scores
    for number in range(3):
        base = number * per_language

        def together(quarter, carry, base=base, held=held, free=free, last=number == 2):
            if not last:
                score_quarter(queries, base + per_language, quarter, passages, free)
            student_pass(base, quarter, held, taught, weights, kl)
            return carry

        lax.fori_loop(0, 4, together, 0)
        held, free = free, held


def first_blocks(chunk_list, raw, store):
    rows = 3 * per_language
    scores = pltpu.VMEM((per_language, passages_all), jnp.float32)
    return call(
        first_kernel,
        "first_blocks",
        [smem, vmem, hbm, hbm],
        [
            (vmem, (rows, passages_all), jnp.bfloat16),
            (vmem, (passages_all + window, width), jnp.bfloat16),
            (vmem, (rows, 128), jnp.float32),
        ],
        [
            pltpu.VMEM((chunk_count, chunk_rows, width), jnp.bfloat16),
            pltpu.VMEM((rows, width), jnp.bfloat16),
            pltpu.VMEM((rows, passages_all), jnp.bfloat16),
            scores,
            scores,
            pltpu.SemaphoreType.DMA((chunk_count,)),
            pltpu.SemaphoreType.DMA((2,)),
        ],
        40,
        6 * 1024**3,
        2 * mib,
    )(*chunk_list, raw, store)


def chunks_of(counts):
    number = (counts + chunk_rows - 1) // chunk_rows
    upto = jnp.arange(holders)[None, :] < jnp.arange(holders)[:, None]
    offsets = jnp.sum(jnp.where(upto, counts[None, :], 0), axis=1)
    firsts = jnp.sum(jnp.where(upto, number[None, :], 0), axis=1)
    index = jnp.arange(chunk_count)[:, None]
    mine = (index >= firsts[None, :]) & (index < (firsts + number)[None, :])
    row = (index - firsts[None, :]) * chunk_rows

    def pick(values):
        return jnp.sum(jnp.where(mine, values, 0), axis=1)

    holder = pick(jnp.arange(holders)[None, :] + 0 * row)
    used = pick(jnp.minimum(counts[None, :] - row, chunk_rows))
    place = jnp.where(used > 0, pick(offsets[None, :] + row), passages_all)
    slots = jnp.arange(chunk_rows)[None, :]
    targets = jnp.where(slots < used[:, None], place[:, None] + slots, -1)
    return (
        jnp.concatenate([holder, pick(row), place]).astype(jnp.int32),
        targets.astype(jnp.int32).reshape(chunk_count // group_chunks, group_rows),
    )


def last_kernel(
    core, passages, before, queries, block, weights, send, keep, kl,
    own, teacher, scores, total, in_sem,
):
    own_copy = pltpu.make_async_copy(block.at[:, pl.ds(0, width)], own, in_sem.at[0])
    teacher_copy = pltpu.make_async_copy(
        block.at[:, pl.ds(width, passages_all)], teacher, in_sem.at[1]
    )
    own_copy.start()
    teacher_copy.start()
    own_copy.wait()

    def score_only(quarter, carry):
        score_quarter(own, 0, quarter, passages, scores)
        return carry

    lax.fori_loop(0, 4, score_only, 0)
    teacher_copy.wait()
    contract = (((0,), (0,)), ((), ()))

    def together(quarter, carry):
        row_pass(quarter, scores, teacher, weights, kl)
        columns = pl.ds(pl.multiple_of(quarter * 512, 512), 512)
        total[columns, :] = lax.dot_general(
            before[:, columns],
            queries[...],
            contract,
            preferred_element_type=jnp.float32,
        )
        return carry

    lax.fori_loop(0, 4, together, 0)
    even = core[0] == 0

    def reduce(j, carry):
        columns = pl.ds(pl.multiple_of(j * 256, 256), 256)
        grad = lax.dot_general(
            weights[:, columns],
            own[...],
            contract,
            preferred_element_type=jnp.float32,
        )
        grad = (grad + total[columns, :]).astype(jnp.bfloat16)
        for part in range(2):
            upper = grad[part * 128 : part * 128 + 64]
            lower = grad[part * 128 + 64 : part * 128 + 128]
            rows = pl.ds(pl.multiple_of(j * 128 + part * 64, 64), 64)
            keep[rows, :] = jnp.where(even, upper, lower)
            send[rows, :] = jnp.where(even, lower, upper)
        return carry

    lax.fori_loop(0, passages_all // 256, reduce, 0)


def last_block(core, passages, weights, queries, block):
    half = (vmem, (passages_all // 2, width), jnp.bfloat16)
    return call(
        last_kernel,
        "last_block",
        [smem] + [vmem] * 3 + [hbm],
        [
            (vmem, (per_language, passages_all), jnp.bfloat16),
            half,
            half,
            (vmem, (per_language, 128), jnp.float32),
        ],
        [
            pltpu.VMEM((per_language, width), jnp.bfloat16),
            pltpu.VMEM((per_language, passages_all), jnp.bfloat16),
            pltpu.VMEM((per_language, passages_all), jnp.float32),
            pltpu.VMEM((passages_all, width), jnp.float32),
            pltpu.SemaphoreType.DMA((2,)),
        ],
        20,
        6 * 1024**3,
        mib,
    )(core, passages, weights, queries, block)


def query_kernel(places, *refs):
    passages, outs = refs[0], refs[-len(places) :]
    rest = list(refs[1 : -len(places)])
    first = [rest.pop(0) for _ in range(3)]
    last = rest if rest else None
    for place, out in zip(places, outs):
        if place is None:
            rows = pl.ds(0, per_language)
            block, value = last[0], last[1][...]
        else:
            rows = pl.ds(place * per_language, per_language)
            block, value = first[0], first[1][rows, :] + first[2][rows, :]

        def step(half, carry, rows=rows, block=block, out=out):
            columns = pl.ds(pl.multiple_of(half * 512, 512), 512)
            out[:, columns] = jnp.dot(
                block[rows, :],
                passages[pl.ds(0, passages_all), columns],
                preferred_element_type=jnp.float32,
            ).astype(jnp.bfloat16)
            return carry

        lax.fori_loop(0, 2, step, 0)
        out[:, pl.ds(width, extra)] = kl_parts(value)


def query_grads(places, passages, first, last=(), flops=1024**3):
    return call(
        functools.partial(query_kernel, places),
        "query_grads",
        [vmem] * (1 + len(first) + len(last)),
        [(vmem, (per_language, width + extra), jnp.bfloat16)] * len(places),
        [],
        8,
        len(places) * flops,
    )(passages, *first, *last)


def pair_kernel(keep, other, out, paired, sems):
    chunk = 256

    def written(i):
        rows = pl.ds(pl.multiple_of(i * chunk, chunk), chunk)
        return pltpu.make_async_copy(paired.at[rows], out.at[rows], sems.at[i])

    def step(i, carry):
        for j in range(4):
            rows = pl.ds(pl.multiple_of(i * chunk + j * 64, 64), 64)
            paired[rows, :] = (
                keep[rows, :].astype(jnp.float32) + other[rows, :].astype(jnp.float32)
            ).astype(jnp.bfloat16)
        written(i).start()
        return carry

    lax.fori_loop(0, 4, step, 0)
    for i in range(4):
        written(i).wait()


def pair_sum(keep, other):
    return call(
        pair_kernel,
        "pair_sum",
        [vmem] * 2,
        [(hbm, keep.shape, jnp.bfloat16)],
        [pltpu.VMEM(keep.shape, jnp.bfloat16), pltpu.SemaphoreType.DMA((4,))],
        8,
        mib,
    )(keep, other)[0]


def restore_kernel(slot, in0, in1, in2, in3, grads_out, kl, select, grads, out_sem):
    rows = lax.broadcasted_iota(jnp.int32, (per_device, per_device), 0)
    select[...] = (rows == slot[0:1, :]).astype(jnp.float32).astype(jnp.bfloat16)
    contract = (((0,), (0,)), ((), ()))

    def joined(columns):
        part = None
        for number, block in enumerate((in0, in1, in2, in3)):
            chosen = select[number * per_language : (number + 1) * per_language, :]
            term = lax.dot_general(
                chosen, block[:, columns], contract, preferred_element_type=jnp.float32
            )
            part = term if part is None else part + term
        return part

    def written(j):
        columns = pl.ds(pl.multiple_of(j * 256, 256), 256)
        return pltpu.make_async_copy(grads.at[j], grads_out.at[:, columns], out_sem.at[j])

    def step(j, carry):
        columns = pl.ds(pl.multiple_of(j * 256, 256), 256)
        grads[j] = joined(columns).astype(jnp.bfloat16)
        written(j).start()
        return carry

    lax.fori_loop(0, width // 256, step, 0)
    column = jnp.sum(joined(pl.ds(width, extra)), axis=1, keepdims=True)
    kl[...] = jnp.transpose(jnp.broadcast_to(column, (per_device, 128)))[:1]
    for j in range(width // 256):
        written(j).wait()


def restore(slot, blocks):
    return call(
        restore_kernel,
        "restore",
        [vmem] * 5,
        [
            (hbm, (per_device, width), jnp.bfloat16),
            (vmem, (1, per_device), jnp.float32),
        ],
        [
            pltpu.VMEM((per_device, per_device), jnp.bfloat16),
            pltpu.VMEM((width // 256, per_device, 256), jnp.bfloat16),
            pltpu.SemaphoreType.DMA((width // 256,)),
        ],
        24,
        2 * 1024**3,
    )(slot, *blocks)


def sum_kernel(pieces, out, held, sems):
    copies = [
        pltpu.make_async_copy(pieces.at[pl.ds(4 * i, 4)], held.at[pl.ds(4 * i, 4)], sems.at[i])
        for i in range(4)
    ]
    for copy in copies:
        copy.start()
    total = jnp.zeros((64, width), jnp.float32)
    for i, copy in enumerate(copies):
        copy.wait()
        for j in range(4):
            total = total + held[4 * i + j].astype(jnp.float32)
    out[...] = total.astype(jnp.bfloat16)


def sum_pieces(pieces):
    return call(
        sum_kernel,
        "sum_pieces",
        [hbm],
        [(vmem, (64, width), jnp.bfloat16)],
        [pltpu.VMEM(pieces.shape, jnp.bfloat16), pltpu.SemaphoreType.DMA((4,))],
        8,
        mib,
    )(pieces)[0]


def shift(array, by):
    pairs = [(i, (i + by) % languages) for i in range(languages)]
    return lax.ppermute(array, "x", pairs)


def on_device(queries, bucket_ids, raw_passages, counts, teacher):
    group = ("y", "z", "c")
    here = lax.axis_index("x").astype(jnp.int32).reshape(1)
    core = lax.axis_index("c").astype(jnp.int32).reshape(1)
    all_raw = lax.all_gather(raw_passages[0], group, axis=0, tiled=True)
    ids = bucket_ids[0]
    out1, out3, slot = sort_rows(here, ids, None, queries[0, 0], teacher[0, 0])
    in1, in3 = shift(out1, 1), shift(out3, 3)
    out2, in0, _ = sort_rows(here, ids, slot, queries[0, 0], teacher[0, 0])
    held_counts, in0, out2 = lax.optimization_barrier((counts, in0, out2))
    holder_counts = lax.all_gather(held_counts[0], group, axis=0, tiled=True)
    chunk_list = chunks_of(holder_counts)
    out2, in1, in3, chunk_list = lax.optimization_barrier((out2, in1, in3, chunk_list))
    in2 = shift(out2, 2)
    store, moved, entropy = teacher_rows((in0, in1, in3))
    all_raw, store, moved, entropy = lax.optimization_barrier((all_raw, store, moved, entropy))
    weights, passages, kl = first_blocks(chunk_list, all_raw, store)
    last_weights, send, keep, last_kl = last_block(core, passages, weights, moved, in2)
    other = lax.ppermute(send, "c", [(0, 1), (1, 0)])
    first = (weights, kl, entropy)
    back1, back3 = query_grads((1, 2), passages, first)
    home1, home3 = shift(back1, -1), shift(back3, -3)
    paired = pair_sum(keep, other)
    spread = lax.all_to_all(
        paired.reshape(16, 64, width), ("y", "z"), split_axis=0, concat_axis=0, tiled=True
    )
    paired, last_weights, home1, home3 = lax.optimization_barrier(
        (paired, last_weights, home1, home3)
    )
    back2, back0 = query_grads(
        (None, 0), passages, first, (last_weights, last_kl), 4 * 1024**3
    )
    home2 = shift(back2, -2)
    grad_passages = sum_pieces(spread)
    grad_queries, kl_rows = restore(slot, (back0, home1, home2, home3))
    return (grad_queries[None, None], grad_passages[None], kl_rows[None])


def solution(mesh):
    split = Mesh(mesh.devices.reshape(4, 4, 4, 2), ("x", "y", "z", "c"))
    group = ("y", "z", "c")
    in_specs = (
        P("x", group, None, None),
        P("x", group, None),
        P("x", group, None, None),
        P("x", group),
        P("x", group, None, None),
    )
    out_specs = (P("x", group, None, None), P("x", group, None), P("x", group, None))
    return jax.shard_map(
        on_device, mesh=split, in_specs=in_specs, out_specs=out_specs, check_vma=False
    )
```

```python
import functools

import jax
import jax.numpy as jnp
from jax import lax
from jax.experimental import pallas as pl
from jax.experimental.pallas import tpu as pltpu
from jax.sharding import Mesh
from jax.sharding import PartitionSpec as P

student_scale = 0.1
languages = 4
holders = 32
capacity = 192
width = 1024
per_device = 1024
per_language = 256
passages_all = 2048
both = width + passages_all
group_chunks = 4
group_rows = 256
window = 272
extra = 128
chunk_rows = 64
chunk_count = 64
store_rows = 6144
mib = 1024 * 1024


def slots_of(ids, here):
    turned = lax.rem(ids - here + languages, languages)
    hot = turned == lax.broadcasted_iota(jnp.int32, (8, per_device), 0)
    earlier = lax.broadcasted_iota(jnp.int32, (per_device, per_device), 0)
    later = lax.broadcasted_iota(jnp.int32, (per_device, per_device), 1)
    upper = (earlier <= later).astype(jnp.float32).astype(jnp.bfloat16)
    hot = hot.astype(jnp.float32)
    ranks = jnp.dot(hot.astype(jnp.bfloat16), upper, preferred_element_type=jnp.float32)
    first = lax.broadcasted_iota(jnp.int32, (8, per_device), 0).astype(jnp.float32) * per_language
    return jnp.sum(hot * (ranks - 1.0 + first), axis=0, keepdims=True).astype(jnp.int32)


vmem = pl.BlockSpec(memory_space=pltpu.VMEM)
smem = pl.BlockSpec(memory_space=pltpu.SMEM)
hbm = pl.BlockSpec(memory_space=pltpu.HBM)


def call(kernel, name, in_specs, outs, scratch, limit, flops, transcendentals=0):
    return pl.pallas_call(
        kernel,
        in_specs=in_specs,
        out_specs=[spec for spec, _, _ in outs],
        out_shape=[jax.ShapeDtypeStruct(shape, dtype) for _, shape, dtype in outs],
        scratch_shapes=scratch,
        compiler_params=pltpu.CompilerParams(vmem_limit_bytes=limit * mib),
        cost_estimate=pl.CostEstimate(
            flops=flops, bytes_accessed=8 * mib, transcendentals=transcendentals
        ),
        name=name,
    )


def sort_kernel(
    first, here, ids, slot_in, queries, teacher, out_a, out_b, slot,
    select, block, moved_a, moved_b, in_sem, out_sem,
):
    tile = 512
    tiles = both // tile

    def read(j):
        source = queries if j < width // tile else teacher
        column = j * tile if j < width // tile else j * tile - width
        return pltpu.make_async_copy(
            source.at[:, pl.ds(column, tile)], block.at[j], in_sem.at[j]
        )

    def written(j):
        columns = pl.ds(j * tile, tile)
        return [
            pltpu.make_async_copy(moved_a.at[j], out_a.at[:, columns], out_sem.at[2 * j]),
            pltpu.make_async_copy(moved_b.at[j], out_b.at[:, columns], out_sem.at[2 * j + 1]),
        ]

    for j in range(tiles):
        read(j).start()
    if first:
        slots = slots_of(ids[...], here[0])
        slot[...] = jnp.broadcast_to(slots, (8, per_device))
    else:
        slots = slot_in[0:1, :]
        slot[...] = jnp.zeros((8, 128), jnp.int32)
    rows = lax.broadcasted_iota(jnp.int32, (per_language, per_device), 0)
    for half, number in enumerate((1, 3) if first else (2, 0)):
        hit = rows + number * per_language == slots
        select[pl.ds(half * per_language, per_language), :] = hit.astype(jnp.float32).astype(
            jnp.bfloat16
        )
    for j in range(tiles):
        read(j).wait()
        moved = jnp.dot(select[...], block[j], preferred_element_type=jnp.float32)
        moved_a[j] = moved[:per_language].astype(jnp.bfloat16)
        moved_b[j] = moved[per_language:].astype(jnp.bfloat16)
        for copy in written(j):
            copy.start()
    for j in range(tiles):
        for copy in written(j):
            copy.wait()


def sort_rows(here, ids, slot, queries, teacher):
    first = slot is None
    tiles = both // 512
    moved = pltpu.VMEM((tiles, per_language, 512), jnp.bfloat16)
    out = (hbm, (per_language, both), jnp.bfloat16)
    return call(
        functools.partial(sort_kernel, first),
        "sort_first" if first else "sort_rest",
        [smem, vmem, vmem, hbm, hbm],
        [out, out, (vmem, (8, per_device) if first else (8, 128), jnp.int32)],
        [
            pltpu.VMEM((2 * per_language, per_device), jnp.bfloat16),
            pltpu.VMEM((tiles, per_device, 512), jnp.bfloat16),
            moved,
            moved,
            pltpu.SemaphoreType.DMA((tiles,)),
            pltpu.SemaphoreType.DMA((2 * tiles,)),
        ],
        60 if first else 28,
        4 * per_language * per_device * both,
    )(here, ids, ids if first else slot, queries, teacher)


def kl_parts(value):
    high = value.astype(jnp.bfloat16).astype(jnp.float32)
    middle = (value - high).astype(jnp.bfloat16).astype(jnp.float32)
    low = value - high - middle
    lane = lax.broadcasted_iota(jnp.int32, value.shape, 1)
    parts = jnp.where(
        lane == 0, high, jnp.where(lane == 1, middle, jnp.where(lane == 2, low, 0.0))
    )
    return parts.astype(jnp.bfloat16)


def row_pass(quarter, scores, block, weights, kl):
    for i in range(4):
        local = pl.ds(pl.multiple_of(quarter * 64 + i * 16, 16), 16)
        own = scores[local, :]
        taught = block[local, :].astype(jnp.float32)
        top = jnp.max(own, axis=1, keepdims=True)
        taught_top = jnp.max(taught, axis=1, keepdims=True)
        grown = jnp.exp(own - top)
        total = jnp.sum(grown, axis=1, keepdims=True)
        shifted = taught - taught_top
        taught_grown = jnp.exp(shifted)
        taught_total = jnp.sum(taught_grown, axis=1, keepdims=True)
        cross = jnp.sum(taught_grown * (shifted - (own - top)), axis=1, keepdims=True)
        diverge = cross / taught_total - jnp.log(taught_total) + jnp.log(total)
        weights[local, :] = (
            grown * (student_scale / total) - taught_grown * (student_scale / taught_total)
        ).astype(jnp.bfloat16)
        kl[local, :] = jnp.broadcast_to(diverge, (16, 128))


def score_quarter(queries, base, quarter, passages, scores):
    columns = pl.ds(pl.multiple_of(quarter * 512, 512), 512)
    scores[:, columns] = (
        lax.dot_general(
            queries[pl.ds(base, per_language), :],
            passages[columns, :],
            (((1,), (1,)), ((), ())),
            preferred_element_type=jnp.float32,
        )
        * student_scale
    )


def teacher_kernel(in0, in1, in2, store, queries, kl, taught_out, sems):
    rows = 3 * per_language

    def saved(number):
        block = pl.ds(number * per_language, per_language)
        behind = pl.ds(rows + number * per_language, per_language)
        return [
            pltpu.make_async_copy(taught_out.at[block], store.at[block], sems.at[2 * number]),
            pltpu.make_async_copy(
                queries.at[block], store.at[behind, pl.ds(0, width)], sems.at[2 * number + 1]
            ),
        ]

    for number, block in enumerate((in0, in1, in2)):

        def rows_of(i, carry, number=number, block=block):
            for part in range(4):
                local = pl.ds(pl.multiple_of(i * 64 + part * 16, 16), 16)
                placed = pl.ds(
                    pl.multiple_of(number * per_language + i * 64 + part * 16, 16), 16
                )
                queries[placed, :] = block[local, pl.ds(0, width)]
                taught = block[local, pl.ds(width, passages_all)].astype(jnp.float32)
                shifted = taught - jnp.max(taught, axis=1, keepdims=True)
                grown = jnp.exp(shifted)
                total = jnp.sum(grown, axis=1, keepdims=True)
                cross = jnp.sum(grown * shifted, axis=1, keepdims=True)
                taught_out[placed, :] = (grown * (student_scale / total)).astype(jnp.bfloat16)
                kl[placed, :] = jnp.broadcast_to(cross / total - jnp.log(total), (16, 128))
            return carry

        lax.fori_loop(0, 4, rows_of, 0)
        for copy in saved(number):
            copy.start()
    for number in range(3):
        for copy in saved(number):
            copy.wait()


def teacher_rows(blocks):
    rows = 3 * per_language
    return call(
        teacher_kernel,
        "teacher_rows",
        [vmem] * 3,
        [
            (hbm, (store_rows, passages_all), jnp.bfloat16),
            (vmem, (rows, width), jnp.bfloat16),
            (vmem, (rows, 128), jnp.float32),
        ],
        [pltpu.VMEM((rows, passages_all), jnp.bfloat16), pltpu.SemaphoreType.DMA((6,))],
        40,
        mib,
        2 * mib,
    )(*blocks)


def student_pass(base, quarter, scores, taught_ref, weights, kl):
    for i in range(4):
        local = pl.ds(pl.multiple_of(quarter * 64 + i * 16, 16), 16)
        placed = pl.ds(pl.multiple_of(base + quarter * 64 + i * 16, 16), 16)
        own = scores[local, :]
        taught = taught_ref[placed, :].astype(jnp.float32)
        shifted = own - jnp.max(own, axis=1, keepdims=True)
        grown = jnp.exp(shifted)
        total = jnp.sum(grown, axis=1, keepdims=True)
        cross = jnp.sum(taught * shifted, axis=1, keepdims=True)
        diverge = jnp.log(total) - cross * (1.0 / student_scale)
        weights[placed, :] = (grown * (student_scale / total) - taught).astype(jnp.bfloat16)
        kl[placed, :] = jnp.broadcast_to(diverge, (16, 128))


def first_kernel(
    chunk_list, target_of, raw, store,
    weights, passages, kl, raw_v, queries, taught, scores, other_scores, raw_sem, in_sem,
):
    def raw_copy(k):
        rows = pl.ds(pl.multiple_of(chunk_list[chunk_count + k], chunk_rows), chunk_rows)
        return pltpu.make_async_copy(raw.at[chunk_list[k], rows], raw_v.at[k], raw_sem.at[k])

    def start_raw(k, carry):
        raw_copy(k).start()
        return carry

    lax.fori_loop(0, chunk_count, start_raw, 0, unroll=4)
    copies = [
        pltpu.make_async_copy(
            store.at[pl.ds(3 * per_language, 3 * per_language), pl.ds(0, width)],
            queries,
            in_sem.at[0],
        ),
        pltpu.make_async_copy(store.at[pl.ds(0, 3 * per_language)], taught, in_sem.at[1]),
    ]
    for copy in copies:
        copy.start()
    passages[pl.ds(0, 16), :] = jnp.zeros((16, width), jnp.bfloat16)

    def place(g, carry):
        for c in range(group_chunks):
            raw_copy(g * group_chunks + c).wait()
        start = pl.multiple_of((chunk_list[2 * chunk_count + g * group_chunks] // 16) * 16, 16)
        target = lax.broadcasted_iota(jnp.int32, (window, group_rows), 0)
        hit = target == target_of[pl.ds(g, 1), :] - start
        chosen = hit.astype(jnp.float32).astype(jnp.bfloat16)
        chunks = raw_v[pl.ds(g * group_chunks, group_chunks)].reshape(group_rows, width)
        moved = jnp.dot(chosen, chunks, preferred_element_type=jnp.float32).astype(jnp.bfloat16)
        head = passages[pl.ds(start, 16), :]
        passages[pl.ds(start, 16), :] = head + moved[:16]
        passages[pl.ds(start + 16, window - 16), :] = moved[16:]
        return carry

    lax.fori_loop(0, chunk_count // group_chunks, place, 0)
    for copy in copies:
        copy.wait()

    def score_only(quarter, carry):
        score_quarter(queries, 0, quarter, passages, scores)
        return carry

    lax.fori_loop(0, 4, score_only, 0)
    held, free = scores, other_scores
    for number in range(3):
        base = number * per_language

        def together(quarter, carry, base=base, held=held, free=free, last=number == 2):
            if not last:
                score_quarter(queries, base + per_language, quarter, passages, free)
            student_pass(base, quarter, held, taught, weights, kl)
            return carry

        lax.fori_loop(0, 4, together, 0)
        held, free = free, held


def first_blocks(chunk_list, raw, store):
    rows = 3 * per_language
    scores = pltpu.VMEM((per_language, passages_all), jnp.float32)
    return call(
        first_kernel,
        "first_blocks",
        [smem, vmem, hbm, hbm],
        [
            (vmem, (rows, passages_all), jnp.bfloat16),
            (vmem, (passages_all + window, width), jnp.bfloat16),
            (vmem, (rows, 128), jnp.float32),
        ],
        [
            pltpu.VMEM((chunk_count, chunk_rows, width), jnp.bfloat16),
            pltpu.VMEM((rows, width), jnp.bfloat16),
            pltpu.VMEM((rows, passages_all), jnp.bfloat16),
            scores,
            scores,
            pltpu.SemaphoreType.DMA((chunk_count,)),
            pltpu.SemaphoreType.DMA((2,)),
        ],
        40,
        6 * 1024**3,
        2 * mib,
    )(*chunk_list, raw, store)


def chunks_of(counts):
    number = (counts + chunk_rows - 1) // chunk_rows
    upto = jnp.arange(holders)[None, :] < jnp.arange(holders)[:, None]
    offsets = jnp.sum(jnp.where(upto, counts[None, :], 0), axis=1)
    firsts = jnp.sum(jnp.where(upto, number[None, :], 0), axis=1)
    index = jnp.arange(chunk_count)[:, None]
    mine = (index >= firsts[None, :]) & (index < (firsts + number)[None, :])
    row = (index - firsts[None, :]) * chunk_rows

    def pick(values):
        return jnp.sum(jnp.where(mine, values, 0), axis=1)

    holder = pick(jnp.arange(holders)[None, :] + 0 * row)
    used = pick(jnp.minimum(counts[None, :] - row, chunk_rows))
    place = jnp.where(used > 0, pick(offsets[None, :] + row), passages_all)
    slots = jnp.arange(chunk_rows)[None, :]
    targets = jnp.where(slots < used[:, None], place[:, None] + slots, -1)
    return (
        jnp.concatenate([holder, pick(row), place]).astype(jnp.int32),
        targets.astype(jnp.int32).reshape(chunk_count // group_chunks, group_rows),
    )


def last_kernel(
    core, passages, before, queries, block, weights, send, keep, kl,
    own, teacher, scores, total, in_sem,
):
    own_copy = pltpu.make_async_copy(block.at[:, pl.ds(0, width)], own, in_sem.at[0])
    teacher_copy = pltpu.make_async_copy(
        block.at[:, pl.ds(width, passages_all)], teacher, in_sem.at[1]
    )
    own_copy.start()
    teacher_copy.start()
    own_copy.wait()

    def score_only(quarter, carry):
        score_quarter(own, 0, quarter, passages, scores)
        return carry

    lax.fori_loop(0, 4, score_only, 0)
    teacher_copy.wait()
    contract = (((0,), (0,)), ((), ()))

    def together(quarter, carry):
        row_pass(quarter, scores, teacher, weights, kl)
        columns = pl.ds(pl.multiple_of(quarter * 512, 512), 512)
        total[columns, :] = lax.dot_general(
            before[:, columns],
            queries[...],
            contract,
            preferred_element_type=jnp.float32,
        )
        return carry

    lax.fori_loop(0, 4, together, 0)
    even = core[0] == 0

    def reduce(j, carry):
        columns = pl.ds(pl.multiple_of(j * 256, 256), 256)
        grad = lax.dot_general(
            weights[:, columns],
            own[...],
            contract,
            preferred_element_type=jnp.float32,
        )
        grad = (grad + total[columns, :]).astype(jnp.bfloat16)
        for part in range(2):
            upper = grad[part * 128 : part * 128 + 64]
            lower = grad[part * 128 + 64 : part * 128 + 128]
            rows = pl.ds(pl.multiple_of(j * 128 + part * 64, 64), 64)
            keep[rows, :] = jnp.where(even, upper, lower)
            send[rows, :] = jnp.where(even, lower, upper)
        return carry

    lax.fori_loop(0, passages_all // 256, reduce, 0)


def last_block(core, passages, weights, queries, block):
    half = (vmem, (passages_all // 2, width), jnp.bfloat16)
    return call(
        last_kernel,
        "last_block",
        [smem] + [vmem] * 3 + [hbm],
        [
            (vmem, (per_language, passages_all), jnp.bfloat16),
            half,
            half,
            (vmem, (per_language, 128), jnp.float32),
        ],
        [
            pltpu.VMEM((per_language, width), jnp.bfloat16),
            pltpu.VMEM((per_language, passages_all), jnp.bfloat16),
            pltpu.VMEM((per_language, passages_all), jnp.float32),
            pltpu.VMEM((passages_all, width), jnp.float32),
            pltpu.SemaphoreType.DMA((2,)),
        ],
        20,
        6 * 1024**3,
        mib,
    )(core, passages, weights, queries, block)


def query_kernel(places, *refs):
    passages, outs = refs[0], refs[-len(places) :]
    rest = list(refs[1 : -len(places)])
    first = [rest.pop(0) for _ in range(3)]
    last = rest if rest else None
    for place, out in zip(places, outs):
        if place is None:
            rows = pl.ds(0, per_language)
            block, value = last[0], last[1][...]
        else:
            rows = pl.ds(place * per_language, per_language)
            block, value = first[0], first[1][rows, :] + first[2][rows, :]

        def step(half, carry, rows=rows, block=block, out=out):
            columns = pl.ds(pl.multiple_of(half * 512, 512), 512)
            out[:, columns] = jnp.dot(
                block[rows, :],
                passages[pl.ds(0, passages_all), columns],
                preferred_element_type=jnp.float32,
            ).astype(jnp.bfloat16)
            return carry

        lax.fori_loop(0, 2, step, 0)
        out[:, pl.ds(width, extra)] = kl_parts(value)


def query_grads(places, passages, first, last=()):
    return call(
        functools.partial(query_kernel, places),
        "query_grads",
        [vmem] * (1 + len(first) + len(last)),
        [(vmem, (per_language, width + extra), jnp.bfloat16)] * len(places),
        [],
        8,
        len(places) * 1024**3,
    )(passages, *first, *last)


def pair_kernel(keep, other, out, paired, sems):
    chunk = 256

    def written(i):
        rows = pl.ds(pl.multiple_of(i * chunk, chunk), chunk)
        return pltpu.make_async_copy(paired.at[rows], out.at[rows], sems.at[i])

    def step(i, carry):
        for j in range(4):
            rows = pl.ds(pl.multiple_of(i * chunk + j * 64, 64), 64)
            paired[rows, :] = (
                keep[rows, :].astype(jnp.float32) + other[rows, :].astype(jnp.float32)
            ).astype(jnp.bfloat16)
        written(i).start()
        return carry

    lax.fori_loop(0, 4, step, 0)
    for i in range(4):
        written(i).wait()


def pair_sum(keep, other):
    return call(
        pair_kernel,
        "pair_sum",
        [vmem] * 2,
        [(hbm, keep.shape, jnp.bfloat16)],
        [pltpu.VMEM(keep.shape, jnp.bfloat16), pltpu.SemaphoreType.DMA((4,))],
        8,
        mib,
    )(keep, other)[0]


def restore_kernel(slot, in0, in1, in2, in3, grads_out, kl, select, grads, out_sem):
    rows = lax.broadcasted_iota(jnp.int32, (per_device, per_device), 0)
    select[...] = (rows == slot[0:1, :]).astype(jnp.float32).astype(jnp.bfloat16)
    contract = (((0,), (0,)), ((), ()))

    def joined(columns):
        part = None
        for number, block in enumerate((in0, in1, in2, in3)):
            chosen = select[number * per_language : (number + 1) * per_language, :]
            term = lax.dot_general(
                chosen, block[:, columns], contract, preferred_element_type=jnp.float32
            )
            part = term if part is None else part + term
        return part

    def written(j):
        columns = pl.ds(pl.multiple_of(j * 256, 256), 256)
        return pltpu.make_async_copy(grads.at[j], grads_out.at[:, columns], out_sem.at[j])

    def step(j, carry):
        columns = pl.ds(pl.multiple_of(j * 256, 256), 256)
        grads[j] = joined(columns).astype(jnp.bfloat16)
        written(j).start()
        return carry

    lax.fori_loop(0, width // 256, step, 0)
    column = jnp.sum(joined(pl.ds(width, extra)), axis=1, keepdims=True)
    kl[...] = jnp.transpose(jnp.broadcast_to(column, (per_device, 128)))[:1]
    for j in range(width // 256):
        written(j).wait()


def restore(slot, blocks):
    return call(
        restore_kernel,
        "restore",
        [vmem] * 5,
        [
            (hbm, (per_device, width), jnp.bfloat16),
            (vmem, (1, per_device), jnp.float32),
        ],
        [
            pltpu.VMEM((per_device, per_device), jnp.bfloat16),
            pltpu.VMEM((width // 256, per_device, 256), jnp.bfloat16),
            pltpu.SemaphoreType.DMA((width // 256,)),
        ],
        24,
        28 * 1024**3,
    )(slot, *blocks)


def sum_kernel(pieces, out, held, sems):
    copies = [
        pltpu.make_async_copy(pieces.at[pl.ds(4 * i, 4)], held.at[pl.ds(4 * i, 4)], sems.at[i])
        for i in range(4)
    ]
    for copy in copies:
        copy.start()
    total = jnp.zeros((64, width), jnp.float32)
    for i, copy in enumerate(copies):
        copy.wait()
        for j in range(4):
            total = total + held[4 * i + j].astype(jnp.float32)
    out[...] = total.astype(jnp.bfloat16)


def sum_pieces(pieces):
    return call(
        sum_kernel,
        "sum_pieces",
        [hbm],
        [(vmem, (64, width), jnp.bfloat16)],
        [pltpu.VMEM(pieces.shape, jnp.bfloat16), pltpu.SemaphoreType.DMA((4,))],
        8,
        mib,
    )(pieces)[0]


def shift(array, by):
    pairs = [(i, (i + by) % languages) for i in range(languages)]
    return lax.ppermute(array, "x", pairs)


def on_device(queries, bucket_ids, raw_passages, counts, teacher):
    group = ("y", "z", "c")
    here = lax.axis_index("x").astype(jnp.int32).reshape(1)
    core = lax.axis_index("c").astype(jnp.int32).reshape(1)
    all_raw = lax.all_gather(raw_passages[0], group, axis=0, tiled=True)
    ids = bucket_ids[0]
    out1, out3, slot = sort_rows(here, ids, None, queries[0, 0], teacher[0, 0])
    in1, in3 = shift(out1, 1), shift(out3, 3)
    out2, in0, _ = sort_rows(here, ids, slot, queries[0, 0], teacher[0, 0])
    held_counts, in0, out2 = lax.optimization_barrier((counts, in0, out2))
    holder_counts = lax.all_gather(held_counts[0], group, axis=0, tiled=True)
    chunk_list = chunks_of(holder_counts)
    out2, in1, in3, chunk_list = lax.optimization_barrier((out2, in1, in3, chunk_list))
    in2 = shift(out2, 2)
    store, moved, entropy = teacher_rows((in0, in1, in3))
    all_raw, store, moved, entropy = lax.optimization_barrier((all_raw, store, moved, entropy))
    weights, passages, kl = first_blocks(chunk_list, all_raw, store)
    last_weights, send, keep, last_kl = last_block(core, passages, weights, moved, in2)
    other = lax.ppermute(send, "c", [(0, 1), (1, 0)])
    back1, back3, back2, back0 = query_grads(
        (1, 2, None, 0), passages, (weights, kl, entropy), (last_weights, last_kl)
    )
    home1, home3, home2 = shift(back1, -1), shift(back3, -3), shift(back2, -2)
    paired = pair_sum(keep, other)
    spread = lax.all_to_all(
        paired.reshape(16, 64, width), ("y", "z"), split_axis=0, concat_axis=0, tiled=True
    )
    grad_passages = sum_pieces(spread)
    grad_queries, kl_rows = restore(slot, (back0, home1, home2, home3))
    return (grad_queries[None, None], grad_passages[None], kl_rows[None])


def solution(mesh):
    split = Mesh(mesh.devices.reshape(4, 4, 4, 2), ("x", "y", "z", "c"))
    group = ("y", "z", "c")
    in_specs = (
        P("x", group, None, None),
        P("x", group, None),
        P("x", group, None, None),
        P("x", group),
        P("x", group, None, None),
    )
    out_specs = (P("x", group, None, None), P("x", group, None), P("x", group, None))
    return jax.shard_map(
        on_device, mesh=split, in_specs=in_specs, out_specs=out_specs, check_vma=False
    )
```

```python
import functools

import jax
import jax.numpy as jnp
from jax import lax
from jax.experimental import pallas as pl
from jax.experimental.pallas import tpu as pltpu
from jax.sharding import Mesh
from jax.sharding import PartitionSpec as P

student_scale = 0.1
languages = 4
holders = 32
capacity = 192
width = 1024
per_device = 1024
per_language = 256
passages_all = 2048
both = width + passages_all
group_chunks = 8
group_rows = 256
window = 272
extra = 128
chunk_rows = 32
chunk_count = 96
store_rows = 6144
mib = 1024 * 1024


def slots_of(ids, here):
    turned = lax.rem(ids - here + languages, languages)
    kinds = lax.broadcasted_iota(jnp.int32, (8, per_device), 0)
    hot = (turned == kinds).astype(jnp.float32)
    parts = per_device // 128
    stacked = jnp.concatenate([hot[:, i * 128 : (i + 1) * 128] for i in range(parts)], axis=0)
    earlier = lax.broadcasted_iota(jnp.int32, (128, 128), 0)
    later = lax.broadcasted_iota(jnp.int32, (128, 128), 1)
    upper = (earlier <= later).astype(jnp.float32).astype(jnp.bfloat16)
    sums = jnp.dot(stacked.astype(jnp.bfloat16), upper, preferred_element_type=jnp.float32)
    before = jnp.zeros((8, 1), jnp.float32)
    ranks = []
    for i in range(parts):
        segment = sums[i * 8 : (i + 1) * 8]
        ranks.append(segment + before)
        before = before + segment[:, 127:128]
    place = jnp.concatenate(ranks, axis=1) - 1.0 + kinds.astype(jnp.float32) * per_language
    return jnp.sum(hot * place, axis=0, keepdims=True).astype(jnp.int32)


vmem = pl.BlockSpec(memory_space=pltpu.VMEM)
smem = pl.BlockSpec(memory_space=pltpu.SMEM)
hbm = pl.BlockSpec(memory_space=pltpu.HBM)


def call(kernel, name, in_specs, outs, scratch, limit, flops, transcendentals=0):
    return pl.pallas_call(
        kernel,
        in_specs=in_specs,
        out_specs=[spec for spec, _, _ in outs],
        out_shape=[jax.ShapeDtypeStruct(shape, dtype) for _, shape, dtype in outs],
        scratch_shapes=scratch,
        compiler_params=pltpu.CompilerParams(vmem_limit_bytes=limit * mib),
        cost_estimate=pl.CostEstimate(
            flops=flops, bytes_accessed=8 * mib, transcendentals=transcendentals
        ),
        name=name,
    )


def sort_kernel(
    first, here, ids, slot_in, queries, teacher, out_a, out_b, slot,
    select, block, moved_a, moved_b, in_sem, out_sem,
):
    tile = 512
    tiles = both // tile

    def read(j):
        source = queries if j < width // tile else teacher
        column = j * tile if j < width // tile else j * tile - width
        return pltpu.make_async_copy(
            source.at[:, pl.ds(column, tile)], block.at[j], in_sem.at[j]
        )

    def written(j):
        columns = pl.ds(j * tile, tile)
        return [
            pltpu.make_async_copy(moved_a.at[j], out_a.at[:, columns], out_sem.at[2 * j]),
            pltpu.make_async_copy(moved_b.at[j], out_b.at[:, columns], out_sem.at[2 * j + 1]),
        ]

    for j in range(tiles):
        read(j).start()
    if first:
        slots = slots_of(ids[...], here[0])
        slot[...] = jnp.broadcast_to(slots, (8, per_device))
    else:
        slots = slot_in[0:1, :]
        slot[...] = jnp.zeros((8, 128), jnp.int32)
    rows = lax.broadcasted_iota(jnp.int32, (per_language, per_device), 0)
    for half, number in enumerate((1, 3) if first else (2, 0)):
        hit = rows + number * per_language == slots
        select[pl.ds(half * per_language, per_language), :] = hit.astype(jnp.float32).astype(
            jnp.bfloat16
        )
    for j in range(tiles):
        read(j).wait()
        moved = jnp.dot(select[...], block[j], preferred_element_type=jnp.float32)
        moved_a[j] = moved[:per_language].astype(jnp.bfloat16)
        moved_b[j] = moved[per_language:].astype(jnp.bfloat16)
        for copy in written(j):
            copy.start()
    for j in range(tiles):
        for copy in written(j):
            copy.wait()


def sort_rows(here, ids, slot, queries, teacher):
    first = slot is None
    tiles = both // 512
    moved = pltpu.VMEM((tiles, per_language, 512), jnp.bfloat16)
    out = (hbm, (per_language, both), jnp.bfloat16)
    return call(
        functools.partial(sort_kernel, first),
        "sort_first" if first else "sort_rest",
        [smem, vmem, vmem, hbm, hbm],
        [out, out, (vmem, (8, per_device) if first else (8, 128), jnp.int32)],
        [
            pltpu.VMEM((2 * per_language, per_device), jnp.bfloat16),
            pltpu.VMEM((tiles, per_device, 512), jnp.bfloat16),
            moved,
            moved,
            pltpu.SemaphoreType.DMA((tiles,)),
            pltpu.SemaphoreType.DMA((2 * tiles,)),
        ],
        60 if first else 28,
        4 * per_language * per_device * both,
    )(here, ids, ids if first else slot, queries, teacher)


def kl_parts(value):
    high = value.astype(jnp.bfloat16).astype(jnp.float32)
    middle = (value - high).astype(jnp.bfloat16).astype(jnp.float32)
    low = value - high - middle
    lane = lax.broadcasted_iota(jnp.int32, value.shape, 1)
    parts = jnp.where(
        lane == 0, high, jnp.where(lane == 1, middle, jnp.where(lane == 2, low, 0.0))
    )
    return parts.astype(jnp.bfloat16)


def row_pass(quarter, scores, block, weights, kl):
    for i in range(4):
        local = pl.ds(pl.multiple_of(quarter * 64 + i * 16, 16), 16)
        own = scores[local, :]
        taught = block[local, :].astype(jnp.float32)
        top = jnp.max(own, axis=1, keepdims=True)
        taught_top = jnp.max(taught, axis=1, keepdims=True)
        grown = jnp.exp(own - top)
        total = jnp.sum(grown, axis=1, keepdims=True)
        shifted = taught - taught_top
        taught_grown = jnp.exp(shifted)
        taught_total = jnp.sum(taught_grown, axis=1, keepdims=True)
        cross = jnp.sum(taught_grown * (shifted - (own - top)), axis=1, keepdims=True)
        diverge = cross / taught_total - jnp.log(taught_total) + jnp.log(total)
        weights[local, :] = (
            grown * (student_scale / total) - taught_grown * (student_scale / taught_total)
        ).astype(jnp.bfloat16)
        kl[local, :] = jnp.broadcast_to(diverge, (16, 128))


def score_quarter(queries, base, quarter, passages, scores):
    columns = pl.ds(pl.multiple_of(quarter * 512, 512), 512)
    scores[:, columns] = (
        lax.dot_general(
            queries[pl.ds(base, per_language), pl.ds(0, width)],
            passages[columns, :],
            (((1,), (1,)), ((), ())),
            preferred_element_type=jnp.float32,
        )
        * student_scale
    )


def teacher_kernel(in0, in1, in2, store, queries, taught_out, parts, sems):
    rows = 3 * per_language

    def saved(number):
        block = pl.ds(number * per_language, per_language)
        behind = pl.ds(rows + number * per_language, per_language)
        return [
            pltpu.make_async_copy(taught_out.at[block], store.at[block], sems.at[number]),
            pltpu.make_async_copy(
                queries.at[block], store.at[behind, pl.ds(0, width)], sems.at[3 + number]
            ),
            pltpu.make_async_copy(
                parts.at[block], store.at[behind, pl.ds(width, extra)], sems.at[6 + number]
            ),
        ]

    for number, block in enumerate((in0, in1, in2)):

        def rows_of(i, carry, number=number, block=block):
            for part in range(4):
                local = pl.ds(pl.multiple_of(i * 64 + part * 16, 16), 16)
                placed = pl.ds(
                    pl.multiple_of(number * per_language + i * 64 + part * 16, 16), 16
                )
                queries[placed, :] = block[local, pl.ds(0, width)]
                taught = block[local, pl.ds(width, passages_all)].astype(jnp.float32)
                shifted = taught - jnp.max(taught, axis=1, keepdims=True)
                grown = jnp.exp(shifted)
                total = jnp.sum(grown, axis=1, keepdims=True)
                cross = jnp.sum(grown * shifted, axis=1, keepdims=True)
                taught_out[placed, :] = (grown * (student_scale / total)).astype(jnp.bfloat16)
                entropy = jnp.broadcast_to(cross / total - jnp.log(total), (16, 128))
                parts[placed, :] = kl_parts(entropy)
            return carry

        lax.fori_loop(0, 4, rows_of, 0)
        for copy in saved(number):
            copy.start()
    for number in range(3):
        for copy in saved(number):
            copy.wait()


def teacher_rows(blocks):
    rows = 3 * per_language
    return call(
        teacher_kernel,
        "teacher_rows",
        [vmem] * 3,
        [
            (hbm, (store_rows, passages_all), jnp.bfloat16),
            (vmem, (rows, width), jnp.bfloat16),
        ],
        [
            pltpu.VMEM((rows, passages_all), jnp.bfloat16),
            pltpu.VMEM((rows, extra), jnp.bfloat16),
            pltpu.SemaphoreType.DMA((9,)),
        ],
        40,
        mib,
        2 * mib,
    )(*blocks)


def student_pass(base, quarter, scores, taught_ref, parts, weights, kl):
    for i in range(4):
        local = pl.ds(pl.multiple_of(quarter * 64 + i * 16, 16), 16)
        placed = pl.ds(pl.multiple_of(base + quarter * 64 + i * 16, 16), 16)
        own = scores[local, :]
        taught = taught_ref[placed, :].astype(jnp.float32)
        shifted = own - jnp.max(own, axis=1, keepdims=True)
        grown = jnp.exp(shifted)
        total = jnp.sum(grown, axis=1, keepdims=True)
        cross = jnp.sum(taught * shifted, axis=1, keepdims=True)
        entropy = jnp.sum(
            parts[placed, pl.ds(width, extra)].astype(jnp.float32), axis=1, keepdims=True
        )
        diverge = entropy + jnp.log(total) - cross * (1.0 / student_scale)
        weights[placed, :] = (grown * (student_scale / total) - taught).astype(jnp.bfloat16)
        kl[placed, :] = jnp.broadcast_to(diverge, (16, 128))


def grad_columns(rows, columns, weights, passages, out):
    out[:, columns] = jnp.dot(
        weights[rows, :],
        passages[pl.ds(0, passages_all), columns],
        preferred_element_type=jnp.float32,
    ).astype(jnp.bfloat16)


def first_kernel(
    chunk_list, target_of, raw, store,
    weights, passages, kl, grad, raw_v, queries, taught, scores, other_scores, raw_sem, in_sem,
):
    def raw_copy(k):
        rows = pl.ds(pl.multiple_of(chunk_list[chunk_count + k], chunk_rows), chunk_rows)
        return pltpu.make_async_copy(raw.at[chunk_list[k], rows], raw_v.at[k], raw_sem.at[k])

    groups = chunk_list[3 * chunk_count]

    def start_group(g, carry):
        for c in range(group_chunks):
            raw_copy(g * group_chunks + c).start()
        return carry

    lax.fori_loop(0, groups, start_group, 0)
    copies = [
        pltpu.make_async_copy(
            store.at[pl.ds(3 * per_language, 3 * per_language), pl.ds(0, width + extra)],
            queries,
            in_sem.at[0],
        ),
        pltpu.make_async_copy(store.at[pl.ds(0, 3 * per_language)], taught, in_sem.at[1]),
    ]
    for copy in copies:
        copy.start()
    passages[pl.ds(0, 16), :] = jnp.zeros((16, width), jnp.bfloat16)

    def place(g, carry):
        for c in range(group_chunks):
            raw_copy(g * group_chunks + c).wait()
        start = pl.multiple_of((chunk_list[2 * chunk_count + g * group_chunks] // 16) * 16, 16)
        target = lax.broadcasted_iota(jnp.int32, (window, group_rows), 0)
        hit = target == target_of[pl.ds(g, 1), :] - start
        chosen = hit.astype(jnp.float32).astype(jnp.bfloat16)
        chunks = raw_v[pl.ds(g * group_chunks, group_chunks)].reshape(group_rows, width)
        moved = jnp.dot(chosen, chunks, preferred_element_type=jnp.float32).astype(jnp.bfloat16)
        head = passages[pl.ds(start, 16), :]
        passages[pl.ds(start, 16), :] = head + moved[:16]
        passages[pl.ds(start + 16, window - 16), :] = moved[16:]
        return carry

    lax.fori_loop(0, groups, place, 0)
    for copy in copies:
        copy.wait()

    def score_only(quarter, carry):
        score_quarter(queries, 0, quarter, passages, scores)
        return carry

    lax.fori_loop(0, 4, score_only, 0)
    held, free = scores, other_scores
    middle = pl.ds(per_language, per_language)
    for number in range(3):
        base = number * per_language

        def together(quarter, carry, base=base, held=held, free=free, last=number == 2):
            if last:
                columns = pl.ds(pl.multiple_of(quarter * 256, 256), 256)
                grad_columns(middle, columns, weights, passages, grad)
            else:
                score_quarter(queries, base + per_language, quarter, passages, free)
            student_pass(base, quarter, held, taught, queries, weights, kl)
            return carry

        lax.fori_loop(0, 4, together, 0)
        held, free = free, held
    grad[:, pl.ds(width, extra)] = kl_parts(kl[middle, :])


def first_blocks(chunk_list, raw, store):
    rows = 3 * per_language
    scores = pltpu.VMEM((per_language, passages_all), jnp.float32)
    return call(
        first_kernel,
        "first_blocks",
        [smem, vmem, hbm, hbm],
        [
            (vmem, (rows, passages_all), jnp.bfloat16),
            (vmem, (passages_all + window, width), jnp.bfloat16),
            (vmem, (rows, 128), jnp.float32),
            (vmem, (per_language, width + extra), jnp.bfloat16),
        ],
        [
            pltpu.VMEM((chunk_count, chunk_rows, width), jnp.bfloat16),
            pltpu.VMEM((rows, width + extra), jnp.bfloat16),
            pltpu.VMEM((rows, passages_all), jnp.bfloat16),
            scores,
            scores,
            pltpu.SemaphoreType.DMA((chunk_count,)),
            pltpu.SemaphoreType.DMA((2,)),
        ],
        40,
        6 * 1024**3,
        2 * mib,
    )(*chunk_list, raw, store)


def chunks_of(counts):
    number = (counts + chunk_rows - 1) // chunk_rows
    upto = jnp.arange(holders)[None, :] < jnp.arange(holders)[:, None]
    offsets = jnp.sum(jnp.where(upto, counts[None, :], 0), axis=1)
    firsts = jnp.sum(jnp.where(upto, number[None, :], 0), axis=1)
    index = jnp.arange(chunk_count)[:, None]
    mine = (index >= firsts[None, :]) & (index < (firsts + number)[None, :])
    row = (index - firsts[None, :]) * chunk_rows

    def pick(values):
        return jnp.sum(jnp.where(mine, values, 0), axis=1)

    holder = pick(jnp.arange(holders)[None, :] + 0 * row)
    used = pick(jnp.minimum(counts[None, :] - row, chunk_rows))
    place = jnp.where(used > 0, pick(offsets[None, :] + row), passages_all)
    slots = jnp.arange(chunk_rows)[None, :]
    groups = (jnp.sum(number) + group_chunks - 1) // group_chunks
    targets = jnp.where(slots < used[:, None], place[:, None] + slots, -1)
    return (
        jnp.concatenate([holder, pick(row), place, groups[None]]).astype(jnp.int32),
        targets.astype(jnp.int32).reshape(chunk_count // group_chunks, group_rows),
    )


def last_kernel(
    core, passages, before, queries, block, weights, send, keep, kl,
    own, teacher, scores, total, in_sem,
):
    own_copy = pltpu.make_async_copy(block.at[:, pl.ds(0, width)], own, in_sem.at[0])
    teacher_copy = pltpu.make_async_copy(
        block.at[:, pl.ds(width, passages_all)], teacher, in_sem.at[1]
    )
    own_copy.start()
    teacher_copy.start()
    own_copy.wait()

    def score_only(quarter, carry):
        score_quarter(own, 0, quarter, passages, scores)
        return carry

    lax.fori_loop(0, 4, score_only, 0)
    teacher_copy.wait()
    contract = (((0,), (0,)), ((), ()))

    def together(quarter, carry):
        row_pass(quarter, scores, teacher, weights, kl)
        columns = pl.ds(pl.multiple_of(quarter * 512, 512), 512)
        total[columns, :] = lax.dot_general(
            before[:, columns],
            queries[...],
            contract,
            preferred_element_type=jnp.float32,
        )
        return carry

    lax.fori_loop(0, 4, together, 0)
    even = core[0] == 0

    def reduce(j, carry):
        columns = pl.ds(pl.multiple_of(j * 256, 256), 256)
        grad = lax.dot_general(
            weights[:, columns],
            own[...],
            contract,
            preferred_element_type=jnp.float32,
        )
        grad = (grad + total[columns, :]).astype(jnp.bfloat16)
        for part in range(2):
            upper = grad[part * 128 : part * 128 + 64]
            lower = grad[part * 128 + 64 : part * 128 + 128]
            rows = pl.ds(pl.multiple_of(j * 128 + part * 64, 64), 64)
            keep[rows, :] = jnp.where(even, upper, lower)
            send[rows, :] = jnp.where(even, lower, upper)
        return carry

    lax.fori_loop(0, passages_all // 256, reduce, 0)


def last_block(core, passages, weights, queries, block):
    half = (vmem, (passages_all // 2, width), jnp.bfloat16)
    return call(
        last_kernel,
        "last_block",
        [smem] + [vmem] * 3 + [hbm],
        [
            (vmem, (per_language, passages_all), jnp.bfloat16),
            half,
            half,
            (vmem, (per_language, 128), jnp.float32),
        ],
        [
            pltpu.VMEM((per_language, width), jnp.bfloat16),
            pltpu.VMEM((per_language, passages_all), jnp.bfloat16),
            pltpu.VMEM((per_language, passages_all), jnp.float32),
            pltpu.VMEM((passages_all, width), jnp.float32),
            pltpu.SemaphoreType.DMA((2,)),
        ],
        20,
        6 * 1024**3,
        mib,
    )(core, passages, weights, queries, block)


def query_kernel(places, passages, *refs):
    for number, place in enumerate(places):
        weights, kl = refs[2 * number], refs[2 * number + 1]
        out = refs[2 * len(places) + number]
        rows = pl.ds(place * per_language, per_language)

        def step(half, carry, rows=rows, weights=weights, out=out):
            columns = pl.ds(pl.multiple_of(half * 512, 512), 512)
            grad_columns(rows, columns, weights, passages, out)
            return carry

        lax.fori_loop(0, 2, step, 0)
        out[:, pl.ds(width, extra)] = kl_parts(kl[rows, :])


def query_grads(places, passages, *arrays):
    return call(
        functools.partial(query_kernel, places),
        "query_grads",
        [vmem] * (1 + len(arrays)),
        [(vmem, (per_language, width + extra), jnp.bfloat16)] * len(places),
        [],
        8,
        len(places) * 1024**3,
    )(passages, *arrays)


def pair_kernel(keep, other, out):
    def step(i, carry):
        rows = pl.ds(pl.multiple_of(i * 64, 64), 64)
        out[rows, :] = (
            keep[rows, :].astype(jnp.float32) + other[rows, :].astype(jnp.float32)
        ).astype(jnp.bfloat16)
        return carry

    lax.fori_loop(0, passages_all // 128, step, 0)


def pair_sum(keep, other):
    return call(
        pair_kernel, "pair_sum", [vmem] * 2, [(vmem, keep.shape, jnp.bfloat16)], [], 8, mib
    )(keep, other)[0]


def restore_kernel(slot, in0, in1, in2, in3, grads_out, kl, select, grads, out_sem):
    rows = lax.broadcasted_iota(jnp.int32, (per_device, per_device), 0)
    select[...] = (rows == slot[0:1, :]).astype(jnp.float32).astype(jnp.bfloat16)
    contract = (((0,), (0,)), ((), ()))

    def joined(columns):
        part = None
        for number, block in enumerate((in0, in1, in2, in3)):
            chosen = select[number * per_language : (number + 1) * per_language, :]
            term = lax.dot_general(
                chosen, block[:, columns], contract, preferred_element_type=jnp.float32
            )
            part = term if part is None else part + term
        return part

    def written(j):
        columns = pl.ds(pl.multiple_of(j * 256, 256), 256)
        return pltpu.make_async_copy(grads.at[j], grads_out.at[:, columns], out_sem.at[j])

    def step(j, carry):
        columns = pl.ds(pl.multiple_of(j * 256, 256), 256)
        grads[j] = joined(columns).astype(jnp.bfloat16)
        written(j).start()
        return carry

    lax.fori_loop(0, width // 256, step, 0)
    column = jnp.sum(joined(pl.ds(width, extra)), axis=1, keepdims=True)
    kl[...] = jnp.transpose(jnp.broadcast_to(column, (per_device, 128)))[:1]
    for j in range(width // 256):
        written(j).wait()


def restore(slot, blocks):
    return call(
        restore_kernel,
        "restore",
        [vmem] * 5,
        [
            (hbm, (per_device, width), jnp.bfloat16),
            (vmem, (1, per_device), jnp.float32),
        ],
        [
            pltpu.VMEM((per_device, per_device), jnp.bfloat16),
            pltpu.VMEM((width // 256, per_device, 256), jnp.bfloat16),
            pltpu.SemaphoreType.DMA((width // 256,)),
        ],
        24,
        28 * 1024**3,
    )(slot, *blocks)


def sum_kernel(pieces, out, held, sems):
    copies = [
        pltpu.make_async_copy(pieces.at[pl.ds(4 * i, 4)], held.at[pl.ds(4 * i, 4)], sems.at[i])
        for i in range(4)
    ]
    for copy in copies:
        copy.start()
    total = jnp.zeros((64, width), jnp.float32)
    for i, copy in enumerate(copies):
        copy.wait()
        for j in range(4):
            total = total + held[4 * i + j].astype(jnp.float32)
    out[...] = total.astype(jnp.bfloat16)


def sum_pieces(pieces):
    return call(
        sum_kernel,
        "sum_pieces",
        [hbm],
        [(vmem, (64, width), jnp.bfloat16)],
        [pltpu.VMEM(pieces.shape, jnp.bfloat16), pltpu.SemaphoreType.DMA((4,))],
        8,
        mib,
    )(pieces)[0]


def shift(array, by):
    pairs = [(i, (i + by) % languages) for i in range(languages)]
    return lax.ppermute(array, "x", pairs)


def on_device(queries, bucket_ids, raw_passages, counts, teacher):
    group = ("y", "z", "c")
    here = lax.axis_index("x").astype(jnp.int32).reshape(1)
    core = lax.axis_index("c").astype(jnp.int32).reshape(1)
    all_raw = lax.all_gather(raw_passages[0], group, axis=0, tiled=True)
    ids = bucket_ids[0]
    out1, out3, slot = sort_rows(here, ids, None, queries[0, 0], teacher[0, 0])
    in1, in3 = shift(out1, 1), shift(out3, 3)
    out2, in0, _ = sort_rows(here, ids, slot, queries[0, 0], teacher[0, 0])
    held_counts, in0, out2 = lax.optimization_barrier((counts, in0, out2))
    holder_counts = lax.all_gather(held_counts[0], group, axis=0, tiled=True)
    chunk_list = chunks_of(holder_counts)
    out2, in1, in3, chunk_list = lax.optimization_barrier((out2, in1, in3, chunk_list))
    in2 = shift(out2, 2)
    store, moved = teacher_rows((in0, in1, in3))
    all_raw, store, moved = lax.optimization_barrier((all_raw, store, moved))
    weights, passages, kl, back1 = first_blocks(chunk_list, all_raw, store)
    last_weights, send, keep, last_kl = last_block(core, passages, weights, moved, in2)
    other = lax.ppermute(send, "c", [(0, 1), (1, 0)])
    back3, back2 = query_grads((2, 0), passages, weights, kl, last_weights, last_kl)
    home1, home3, home2 = shift(back1, -1), shift(back3, -3), shift(back2, -2)
    paired = pair_sum(keep, other)
    spread = lax.all_to_all(
        paired.reshape(16, 64, width), ("y", "z"), split_axis=0, concat_axis=0, tiled=True
    )
    paired, weights = lax.optimization_barrier((paired, weights))
    (back0,) = query_grads((0,), passages, weights, kl)
    grad_passages = sum_pieces(spread)
    grad_queries, kl_rows = restore(slot, (back0, home1, home2, home3))
    return (grad_queries[None, None], grad_passages[None], kl_rows[None])


def solution(mesh):
    split = Mesh(mesh.devices.reshape(4, 4, 4, 2), ("x", "y", "z", "c"))
    group = ("y", "z", "c")
    in_specs = (
        P("x", group, None, None),
        P("x", group, None),
        P("x", group, None, None),
        P("x", group),
        P("x", group, None, None),
    )
    out_specs = (P("x", group, None, None), P("x", group, None), P("x", group, None))
    return jax.shard_map(
        on_device, mesh=split, in_specs=in_specs, out_specs=out_specs, check_vma=False
    )
```

```python
import functools

import jax
import jax.numpy as jnp
from jax import lax
from jax.experimental import pallas as pl
from jax.experimental.pallas import tpu as pltpu
from jax.sharding import Mesh
from jax.sharding import PartitionSpec as P

student_scale = 0.1
languages = 4
holders = 32
capacity = 192
width = 1024
per_device = 1024
per_language = 256
passages_all = 2048
both = width + passages_all
group_chunks = 8
group_rows = 256
window = 272
extra = 128
chunk_rows = 32
chunk_count = 96
store_rows = 6144
mib = 1024 * 1024


def slots_of(ids, here):
    turned = lax.rem(ids - here + languages, languages)
    kinds = lax.broadcasted_iota(jnp.int32, (8, per_device), 0)
    hot = (turned == kinds).astype(jnp.float32)
    parts = per_device // 128
    stacked = jnp.concatenate([hot[:, i * 128 : (i + 1) * 128] for i in range(parts)], axis=0)
    earlier = lax.broadcasted_iota(jnp.int32, (128, 128), 0)
    later = lax.broadcasted_iota(jnp.int32, (128, 128), 1)
    upper = (earlier <= later).astype(jnp.float32).astype(jnp.bfloat16)
    sums = jnp.dot(stacked.astype(jnp.bfloat16), upper, preferred_element_type=jnp.float32)
    before = jnp.zeros((8, 1), jnp.float32)
    ranks = []
    for i in range(parts):
        segment = sums[i * 8 : (i + 1) * 8]
        ranks.append(segment + before)
        before = before + segment[:, 127:128]
    place = jnp.concatenate(ranks, axis=1) - 1.0 + kinds.astype(jnp.float32) * per_language
    return jnp.sum(hot * place, axis=0, keepdims=True).astype(jnp.int32)


vmem = pl.BlockSpec(memory_space=pltpu.VMEM)
smem = pl.BlockSpec(memory_space=pltpu.SMEM)
hbm = pl.BlockSpec(memory_space=pltpu.HBM)


def call(kernel, name, in_specs, outs, scratch, limit, flops, transcendentals=0):
    return pl.pallas_call(
        kernel,
        in_specs=in_specs,
        out_specs=[spec for spec, _, _ in outs],
        out_shape=[jax.ShapeDtypeStruct(shape, dtype) for _, shape, dtype in outs],
        scratch_shapes=scratch,
        compiler_params=pltpu.CompilerParams(vmem_limit_bytes=limit * mib),
        cost_estimate=pl.CostEstimate(
            flops=flops, bytes_accessed=8 * mib, transcendentals=transcendentals
        ),
        name=name,
    )


def sort_kernel(
    first, here, ids, slot_in, queries, teacher, out_a, out_b, slot,
    select, block, moved_a, moved_b, in_sem, out_sem,
):
    tile = 512
    tiles = both // tile

    def read(j):
        source = queries if j < width // tile else teacher
        column = j * tile if j < width // tile else j * tile - width
        return pltpu.make_async_copy(
            source.at[:, pl.ds(column, tile)], block.at[j], in_sem.at[j]
        )

    def written(j):
        columns = pl.ds(j * tile, tile)
        return [
            pltpu.make_async_copy(moved_a.at[j], out_a.at[:, columns], out_sem.at[2 * j]),
            pltpu.make_async_copy(moved_b.at[j], out_b.at[:, columns], out_sem.at[2 * j + 1]),
        ]

    for j in range(tiles):
        read(j).start()
    if first:
        slots = slots_of(ids[...], here[0])
        slot[...] = jnp.broadcast_to(slots, (8, per_device))
    else:
        slots = slot_in[0:1, :]
        slot[...] = jnp.zeros((8, 128), jnp.int32)
    rows = lax.broadcasted_iota(jnp.int32, (per_language, per_device), 0)
    for half, number in enumerate((1, 3) if first else (2, 0)):
        hit = rows + number * per_language == slots
        select[pl.ds(half * per_language, per_language), :] = hit.astype(jnp.float32).astype(
            jnp.bfloat16
        )
    for j in range(tiles):
        read(j).wait()
        moved = jnp.dot(select[...], block[j], preferred_element_type=jnp.float32)
        moved_a[j] = moved[:per_language].astype(jnp.bfloat16)
        moved_b[j] = moved[per_language:].astype(jnp.bfloat16)
        for copy in written(j):
            copy.start()
    for j in range(tiles):
        for copy in written(j):
            copy.wait()


def sort_rows(here, ids, slot, queries, teacher):
    first = slot is None
    tiles = both // 512
    moved = pltpu.VMEM((tiles, per_language, 512), jnp.bfloat16)
    out = (hbm, (per_language, both), jnp.bfloat16)
    return call(
        functools.partial(sort_kernel, first),
        "sort_first" if first else "sort_rest",
        [smem, vmem, vmem, hbm, hbm],
        [out, out, (vmem, (8, per_device) if first else (8, 128), jnp.int32)],
        [
            pltpu.VMEM((2 * per_language, per_device), jnp.bfloat16),
            pltpu.VMEM((tiles, per_device, 512), jnp.bfloat16),
            moved,
            moved,
            pltpu.SemaphoreType.DMA((tiles,)),
            pltpu.SemaphoreType.DMA((2 * tiles,)),
        ],
        60 if first else 28,
        4 * per_language * per_device * both,
    )(here, ids, ids if first else slot, queries, teacher)


def kl_parts(value):
    high = value.astype(jnp.bfloat16).astype(jnp.float32)
    middle = (value - high).astype(jnp.bfloat16).astype(jnp.float32)
    low = value - high - middle
    lane = lax.broadcasted_iota(jnp.int32, value.shape, 1)
    parts = jnp.where(
        lane == 0, high, jnp.where(lane == 1, middle, jnp.where(lane == 2, low, 0.0))
    )
    return parts.astype(jnp.bfloat16)


def row_pass(quarter, scores, block, weights, kl):
    for i in range(4):
        local = pl.ds(pl.multiple_of(quarter * 64 + i * 16, 16), 16)
        own = scores[local, :]
        taught = block[local, :].astype(jnp.float32)
        top = jnp.max(own, axis=1, keepdims=True)
        taught_top = jnp.max(taught, axis=1, keepdims=True)
        grown = jnp.exp(own - top)
        total = jnp.sum(grown, axis=1, keepdims=True)
        shifted = taught - taught_top
        taught_grown = jnp.exp(shifted)
        taught_total = jnp.sum(taught_grown, axis=1, keepdims=True)
        cross = jnp.sum(taught_grown * (shifted - (own - top)), axis=1, keepdims=True)
        diverge = cross / taught_total - jnp.log(taught_total) + jnp.log(total)
        weights[local, :] = (
            grown * (student_scale / total) - taught_grown * (student_scale / taught_total)
        ).astype(jnp.bfloat16)
        kl[local, :] = jnp.broadcast_to(diverge, (16, 128))


def score_quarter(queries, base, quarter, passages, scores):
    columns = pl.ds(pl.multiple_of(quarter * 512, 512), 512)
    scores[:, columns] = (
        lax.dot_general(
            queries[pl.ds(base, per_language), pl.ds(0, width)],
            passages[columns, :],
            (((1,), (1,)), ((), ())),
            preferred_element_type=jnp.float32,
        )
        * student_scale
    )


def teacher_kernel(in0, in1, in2, store, queries, taught_out, parts, sems):
    rows = 3 * per_language

    def saved(number):
        block = pl.ds(number * per_language, per_language)
        behind = pl.ds(rows + number * per_language, per_language)
        return [
            pltpu.make_async_copy(taught_out.at[block], store.at[block], sems.at[number]),
            pltpu.make_async_copy(
                queries.at[block], store.at[behind, pl.ds(0, width)], sems.at[3 + number]
            ),
            pltpu.make_async_copy(
                parts.at[block], store.at[behind, pl.ds(width, extra)], sems.at[6 + number]
            ),
        ]

    for number, block in enumerate((in0, in1, in2)):

        def rows_of(i, carry, number=number, block=block):
            for part in range(4):
                local = pl.ds(pl.multiple_of(i * 64 + part * 16, 16), 16)
                placed = pl.ds(
                    pl.multiple_of(number * per_language + i * 64 + part * 16, 16), 16
                )
                queries[placed, :] = block[local, pl.ds(0, width)]
                taught = block[local, pl.ds(width, passages_all)].astype(jnp.float32)
                shifted = taught - jnp.max(taught, axis=1, keepdims=True)
                grown = jnp.exp(shifted)
                total = jnp.sum(grown, axis=1, keepdims=True)
                cross = jnp.sum(grown * shifted, axis=1, keepdims=True)
                taught_out[placed, :] = (grown * (student_scale / total)).astype(jnp.bfloat16)
                entropy = jnp.broadcast_to(cross / total - jnp.log(total), (16, 128))
                parts[placed, :] = kl_parts(entropy)
            return carry

        lax.fori_loop(0, 4, rows_of, 0)
        for copy in saved(number):
            copy.start()
    for number in range(3):
        for copy in saved(number):
            copy.wait()


def teacher_rows(blocks):
    rows = 3 * per_language
    return call(
        teacher_kernel,
        "teacher_rows",
        [vmem] * 3,
        [
            (hbm, (store_rows, passages_all), jnp.bfloat16),
            (vmem, (rows, width), jnp.bfloat16),
        ],
        [
            pltpu.VMEM((rows, passages_all), jnp.bfloat16),
            pltpu.VMEM((rows, extra), jnp.bfloat16),
            pltpu.SemaphoreType.DMA((9,)),
        ],
        40,
        mib,
        2 * mib,
    )(*blocks)


def student_pass(base, quarter, scores, taught_ref, parts, weights, kl):
    for i in range(4):
        local = pl.ds(pl.multiple_of(quarter * 64 + i * 16, 16), 16)
        placed = pl.ds(pl.multiple_of(base + quarter * 64 + i * 16, 16), 16)
        own = scores[local, :]
        taught = taught_ref[placed, :].astype(jnp.float32)
        shifted = own - jnp.max(own, axis=1, keepdims=True)
        grown = jnp.exp(shifted)
        total = jnp.sum(grown, axis=1, keepdims=True)
        cross = jnp.sum(taught * shifted, axis=1, keepdims=True)
        entropy = jnp.sum(
            parts[placed, pl.ds(width, extra)].astype(jnp.float32), axis=1, keepdims=True
        )
        diverge = entropy + jnp.log(total) - cross * (1.0 / student_scale)
        weights[placed, :] = (grown * (student_scale / total) - taught).astype(jnp.bfloat16)
        kl[placed, :] = jnp.broadcast_to(diverge, (16, 128))


def grad_columns(rows, columns, weights, passages, out):
    out[:, columns] = jnp.dot(
        weights[rows, :],
        passages[pl.ds(0, passages_all), columns],
        preferred_element_type=jnp.float32,
    ).astype(jnp.bfloat16)


def first_kernel(
    chunk_list, target_of, raw, store,
    weights, passages, kl, grad, raw_v, queries, taught, scores, other_scores, raw_sem, in_sem,
):
    def raw_copy(k):
        rows = pl.ds(pl.multiple_of(chunk_list[chunk_count + k], chunk_rows), chunk_rows)
        return pltpu.make_async_copy(raw.at[chunk_list[k], rows], raw_v.at[k], raw_sem.at[k])

    groups = chunk_list[3 * chunk_count]

    def start_group(g, carry):
        for c in range(2 * group_chunks):
            raw_copy(2 * g * group_chunks + c).start()
        return carry

    lax.fori_loop(0, groups, start_group, 0)
    copies = [
        pltpu.make_async_copy(
            store.at[pl.ds(3 * per_language, 3 * per_language), pl.ds(0, width + extra)],
            queries,
            in_sem.at[0],
        ),
        pltpu.make_async_copy(store.at[pl.ds(0, 3 * per_language)], taught, in_sem.at[1]),
    ]
    for copy in copies:
        copy.start()
    passages[pl.ds(0, 16), :] = jnp.zeros((16, width), jnp.bfloat16)

    def place(pair, carry):
        ready = []
        for g in (2 * pair, 2 * pair + 1):
            for c in range(group_chunks):
                raw_copy(g * group_chunks + c).wait()
        for g in (2 * pair, 2 * pair + 1):
            first = chunk_list[2 * chunk_count + g * group_chunks]
            start = pl.multiple_of((first // 16) * 16, 16)
            target = lax.broadcasted_iota(jnp.int32, (window, group_rows), 0)
            hit = target == target_of[pl.ds(g, 1), :] - start
            chosen = hit.astype(jnp.float32).astype(jnp.bfloat16)
            chunks = raw_v[pl.ds(g * group_chunks, group_chunks)].reshape(group_rows, width)
            moved = jnp.dot(chosen, chunks, preferred_element_type=jnp.float32)
            ready.append((start, moved.astype(jnp.bfloat16)))
        for start, moved in ready:
            head = passages[pl.ds(start, 16), :]
            passages[pl.ds(start, 16), :] = head + moved[:16]
            passages[pl.ds(start + 16, window - 16), :] = moved[16:]
        return carry

    lax.fori_loop(0, groups, place, 0)
    for copy in copies:
        copy.wait()

    def score_only(quarter, carry):
        score_quarter(queries, 0, quarter, passages, scores)
        return carry

    lax.fori_loop(0, 4, score_only, 0)
    held, free = scores, other_scores
    middle = pl.ds(per_language, per_language)
    for number in range(3):
        base = number * per_language

        def together(quarter, carry, base=base, held=held, free=free, last=number == 2):
            if last:
                columns = pl.ds(pl.multiple_of(quarter * 256, 256), 256)
                grad_columns(middle, columns, weights, passages, grad)
            else:
                score_quarter(queries, base + per_language, quarter, passages, free)
            student_pass(base, quarter, held, taught, queries, weights, kl)
            return carry

        lax.fori_loop(0, 4, together, 0)
        held, free = free, held
    grad[:, pl.ds(width, extra)] = kl_parts(kl[middle, :])


def first_blocks(chunk_list, raw, store):
    rows = 3 * per_language
    scores = pltpu.VMEM((per_language, passages_all), jnp.float32)
    return call(
        first_kernel,
        "first_blocks",
        [smem, vmem, hbm, hbm],
        [
            (vmem, (rows, passages_all), jnp.bfloat16),
            (vmem, (passages_all + window, width), jnp.bfloat16),
            (vmem, (rows, 128), jnp.float32),
            (vmem, (per_language, width + extra), jnp.bfloat16),
        ],
        [
            pltpu.VMEM((chunk_count, chunk_rows, width), jnp.bfloat16),
            pltpu.VMEM((rows, width + extra), jnp.bfloat16),
            pltpu.VMEM((rows, passages_all), jnp.bfloat16),
            scores,
            scores,
            pltpu.SemaphoreType.DMA((chunk_count,)),
            pltpu.SemaphoreType.DMA((2,)),
        ],
        40,
        6 * 1024**3,
        2 * mib,
    )(*chunk_list, raw, store)


def chunks_of(counts):
    number = (counts + chunk_rows - 1) // chunk_rows
    upto = jnp.arange(holders)[None, :] < jnp.arange(holders)[:, None]
    offsets = jnp.sum(jnp.where(upto, counts[None, :], 0), axis=1)
    firsts = jnp.sum(jnp.where(upto, number[None, :], 0), axis=1)
    index = jnp.arange(chunk_count)[:, None]
    mine = (index >= firsts[None, :]) & (index < (firsts + number)[None, :])
    row = (index - firsts[None, :]) * chunk_rows

    def pick(values):
        return jnp.sum(jnp.where(mine, values, 0), axis=1)

    holder = pick(jnp.arange(holders)[None, :] + 0 * row)
    used = pick(jnp.minimum(counts[None, :] - row, chunk_rows))
    place = jnp.where(used > 0, pick(offsets[None, :] + row), passages_all)
    slots = jnp.arange(chunk_rows)[None, :]
    groups = (jnp.sum(number) + 2 * group_chunks - 1) // (2 * group_chunks)
    targets = jnp.where(slots < used[:, None], place[:, None] + slots, -1)
    return (
        jnp.concatenate([holder, pick(row), place, groups[None]]).astype(jnp.int32),
        targets.astype(jnp.int32).reshape(chunk_count // group_chunks, group_rows),
    )


def last_kernel(
    core, passages, before, queries, block, weights, send, keep, kl,
    own, teacher, scores, total, in_sem,
):
    own_copy = pltpu.make_async_copy(block.at[:, pl.ds(0, width)], own, in_sem.at[0])
    teacher_copy = pltpu.make_async_copy(
        block.at[:, pl.ds(width, passages_all)], teacher, in_sem.at[1]
    )
    own_copy.start()
    teacher_copy.start()
    own_copy.wait()

    def score_only(quarter, carry):
        score_quarter(own, 0, quarter, passages, scores)
        return carry

    lax.fori_loop(0, 4, score_only, 0)
    teacher_copy.wait()
    contract = (((0,), (0,)), ((), ()))

    def together(quarter, carry):
        row_pass(quarter, scores, teacher, weights, kl)
        columns = pl.ds(pl.multiple_of(quarter * 512, 512), 512)
        total[columns, :] = lax.dot_general(
            before[:, columns],
            queries[...],
            contract,
            preferred_element_type=jnp.float32,
        )
        return carry

    lax.fori_loop(0, 4, together, 0)
    even = core[0] == 0

    def reduce(j, carry):
        columns = pl.ds(pl.multiple_of(j * 256, 256), 256)
        grad = lax.dot_general(
            weights[:, columns],
            own[...],
            contract,
            preferred_element_type=jnp.float32,
        )
        grad = (grad + total[columns, :]).astype(jnp.bfloat16)
        for part in range(2):
            upper = grad[part * 128 : part * 128 + 64]
            lower = grad[part * 128 + 64 : part * 128 + 128]
            rows = pl.ds(pl.multiple_of(j * 128 + part * 64, 64), 64)
            keep[rows, :] = jnp.where(even, upper, lower)
            send[rows, :] = jnp.where(even, lower, upper)
        return carry

    lax.fori_loop(0, passages_all // 256, reduce, 0)


def last_block(core, passages, weights, queries, block):
    half = (vmem, (passages_all // 2, width), jnp.bfloat16)
    return call(
        last_kernel,
        "last_block",
        [smem] + [vmem] * 3 + [hbm],
        [
            (vmem, (per_language, passages_all), jnp.bfloat16),
            half,
            half,
            (vmem, (per_language, 128), jnp.float32),
        ],
        [
            pltpu.VMEM((per_language, width), jnp.bfloat16),
            pltpu.VMEM((per_language, passages_all), jnp.bfloat16),
            pltpu.VMEM((per_language, passages_all), jnp.float32),
            pltpu.VMEM((passages_all, width), jnp.float32),
            pltpu.SemaphoreType.DMA((2,)),
        ],
        20,
        6 * 1024**3,
        mib,
    )(core, passages, weights, queries, block)


def query_kernel(places, passages, *refs):
    for number, place in enumerate(places):
        weights, kl = refs[2 * number], refs[2 * number + 1]
        out = refs[2 * len(places) + number]
        rows = pl.ds(place * per_language, per_language)

        def step(half, carry, rows=rows, weights=weights, out=out):
            columns = pl.ds(pl.multiple_of(half * 512, 512), 512)
            grad_columns(rows, columns, weights, passages, out)
            return carry

        lax.fori_loop(0, 2, step, 0)
        out[:, pl.ds(width, extra)] = kl_parts(kl[rows, :])


def query_grads(places, passages, *arrays):
    return call(
        functools.partial(query_kernel, places),
        "query_grads",
        [vmem] * (1 + len(arrays)),
        [(vmem, (per_language, width + extra), jnp.bfloat16)] * len(places),
        [],
        8,
        len(places) * 1024**3,
    )(passages, *arrays)


def pair_kernel(keep, other, out):
    def step(i, carry):
        rows = pl.ds(pl.multiple_of(i * 64, 64), 64)
        out[rows, :] = (
            keep[rows, :].astype(jnp.float32) + other[rows, :].astype(jnp.float32)
        ).astype(jnp.bfloat16)
        return carry

    lax.fori_loop(0, passages_all // 128, step, 0)


def pair_sum(keep, other):
    return call(
        pair_kernel, "pair_sum", [vmem] * 2, [(vmem, keep.shape, jnp.bfloat16)], [], 8, mib
    )(keep, other)[0]


def restore_kernel(slot, in0, in1, in2, in3, grads_out, kl, select, grads, out_sem):
    rows = lax.broadcasted_iota(jnp.int32, (per_device, per_device), 0)
    select[...] = (rows == slot[0:1, :]).astype(jnp.float32).astype(jnp.bfloat16)
    contract = (((0,), (0,)), ((), ()))

    def joined(columns):
        part = None
        for number, block in enumerate((in0, in1, in2, in3)):
            chosen = select[number * per_language : (number + 1) * per_language, :]
            term = lax.dot_general(
                chosen, block[:, columns], contract, preferred_element_type=jnp.float32
            )
            part = term if part is None else part + term
        return part

    def written(j):
        columns = pl.ds(pl.multiple_of(j * 256, 256), 256)
        return pltpu.make_async_copy(grads.at[j], grads_out.at[:, columns], out_sem.at[j])

    def step(j, carry):
        columns = pl.ds(pl.multiple_of(j * 256, 256), 256)
        grads[j] = joined(columns).astype(jnp.bfloat16)
        written(j).start()
        return carry

    lax.fori_loop(0, width // 256, step, 0)
    column = jnp.sum(joined(pl.ds(width, extra)), axis=1, keepdims=True)
    kl[...] = jnp.transpose(jnp.broadcast_to(column, (per_device, 128)))[:1]
    for j in range(width // 256):
        written(j).wait()


def restore(slot, blocks):
    return call(
        restore_kernel,
        "restore",
        [vmem] * 5,
        [
            (hbm, (per_device, width), jnp.bfloat16),
            (vmem, (1, per_device), jnp.float32),
        ],
        [
            pltpu.VMEM((per_device, per_device), jnp.bfloat16),
            pltpu.VMEM((width // 256, per_device, 256), jnp.bfloat16),
            pltpu.SemaphoreType.DMA((width // 256,)),
        ],
        24,
        28 * 1024**3,
    )(slot, *blocks)


def sum_kernel(pieces, out, held, sems):
    copies = [
        pltpu.make_async_copy(pieces.at[pl.ds(4 * i, 4)], held.at[pl.ds(4 * i, 4)], sems.at[i])
        for i in range(4)
    ]
    for copy in copies:
        copy.start()
    total = jnp.zeros((64, width), jnp.float32)
    for i, copy in enumerate(copies):
        copy.wait()
        for j in range(4):
            total = total + held[4 * i + j].astype(jnp.float32)
    out[...] = total.astype(jnp.bfloat16)


def sum_pieces(pieces):
    return call(
        sum_kernel,
        "sum_pieces",
        [hbm],
        [(vmem, (64, width), jnp.bfloat16)],
        [pltpu.VMEM(pieces.shape, jnp.bfloat16), pltpu.SemaphoreType.DMA((4,))],
        8,
        mib,
    )(pieces)[0]


def shift(array, by):
    pairs = [(i, (i + by) % languages) for i in range(languages)]
    return lax.ppermute(array, "x", pairs)


def on_device(queries, bucket_ids, raw_passages, counts, teacher):
    group = ("y", "z", "c")
    here = lax.axis_index("x").astype(jnp.int32).reshape(1)
    core = lax.axis_index("c").astype(jnp.int32).reshape(1)
    all_raw = lax.all_gather(raw_passages[0], group, axis=0, tiled=True)
    ids = bucket_ids[0]
    out1, out3, slot = sort_rows(here, ids, None, queries[0, 0], teacher[0, 0])
    in1, in3 = shift(out1, 1), shift(out3, 3)
    out2, in0, zeros = sort_rows(here, ids, slot, queries[0, 0], teacher[0, 0])
    holder_counts = lax.all_gather(counts[0] + zeros[0, 0], group, axis=0, tiled=True)
    chunk_list = chunks_of(holder_counts)
    out2, chunk_list = lax.optimization_barrier((out2, chunk_list))
    in2 = shift(out2, 2)
    store, moved = teacher_rows((in0, in1, in3))
    all_raw, store, moved = lax.optimization_barrier((all_raw, store, moved))
    weights, passages, kl, back1 = first_blocks(chunk_list, all_raw, store)
    last_weights, send, keep, last_kl = last_block(core, passages, weights, moved, in2)
    other = lax.ppermute(send, "c", [(0, 1), (1, 0)])
    back3, back2 = query_grads((2, 0), passages, weights, kl, last_weights, last_kl)
    home1, home3, home2 = shift(back1, -1), shift(back3, -3), shift(back2, -2)
    paired = pair_sum(keep, other)
    spread = lax.all_to_all(
        paired.reshape(16, 64, width), ("y", "z"), split_axis=0, concat_axis=0, tiled=True
    )
    paired, weights = lax.optimization_barrier((paired, weights))
    (back0,) = query_grads((0,), passages, weights, kl)
    grad_passages = sum_pieces(spread)
    grad_queries, kl_rows = restore(slot, (back0, home1, home2, home3))
    return (grad_queries[None, None], grad_passages[None], kl_rows[None])


def solution(mesh):
    split = Mesh(mesh.devices.reshape(4, 4, 4, 2), ("x", "y", "z", "c"))
    group = ("y", "z", "c")
    in_specs = (
        P("x", group, None, None),
        P("x", group, None),
        P("x", group, None, None),
        P("x", group),
        P("x", group, None, None),
    )
    out_specs = (P("x", group, None, None), P("x", group, None), P("x", group, None))
    return jax.shard_map(
        on_device, mesh=split, in_specs=in_specs, out_specs=out_specs, check_vma=False
    )
```

```python
import functools

import jax
import jax.numpy as jnp
from jax import lax
from jax.experimental import pallas as pl
from jax.experimental.pallas import tpu as pltpu
from jax.sharding import Mesh
from jax.sharding import PartitionSpec as P

student_scale = 0.1
languages = 4
holders = 32
capacity = 192
width = 1024
per_device = 1024
per_language = 256
passages_all = 2048
both = width + passages_all
group_chunks = 8
group_rows = 256
window = 272
extra = 128
chunk_rows = 32
chunk_count = 96
store_rows = 6144
mib = 1024 * 1024


def slots_of(ids, here):
    turned = lax.rem(ids - here + languages, languages)
    kinds = lax.broadcasted_iota(jnp.int32, (8, per_device), 0)
    hot = (turned == kinds).astype(jnp.float32)
    parts = per_device // 128
    stacked = jnp.concatenate([hot[:, i * 128 : (i + 1) * 128] for i in range(parts)], axis=0)
    earlier = lax.broadcasted_iota(jnp.int32, (128, 128), 0)
    later = lax.broadcasted_iota(jnp.int32, (128, 128), 1)
    upper = (earlier <= later).astype(jnp.float32).astype(jnp.bfloat16)
    sums = jnp.dot(stacked.astype(jnp.bfloat16), upper, preferred_element_type=jnp.float32)
    before = jnp.zeros((8, 1), jnp.float32)
    ranks = []
    for i in range(parts):
        segment = sums[i * 8 : (i + 1) * 8]
        ranks.append(segment + before)
        before = before + segment[:, 127:128]
    place = jnp.concatenate(ranks, axis=1) - 1.0 + kinds.astype(jnp.float32) * per_language
    return jnp.sum(hot * place, axis=0, keepdims=True).astype(jnp.int32)


vmem = pl.BlockSpec(memory_space=pltpu.VMEM)
smem = pl.BlockSpec(memory_space=pltpu.SMEM)
hbm = pl.BlockSpec(memory_space=pltpu.HBM)


def call(kernel, name, in_specs, outs, scratch, limit, flops, transcendentals=0):
    return pl.pallas_call(
        kernel,
        in_specs=in_specs,
        out_specs=[spec for spec, _, _ in outs],
        out_shape=[jax.ShapeDtypeStruct(shape, dtype) for _, shape, dtype in outs],
        scratch_shapes=scratch,
        compiler_params=pltpu.CompilerParams(vmem_limit_bytes=limit * mib),
        cost_estimate=pl.CostEstimate(
            flops=flops, bytes_accessed=8 * mib, transcendentals=transcendentals
        ),
        name=name,
    )


def sort_kernel(
    first, here, ids, slot_in, queries, teacher, out_a, out_b, slot,
    select, block, moved_a, moved_b, in_sem, out_sem,
):
    tile = 512
    tiles = both // tile

    def read(j):
        source = queries if j < width // tile else teacher
        column = j * tile if j < width // tile else j * tile - width
        return pltpu.make_async_copy(
            source.at[:, pl.ds(column, tile)], block.at[j], in_sem.at[j]
        )

    def written(j):
        columns = pl.ds(j * tile, tile)
        return [
            pltpu.make_async_copy(moved_a.at[j], out_a.at[:, columns], out_sem.at[2 * j]),
            pltpu.make_async_copy(moved_b.at[j], out_b.at[:, columns], out_sem.at[2 * j + 1]),
        ]

    for j in range(tiles):
        read(j).start()
    if first:
        slots = slots_of(ids[...], here[0])
        slot[...] = jnp.broadcast_to(slots, (8, per_device))
    else:
        slots = slot_in[0:1, :]
        slot[...] = jnp.zeros((8, 128), jnp.int32)
    rows = lax.broadcasted_iota(jnp.int32, (per_language, per_device), 0)
    for half, number in enumerate((1, 3) if first else (2, 0)):
        hit = rows + number * per_language == slots
        select[pl.ds(half * per_language, per_language), :] = hit.astype(jnp.float32).astype(
            jnp.bfloat16
        )
    for j in range(tiles):
        read(j).wait()
        moved = jnp.dot(select[...], block[j], preferred_element_type=jnp.float32)
        moved_a[j] = moved[:per_language].astype(jnp.bfloat16)
        moved_b[j] = moved[per_language:].astype(jnp.bfloat16)
        for copy in written(j):
            copy.start()
    for j in range(tiles):
        for copy in written(j):
            copy.wait()


def sort_rows(here, ids, slot, queries, teacher):
    first = slot is None
    tiles = both // 512
    moved = pltpu.VMEM((tiles, per_language, 512), jnp.bfloat16)
    out = (hbm, (per_language, both), jnp.bfloat16)
    return call(
        functools.partial(sort_kernel, first),
        "sort_first" if first else "sort_rest",
        [smem, vmem, vmem, hbm, hbm],
        [out, out, (vmem, (8, per_device) if first else (8, 128), jnp.int32)],
        [
            pltpu.VMEM((2 * per_language, per_device), jnp.bfloat16),
            pltpu.VMEM((tiles, per_device, 512), jnp.bfloat16),
            moved,
            moved,
            pltpu.SemaphoreType.DMA((tiles,)),
            pltpu.SemaphoreType.DMA((2 * tiles,)),
        ],
        60 if first else 28,
        4 * per_language * per_device * both,
    )(here, ids, ids if first else slot, queries, teacher)


def kl_parts(value):
    high = value.astype(jnp.bfloat16).astype(jnp.float32)
    middle = (value - high).astype(jnp.bfloat16).astype(jnp.float32)
    low = value - high - middle
    lane = lax.broadcasted_iota(jnp.int32, value.shape, 1)
    parts = jnp.where(
        lane == 0, high, jnp.where(lane == 1, middle, jnp.where(lane == 2, low, 0.0))
    )
    return parts.astype(jnp.bfloat16)


def row_pass(quarter, scores, block, weights, kl):
    for i in range(4):
        local = pl.ds(pl.multiple_of(quarter * 64 + i * 16, 16), 16)
        own = scores[local, :]
        taught = block[local, :].astype(jnp.float32)
        top = jnp.max(own, axis=1, keepdims=True)
        taught_top = jnp.max(taught, axis=1, keepdims=True)
        grown = jnp.exp(own - top)
        total = jnp.sum(grown, axis=1, keepdims=True)
        shifted = taught - taught_top
        taught_grown = jnp.exp(shifted)
        taught_total = jnp.sum(taught_grown, axis=1, keepdims=True)
        cross = jnp.sum(taught_grown * (shifted - (own - top)), axis=1, keepdims=True)
        diverge = cross / taught_total - jnp.log(taught_total) + jnp.log(total)
        weights[local, :] = (
            grown * (student_scale / total) - taught_grown * (student_scale / taught_total)
        ).astype(jnp.bfloat16)
        kl[local, :] = jnp.broadcast_to(diverge, (16, 128))


def score_quarter(queries, base, quarter, passages, scores):
    columns = pl.ds(pl.multiple_of(quarter * 512, 512), 512)
    scores[:, columns] = (
        lax.dot_general(
            queries[pl.ds(base, per_language), pl.ds(0, width)],
            passages[columns, :],
            (((1,), (1,)), ((), ())),
            preferred_element_type=jnp.float32,
        )
        * student_scale
    )


def teacher_kernel(in0, in1, in2, store, queries, taught_out, parts, sems):
    rows = 3 * per_language

    def saved(number):
        block = pl.ds(number * per_language, per_language)
        behind = pl.ds(rows + number * per_language, per_language)
        return [
            pltpu.make_async_copy(taught_out.at[block], store.at[block], sems.at[number]),
            pltpu.make_async_copy(
                queries.at[block], store.at[behind, pl.ds(0, width)], sems.at[3 + number]
            ),
            pltpu.make_async_copy(
                parts.at[block], store.at[behind, pl.ds(width, extra)], sems.at[6 + number]
            ),
        ]

    for number, block in enumerate((in0, in1, in2)):

        def rows_of(i, carry, number=number, block=block):
            for part in range(4):
                local = pl.ds(pl.multiple_of(i * 64 + part * 16, 16), 16)
                placed = pl.ds(
                    pl.multiple_of(number * per_language + i * 64 + part * 16, 16), 16
                )
                queries[placed, :] = block[local, pl.ds(0, width)]
                taught = block[local, pl.ds(width, passages_all)].astype(jnp.float32)
                shifted = taught - jnp.max(taught, axis=1, keepdims=True)
                grown = jnp.exp(shifted)
                total = jnp.sum(grown, axis=1, keepdims=True)
                cross = jnp.sum(grown * shifted, axis=1, keepdims=True)
                taught_out[placed, :] = (grown * (student_scale / total)).astype(jnp.bfloat16)
                entropy = jnp.broadcast_to(cross / total - jnp.log(total), (16, 128))
                parts[placed, :] = kl_parts(entropy)
            return carry

        lax.fori_loop(0, 4, rows_of, 0)
        for copy in saved(number):
            copy.start()
    for number in range(3):
        for copy in saved(number):
            copy.wait()


def teacher_rows(blocks):
    rows = 3 * per_language
    return call(
        teacher_kernel,
        "teacher_rows",
        [vmem] * 3,
        [
            (hbm, (store_rows, passages_all), jnp.bfloat16),
            (vmem, (rows, width), jnp.bfloat16),
        ],
        [
            pltpu.VMEM((rows, passages_all), jnp.bfloat16),
            pltpu.VMEM((rows, extra), jnp.bfloat16),
            pltpu.SemaphoreType.DMA((9,)),
        ],
        40,
        mib,
        2 * mib,
    )(*blocks)


def student_pass(base, quarter, scores, taught_ref, parts, weights, kl):
    for i in range(4):
        local = pl.ds(pl.multiple_of(quarter * 64 + i * 16, 16), 16)
        placed = pl.ds(pl.multiple_of(base + quarter * 64 + i * 16, 16), 16)
        own = scores[local, :]
        taught = taught_ref[placed, :].astype(jnp.float32)
        shifted = own - jnp.max(own, axis=1, keepdims=True)
        grown = jnp.exp(shifted)
        total = jnp.sum(grown, axis=1, keepdims=True)
        cross = jnp.sum(taught * shifted, axis=1, keepdims=True)
        entropy = jnp.sum(
            parts[placed, pl.ds(width, extra)].astype(jnp.float32), axis=1, keepdims=True
        )
        diverge = entropy + jnp.log(total) - cross * (1.0 / student_scale)
        weights[placed, :] = (grown * (student_scale / total) - taught).astype(jnp.bfloat16)
        kl[placed, :] = jnp.broadcast_to(diverge, (16, 128))


def grad_columns(rows, columns, weights, passages, out):
    out[:, columns] = jnp.dot(
        weights[rows, :],
        passages[pl.ds(0, passages_all), columns],
        preferred_element_type=jnp.float32,
    ).astype(jnp.bfloat16)


def first_kernel(
    chunk_list, target_of, raw, store,
    weights, passages, kl, grad, raw_v, queries, taught, scores, other_scores, raw_sem, in_sem,
):
    def raw_copy(k):
        rows = pl.ds(pl.multiple_of(chunk_list[chunk_count + k], chunk_rows), chunk_rows)
        return pltpu.make_async_copy(raw.at[chunk_list[k], rows], raw_v.at[k], raw_sem.at[k])

    groups = chunk_list[3 * chunk_count]

    def start_group(g, carry):
        for c in range(group_chunks):
            raw_copy(g * group_chunks + c).start()
        return carry

    lax.fori_loop(0, groups, start_group, 0)
    copies = [
        pltpu.make_async_copy(
            store.at[pl.ds(3 * per_language, 3 * per_language), pl.ds(0, width + extra)],
            queries,
            in_sem.at[0],
        ),
        pltpu.make_async_copy(store.at[pl.ds(0, 3 * per_language)], taught, in_sem.at[1]),
    ]
    for copy in copies:
        copy.start()
    passages[pl.ds(0, 16), :] = jnp.zeros((16, width), jnp.bfloat16)

    def place(g, carry):
        for c in range(group_chunks):
            raw_copy(g * group_chunks + c).wait()
        start = pl.multiple_of((chunk_list[2 * chunk_count + g * group_chunks] // 16) * 16, 16)
        target = lax.broadcasted_iota(jnp.int32, (window, group_rows), 0)
        hit = target == target_of[pl.ds(g, 1), :] - start
        chosen = hit.astype(jnp.float32).astype(jnp.bfloat16)
        chunks = raw_v[pl.ds(g * group_chunks, group_chunks)].reshape(group_rows, width)
        moved = jnp.dot(chosen, chunks, preferred_element_type=jnp.float32).astype(jnp.bfloat16)
        head = passages[pl.ds(start, 16), :]
        passages[pl.ds(start, 16), :] = head + moved[:16]
        passages[pl.ds(start + 16, window - 16), :] = moved[16:]
        return carry

    lax.fori_loop(0, groups, place, 0)
    for copy in copies:
        copy.wait()

    def score_only(quarter, carry):
        score_quarter(queries, 0, quarter, passages, scores)
        return carry

    lax.fori_loop(0, 4, score_only, 0)
    held, free = scores, other_scores
    middle = pl.ds(per_language, per_language)
    for number in range(3):
        base = number * per_language

        def together(quarter, carry, base=base, held=held, free=free, last=number == 2):
            if last:
                columns = pl.ds(pl.multiple_of(quarter * 256, 256), 256)
                grad_columns(middle, columns, weights, passages, grad)
            else:
                score_quarter(queries, base + per_language, quarter, passages, free)
            student_pass(base, quarter, held, taught, queries, weights, kl)
            return carry

        lax.fori_loop(0, 4, together, 0)
        held, free = free, held
    grad[:, pl.ds(width, extra)] = kl_parts(kl[middle, :])


def first_blocks(chunk_list, raw, store):
    rows = 3 * per_language
    scores = pltpu.VMEM((per_language, passages_all), jnp.float32)
    return call(
        first_kernel,
        "first_blocks",
        [smem, vmem, hbm, hbm],
        [
            (vmem, (rows, passages_all), jnp.bfloat16),
            (vmem, (passages_all + window, width), jnp.bfloat16),
            (vmem, (rows, 128), jnp.float32),
            (vmem, (per_language, width + extra), jnp.bfloat16),
        ],
        [
            pltpu.VMEM((chunk_count, chunk_rows, width), jnp.bfloat16),
            pltpu.VMEM((rows, width + extra), jnp.bfloat16),
            pltpu.VMEM((rows, passages_all), jnp.bfloat16),
            scores,
            scores,
            pltpu.SemaphoreType.DMA((chunk_count,)),
            pltpu.SemaphoreType.DMA((2,)),
        ],
        40,
        6 * 1024**3,
        2 * mib,
    )(*chunk_list, raw, store)


def chunks_of(counts):
    number = (counts + chunk_rows - 1) // chunk_rows
    upto = jnp.arange(holders)[None, :] < jnp.arange(holders)[:, None]
    offsets = jnp.sum(jnp.where(upto, counts[None, :], 0), axis=1)
    firsts = jnp.sum(jnp.where(upto, number[None, :], 0), axis=1)
    index = jnp.arange(chunk_count)[:, None]
    mine = (index >= firsts[None, :]) & (index < (firsts + number)[None, :])
    row = (index - firsts[None, :]) * chunk_rows

    def pick(values):
        return jnp.sum(jnp.where(mine, values, 0), axis=1)

    holder = pick(jnp.arange(holders)[None, :] + 0 * row)
    used = pick(jnp.minimum(counts[None, :] - row, chunk_rows))
    place = jnp.where(used > 0, pick(offsets[None, :] + row), passages_all)
    slots = jnp.arange(chunk_rows)[None, :]
    groups = (jnp.sum(number) + group_chunks - 1) // group_chunks
    targets = jnp.where(slots < used[:, None], place[:, None] + slots, -1)
    return (
        jnp.concatenate([holder, pick(row), place, groups[None]]).astype(jnp.int32),
        targets.astype(jnp.int32).reshape(chunk_count // group_chunks, group_rows),
    )


def last_kernel(
    core, passages, before, queries, block, weights, send, keep, kl,
    own, teacher, scores, total, in_sem,
):
    own_copy = pltpu.make_async_copy(block.at[:, pl.ds(0, width)], own, in_sem.at[0])
    teacher_copy = pltpu.make_async_copy(
        block.at[:, pl.ds(width, passages_all)], teacher, in_sem.at[1]
    )
    own_copy.start()
    teacher_copy.start()
    own_copy.wait()

    def score_only(quarter, carry):
        score_quarter(own, 0, quarter, passages, scores)
        return carry

    lax.fori_loop(0, 4, score_only, 0)
    teacher_copy.wait()
    contract = (((0,), (0,)), ((), ()))

    def together(quarter, carry):
        row_pass(quarter, scores, teacher, weights, kl)
        columns = pl.ds(pl.multiple_of(quarter * 512, 512), 512)
        total[columns, :] = lax.dot_general(
            before[:, columns],
            queries[...],
            contract,
            preferred_element_type=jnp.float32,
        )
        return carry

    lax.fori_loop(0, 4, together, 0)
    even = core[0] == 0

    def reduce(j, carry):
        columns = pl.ds(pl.multiple_of(j * 256, 256), 256)
        grad = lax.dot_general(
            weights[:, columns],
            own[...],
            contract,
            preferred_element_type=jnp.float32,
        )
        grad = (grad + total[columns, :]).astype(jnp.bfloat16)
        for part in range(2):
            upper = grad[part * 128 : part * 128 + 64]
            lower = grad[part * 128 + 64 : part * 128 + 128]
            rows = pl.ds(pl.multiple_of(j * 128 + part * 64, 64), 64)
            keep[rows, :] = jnp.where(even, upper, lower)
            send[rows, :] = jnp.where(even, lower, upper)
        return carry

    lax.fori_loop(0, passages_all // 256, reduce, 0)


def last_block(core, passages, weights, queries, block):
    half = (vmem, (passages_all // 2, width), jnp.bfloat16)
    return call(
        last_kernel,
        "last_block",
        [smem] + [vmem] * 3 + [hbm],
        [
            (vmem, (per_language, passages_all), jnp.bfloat16),
            half,
            half,
            (vmem, (per_language, 128), jnp.float32),
        ],
        [
            pltpu.VMEM((per_language, width), jnp.bfloat16),
            pltpu.VMEM((per_language, passages_all), jnp.bfloat16),
            pltpu.VMEM((per_language, passages_all), jnp.float32),
            pltpu.VMEM((passages_all, width), jnp.float32),
            pltpu.SemaphoreType.DMA((2,)),
        ],
        20,
        6 * 1024**3,
        mib,
    )(core, passages, weights, queries, block)


def query_kernel(places, passages, *refs):
    for number, place in enumerate(places):
        weights, kl = refs[2 * number], refs[2 * number + 1]
        out = refs[2 * len(places) + number]
        rows = pl.ds(place * per_language, per_language)

        def step(half, carry, rows=rows, weights=weights, out=out):
            columns = pl.ds(pl.multiple_of(half * 512, 512), 512)
            grad_columns(rows, columns, weights, passages, out)
            return carry

        lax.fori_loop(0, 2, step, 0)
        out[:, pl.ds(width, extra)] = kl_parts(kl[rows, :])


def query_grads(places, passages, *arrays):
    return call(
        functools.partial(query_kernel, places),
        "query_grads",
        [vmem] * (1 + len(arrays)),
        [(vmem, (per_language, width + extra), jnp.bfloat16)] * len(places),
        [],
        8,
        len(places) * 1024**3,
    )(passages, *arrays)


def pair_kernel(keep, other, out):
    def step(i, carry):
        rows = pl.ds(pl.multiple_of(i * 64, 64), 64)
        out[rows, :] = (
            keep[rows, :].astype(jnp.float32) + other[rows, :].astype(jnp.float32)
        ).astype(jnp.bfloat16)
        return carry

    lax.fori_loop(0, passages_all // 128, step, 0)


def pair_sum(keep, other):
    return call(
        pair_kernel, "pair_sum", [vmem] * 2, [(vmem, keep.shape, jnp.bfloat16)], [], 8, mib
    )(keep, other)[0]


def selection(slot, numbers, select):
    rows = lax.broadcasted_iota(jnp.int32, (per_language, per_device), 0)
    for half, number in enumerate(numbers):
        hit = rows + number * per_language == slot[0:1, :]
        select[half * per_language : (half + 1) * per_language, :] = hit.astype(
            jnp.float32
        ).astype(jnp.bfloat16)


def joined(select, blocks, columns):
    part = None
    for half, block in enumerate(blocks):
        term = lax.dot_general(
            select[half * per_language : (half + 1) * per_language, :],
            block[:, columns],
            (((0,), (0,)), ((), ())),
            preferred_element_type=jnp.float32,
        )
        part = term if part is None else part + term
    return part


def restore_first_kernel(slot, in0, in1, out, select):
    selection(slot, (0, 1), select)

    def step(j, carry):
        columns = pl.ds(pl.multiple_of(j * 256, 256), 256)
        out[:, columns] = joined(select, (in0, in1), columns).astype(jnp.bfloat16)
        return carry

    lax.fori_loop(0, width // 256, step, 0)
    columns = pl.ds(width, extra)
    out[:, columns] = joined(select, (in0, in1), columns).astype(jnp.bfloat16)


def restore_last_kernel(slot, begun, in2, in3, grads_out, kl, select, grads, out_sem):
    selection(slot, (2, 3), select)

    def written(j):
        columns = pl.ds(pl.multiple_of(j * 256, 256), 256)
        return pltpu.make_async_copy(grads.at[j], grads_out.at[:, columns], out_sem.at[j])

    def step(j, carry):
        columns = pl.ds(pl.multiple_of(j * 256, 256), 256)
        added = joined(select, (in2, in3), columns) + begun[:, columns].astype(jnp.float32)
        grads[j] = added.astype(jnp.bfloat16)
        written(j).start()
        return carry

    lax.fori_loop(0, width // 256, step, 0)
    columns = pl.ds(width, extra)
    parts = joined(select, (in2, in3), columns) + begun[:, columns].astype(jnp.float32)
    column = jnp.sum(parts, axis=1, keepdims=True)
    kl[...] = jnp.transpose(jnp.broadcast_to(column, (per_device, 128)))[:1]
    for j in range(width // 256):
        written(j).wait()


def restore_first(slot, blocks):
    return call(
        restore_first_kernel,
        "restore_first",
        [vmem] * 3,
        [(vmem, (per_device, width + extra), jnp.bfloat16)],
        [pltpu.VMEM((2 * per_language, per_device), jnp.bfloat16)],
        16,
        15 * 1024**3,
    )(slot, *blocks)[0]


def restore_last(slot, begun, blocks):
    return call(
        restore_last_kernel,
        "restore_last",
        [vmem] * 4,
        [
            (hbm, (per_device, width), jnp.bfloat16),
            (vmem, (1, per_device), jnp.float32),
        ],
        [
            pltpu.VMEM((2 * per_language, per_device), jnp.bfloat16),
            pltpu.VMEM((width // 256, per_device, 256), jnp.bfloat16),
            pltpu.SemaphoreType.DMA((width // 256,)),
        ],
        24,
        1024**3,
    )(slot, begun, *blocks)


def sum_kernel(pieces, out, held, sems):
    copies = [
        pltpu.make_async_copy(pieces.at[pl.ds(4 * i, 4)], held.at[pl.ds(4 * i, 4)], sems.at[i])
        for i in range(4)
    ]
    for copy in copies:
        copy.start()
    total = jnp.zeros((64, width), jnp.float32)
    for i, copy in enumerate(copies):
        copy.wait()
        for j in range(4):
            total = total + held[4 * i + j].astype(jnp.float32)
    out[...] = total.astype(jnp.bfloat16)


def sum_pieces(pieces):
    return call(
        sum_kernel,
        "sum_pieces",
        [hbm],
        [(vmem, (64, width), jnp.bfloat16)],
        [pltpu.VMEM(pieces.shape, jnp.bfloat16), pltpu.SemaphoreType.DMA((4,))],
        8,
        mib,
    )(pieces)[0]


def shift(array, by):
    pairs = [(i, (i + by) % languages) for i in range(languages)]
    return lax.ppermute(array, "x", pairs)


def on_device(queries, bucket_ids, raw_passages, counts, teacher):
    group = ("y", "z", "c")
    here = lax.axis_index("x").astype(jnp.int32).reshape(1)
    core = lax.axis_index("c").astype(jnp.int32).reshape(1)
    all_raw = lax.all_gather(raw_passages[0], group, axis=0, tiled=True)
    ids = bucket_ids[0]
    out1, out3, slot = sort_rows(here, ids, None, queries[0, 0], teacher[0, 0])
    in1, in3 = shift(out1, 1), shift(out3, 3)
    out2, in0, _ = sort_rows(here, ids, slot, queries[0, 0], teacher[0, 0])
    held_counts, in0, out2 = lax.optimization_barrier((counts, in0, out2))
    holder_counts = lax.all_gather(held_counts[0], group, axis=0, tiled=True)
    chunk_list = chunks_of(holder_counts)
    out2, in1, in3, chunk_list = lax.optimization_barrier((out2, in1, in3, chunk_list))
    in2 = shift(out2, 2)
    store, moved = teacher_rows((in0, in1, in3))
    all_raw, store, moved = lax.optimization_barrier((all_raw, store, moved))
    weights, passages, kl, back1 = first_blocks(chunk_list, all_raw, store)
    last_weights, send, keep, last_kl = last_block(core, passages, weights, moved, in2)
    other = lax.ppermute(send, "c", [(0, 1), (1, 0)])
    back3, back2 = query_grads((2, 0), passages, weights, kl, last_weights, last_kl)
    keep, back3, back2 = lax.optimization_barrier((keep, back3, back2))
    home1, home3, home2 = shift(back1, -1), shift(back3, -3), shift(back2, -2)
    paired = pair_sum(keep, other)
    spread = lax.all_to_all(
        paired.reshape(16, 64, width), ("y", "z"), split_axis=0, concat_axis=0, tiled=True
    )
    paired, weights = lax.optimization_barrier((paired, weights))
    (back0,) = query_grads((0,), passages, weights, kl)
    grad_passages = sum_pieces(spread)
    begun = restore_first(slot, (back0, home1))
    grad_queries, kl_rows = restore_last(slot, begun, (home2, home3))
    return (grad_queries[None, None], grad_passages[None], kl_rows[None])


def solution(mesh):
    split = Mesh(mesh.devices.reshape(4, 4, 4, 2), ("x", "y", "z", "c"))
    group = ("y", "z", "c")
    in_specs = (
        P("x", group, None, None),
        P("x", group, None),
        P("x", group, None, None),
        P("x", group),
        P("x", group, None, None),
    )
    out_specs = (P("x", group, None, None), P("x", group, None), P("x", group, None))
    return jax.shard_map(
        on_device, mesh=split, in_specs=in_specs, out_specs=out_specs, check_vma=False
    )
```

```python
import functools

import jax
import jax.numpy as jnp
from jax import lax
from jax.experimental import pallas as pl
from jax.experimental.pallas import tpu as pltpu
from jax.sharding import Mesh
from jax.sharding import PartitionSpec as P

student_scale = 0.1
languages = 4
holders = 32
capacity = 192
width = 1024
per_device = 1024
per_language = 256
passages_all = 2048
both = width + passages_all
group_chunks = 8
group_rows = 256
window = 272
extra = 128
chunk_rows = 32
chunk_count = 96
store_rows = 6144
mib = 1024 * 1024


def slots_of(ids, here):
    turned = lax.rem(ids - here + languages, languages)
    kinds = lax.broadcasted_iota(jnp.int32, (8, per_device), 0)
    hot = (turned == kinds).astype(jnp.float32)
    parts = per_device // 128
    stacked = jnp.concatenate([hot[:, i * 128 : (i + 1) * 128] for i in range(parts)], axis=0)
    earlier = lax.broadcasted_iota(jnp.int32, (128, 128), 0)
    later = lax.broadcasted_iota(jnp.int32, (128, 128), 1)
    upper = (earlier <= later).astype(jnp.float32).astype(jnp.bfloat16)
    sums = jnp.dot(stacked.astype(jnp.bfloat16), upper, preferred_element_type=jnp.float32)
    before = jnp.zeros((8, 1), jnp.float32)
    ranks = []
    for i in range(parts):
        segment = sums[i * 8 : (i + 1) * 8]
        ranks.append(segment + before)
        before = before + segment[:, 127:128]
    place = jnp.concatenate(ranks, axis=1) - 1.0 + kinds.astype(jnp.float32) * per_language
    return jnp.sum(hot * place, axis=0, keepdims=True).astype(jnp.int32)


vmem = pl.BlockSpec(memory_space=pltpu.VMEM)
smem = pl.BlockSpec(memory_space=pltpu.SMEM)
hbm = pl.BlockSpec(memory_space=pltpu.HBM)


def call(kernel, name, in_specs, outs, scratch, limit, flops, transcendentals=0):
    return pl.pallas_call(
        kernel,
        in_specs=in_specs,
        out_specs=[spec for spec, _, _ in outs],
        out_shape=[jax.ShapeDtypeStruct(shape, dtype) for _, shape, dtype in outs],
        scratch_shapes=scratch,
        compiler_params=pltpu.CompilerParams(vmem_limit_bytes=limit * mib),
        cost_estimate=pl.CostEstimate(
            flops=flops, bytes_accessed=8 * mib, transcendentals=transcendentals
        ),
        name=name,
    )


def sort_kernel(
    first, here, ids, slot_in, queries, teacher, out_a, out_b, slot,
    select, block, moved_a, moved_b, in_sem, out_sem,
):
    tile = 512
    tiles = both // tile

    def read(j):
        source = queries if j < width // tile else teacher
        column = j * tile if j < width // tile else j * tile - width
        return pltpu.make_async_copy(
            source.at[:, pl.ds(column, tile)], block.at[j], in_sem.at[j]
        )

    def written(j):
        columns = pl.ds(j * tile, tile)
        return [
            pltpu.make_async_copy(moved_a.at[j], out_a.at[:, columns], out_sem.at[2 * j]),
            pltpu.make_async_copy(moved_b.at[j], out_b.at[:, columns], out_sem.at[2 * j + 1]),
        ]

    for j in range(tiles):
        read(j).start()
    if first:
        slots = slots_of(ids[...], here[0])
        slot[...] = jnp.broadcast_to(slots, (8, per_device))
    else:
        slots = slot_in[0:1, :]
        slot[...] = jnp.zeros((8, 128), jnp.int32)
    rows = lax.broadcasted_iota(jnp.int32, (per_language, per_device), 0)
    for half, number in enumerate((1, 3) if first else (2, 0)):
        hit = rows + number * per_language == slots
        select[pl.ds(half * per_language, per_language), :] = hit.astype(jnp.float32).astype(
            jnp.bfloat16
        )
    for j in range(tiles):
        read(j).wait()
        moved = jnp.dot(select[...], block[j], preferred_element_type=jnp.float32)
        moved_a[j] = moved[:per_language].astype(jnp.bfloat16)
        moved_b[j] = moved[per_language:].astype(jnp.bfloat16)
        for copy in written(j):
            copy.start()
    for j in range(tiles):
        for copy in written(j):
            copy.wait()


def sort_rows(here, ids, slot, queries, teacher):
    first = slot is None
    tiles = both // 512
    moved = pltpu.VMEM((tiles, per_language, 512), jnp.bfloat16)
    out = (hbm, (per_language, both), jnp.bfloat16)
    return call(
        functools.partial(sort_kernel, first),
        "sort_first" if first else "sort_rest",
        [smem, vmem, vmem, hbm, hbm],
        [out, out, (vmem, (8, per_device) if first else (8, 128), jnp.int32)],
        [
            pltpu.VMEM((2 * per_language, per_device), jnp.bfloat16),
            pltpu.VMEM((tiles, per_device, 512), jnp.bfloat16),
            moved,
            moved,
            pltpu.SemaphoreType.DMA((tiles,)),
            pltpu.SemaphoreType.DMA((2 * tiles,)),
        ],
        60 if first else 28,
        4 * per_language * per_device * both,
    )(here, ids, ids if first else slot, queries, teacher)


def kl_parts(value):
    high = value.astype(jnp.bfloat16).astype(jnp.float32)
    middle = (value - high).astype(jnp.bfloat16).astype(jnp.float32)
    low = value - high - middle
    lane = lax.broadcasted_iota(jnp.int32, value.shape, 1)
    parts = jnp.where(
        lane == 0, high, jnp.where(lane == 1, middle, jnp.where(lane == 2, low, 0.0))
    )
    return parts.astype(jnp.bfloat16)


def row_pass(quarter, scores, block, weights, kl):
    for i in range(4):
        local = pl.ds(pl.multiple_of(quarter * 64 + i * 16, 16), 16)
        own = scores[local, :]
        taught = block[local, :].astype(jnp.float32)
        top = jnp.max(own, axis=1, keepdims=True)
        taught_top = jnp.max(taught, axis=1, keepdims=True)
        grown = jnp.exp(own - top)
        total = jnp.sum(grown, axis=1, keepdims=True)
        shifted = taught - taught_top
        taught_grown = jnp.exp(shifted)
        taught_total = jnp.sum(taught_grown, axis=1, keepdims=True)
        cross = jnp.sum(taught_grown * (shifted - (own - top)), axis=1, keepdims=True)
        diverge = cross / taught_total - jnp.log(taught_total) + jnp.log(total)
        weights[local, :] = (
            grown * (student_scale / total) - taught_grown * (student_scale / taught_total)
        ).astype(jnp.bfloat16)
        kl[local, :] = jnp.broadcast_to(diverge, (16, 128))


def score_quarter(queries, base, quarter, passages, scores):
    columns = pl.ds(pl.multiple_of(quarter * 512, 512), 512)
    scores[:, columns] = (
        lax.dot_general(
            queries[pl.ds(base, per_language), pl.ds(0, width)],
            passages[columns, :],
            (((1,), (1,)), ((), ())),
            preferred_element_type=jnp.float32,
        )
        * student_scale
    )


def teacher_kernel(in0, in1, in2, store, queries, taught_out, parts, sems):
    rows = 3 * per_language

    def saved(number):
        block = pl.ds(number * per_language, per_language)
        behind = pl.ds(rows + number * per_language, per_language)
        return [
            pltpu.make_async_copy(taught_out.at[block], store.at[block], sems.at[number]),
            pltpu.make_async_copy(
                queries.at[block], store.at[behind, pl.ds(0, width)], sems.at[3 + number]
            ),
            pltpu.make_async_copy(
                parts.at[block], store.at[behind, pl.ds(width, extra)], sems.at[6 + number]
            ),
        ]

    for number, block in enumerate((in0, in1, in2)):

        def rows_of(i, carry, number=number, block=block):
            for part in range(4):
                local = pl.ds(pl.multiple_of(i * 64 + part * 16, 16), 16)
                placed = pl.ds(
                    pl.multiple_of(number * per_language + i * 64 + part * 16, 16), 16
                )
                queries[placed, :] = block[local, pl.ds(0, width)]
                taught = block[local, pl.ds(width, passages_all)].astype(jnp.float32)
                shifted = taught - jnp.max(taught, axis=1, keepdims=True)
                grown = jnp.exp(shifted)
                total = jnp.sum(grown, axis=1, keepdims=True)
                cross = jnp.sum(grown * shifted, axis=1, keepdims=True)
                taught_out[placed, :] = (grown * (student_scale / total)).astype(jnp.bfloat16)
                entropy = jnp.broadcast_to(cross / total - jnp.log(total), (16, 128))
                parts[placed, :] = kl_parts(entropy)
            return carry

        lax.fori_loop(0, 4, rows_of, 0)
        for copy in saved(number):
            copy.start()
    for number in range(3):
        for copy in saved(number):
            copy.wait()


def teacher_rows(blocks):
    rows = 3 * per_language
    return call(
        teacher_kernel,
        "teacher_rows",
        [vmem] * 3,
        [
            (hbm, (store_rows, passages_all), jnp.bfloat16),
            (vmem, (rows, width), jnp.bfloat16),
        ],
        [
            pltpu.VMEM((rows, passages_all), jnp.bfloat16),
            pltpu.VMEM((rows, extra), jnp.bfloat16),
            pltpu.SemaphoreType.DMA((9,)),
        ],
        40,
        mib,
        2 * mib,
    )(*blocks)


def student_pass(base, quarter, scores, taught_ref, parts, weights, kl):
    for i in range(4):
        local = pl.ds(pl.multiple_of(quarter * 64 + i * 16, 16), 16)
        placed = pl.ds(pl.multiple_of(base + quarter * 64 + i * 16, 16), 16)
        own = scores[local, :]
        taught = taught_ref[placed, :].astype(jnp.float32)
        shifted = own - jnp.max(own, axis=1, keepdims=True)
        grown = jnp.exp(shifted)
        total = jnp.sum(grown, axis=1, keepdims=True)
        cross = jnp.sum(taught * shifted, axis=1, keepdims=True)
        entropy = jnp.sum(
            parts[placed, pl.ds(width, extra)].astype(jnp.float32), axis=1, keepdims=True
        )
        diverge = entropy + jnp.log(total) - cross * (1.0 / student_scale)
        weights[placed, :] = (grown * (student_scale / total) - taught).astype(jnp.bfloat16)
        kl[placed, :] = jnp.broadcast_to(diverge, (16, 128))


def grad_columns(rows, columns, weights, passages, out):
    out[:, columns] = jnp.dot(
        weights[rows, :],
        passages[pl.ds(0, passages_all), columns],
        preferred_element_type=jnp.float32,
    ).astype(jnp.bfloat16)


def first_kernel(
    chunk_list, target_of, raw, store,
    weights, passages, kl, grad, raw_v, queries, taught, scores, other_scores, raw_sem, in_sem,
):
    def raw_copy(k):
        rows = pl.ds(pl.multiple_of(chunk_list[chunk_count + k], chunk_rows), chunk_rows)
        return pltpu.make_async_copy(raw.at[chunk_list[k], rows], raw_v.at[k], raw_sem.at[k])

    groups = chunk_list[3 * chunk_count]

    def start_group(g, carry):
        for c in range(group_chunks):
            raw_copy(g * group_chunks + c).start()
        return carry

    lax.fori_loop(0, groups, start_group, 0)
    copies = [
        pltpu.make_async_copy(
            store.at[pl.ds(3 * per_language, 3 * per_language), pl.ds(0, width + extra)],
            queries,
            in_sem.at[0],
        ),
        pltpu.make_async_copy(store.at[pl.ds(0, 3 * per_language)], taught, in_sem.at[1]),
    ]
    for copy in copies:
        copy.start()
    passages[pl.ds(0, 16), :] = jnp.zeros((16, width), jnp.bfloat16)

    def place(g, carry):
        for c in range(group_chunks):
            raw_copy(g * group_chunks + c).wait()
        start = pl.multiple_of((chunk_list[2 * chunk_count + g * group_chunks] // 16) * 16, 16)
        target = lax.broadcasted_iota(jnp.int32, (window, group_rows), 0)
        hit = target == target_of[pl.ds(g, 1), :] - start
        chosen = hit.astype(jnp.float32).astype(jnp.bfloat16)
        chunks = raw_v[pl.ds(g * group_chunks, group_chunks)].reshape(group_rows, width)
        moved = jnp.dot(chosen, chunks, preferred_element_type=jnp.float32).astype(jnp.bfloat16)
        head = passages[pl.ds(start, 16), :]
        passages[pl.ds(start, 16), :] = head + moved[:16]
        passages[pl.ds(start + 16, window - 16), :] = moved[16:]
        return carry

    lax.fori_loop(0, groups, place, 0)
    for copy in copies:
        copy.wait()

    def score_only(quarter, carry):
        score_quarter(queries, 0, quarter, passages, scores)
        return carry

    lax.fori_loop(0, 4, score_only, 0)
    held, free = scores, other_scores
    middle = pl.ds(per_language, per_language)
    for number in range(3):
        base = number * per_language

        def together(quarter, carry, base=base, held=held, free=free, last=number == 2):
            if last:
                columns = pl.ds(pl.multiple_of(quarter * 256, 256), 256)
                grad_columns(middle, columns, weights, passages, grad)
            else:
                score_quarter(queries, base + per_language, quarter, passages, free)
            student_pass(base, quarter, held, taught, queries, weights, kl)
            return carry

        lax.fori_loop(0, 4, together, 0)
        held, free = free, held
    grad[:, pl.ds(width, extra)] = kl_parts(kl[middle, :])


def first_blocks(chunk_list, raw, store):
    rows = 3 * per_language
    scores = pltpu.VMEM((per_language, passages_all), jnp.float32)
    return call(
        first_kernel,
        "first_blocks",
        [smem, vmem, hbm, hbm],
        [
            (vmem, (rows, passages_all), jnp.bfloat16),
            (vmem, (passages_all + window, width), jnp.bfloat16),
            (vmem, (rows, 128), jnp.float32),
            (vmem, (per_language, width + extra), jnp.bfloat16),
        ],
        [
            pltpu.VMEM((chunk_count, chunk_rows, width), jnp.bfloat16),
            pltpu.VMEM((rows, width + extra), jnp.bfloat16),
            pltpu.VMEM((rows, passages_all), jnp.bfloat16),
            scores,
            scores,
            pltpu.SemaphoreType.DMA((chunk_count,)),
            pltpu.SemaphoreType.DMA((2,)),
        ],
        40,
        6 * 1024**3,
        2 * mib,
    )(*chunk_list, raw, store)


def chunks_of(counts):
    number = (counts + chunk_rows - 1) // chunk_rows
    upto = jnp.arange(holders)[None, :] < jnp.arange(holders)[:, None]
    offsets = jnp.sum(jnp.where(upto, counts[None, :], 0), axis=1)
    firsts = jnp.sum(jnp.where(upto, number[None, :], 0), axis=1)
    index = jnp.arange(chunk_count)[:, None]
    mine = (index >= firsts[None, :]) & (index < (firsts + number)[None, :])
    row = (index - firsts[None, :]) * chunk_rows

    def pick(values):
        return jnp.sum(jnp.where(mine, values, 0), axis=1)

    holder = pick(jnp.arange(holders)[None, :] + 0 * row)
    used = pick(jnp.minimum(counts[None, :] - row, chunk_rows))
    place = jnp.where(used > 0, pick(offsets[None, :] + row), passages_all)
    slots = jnp.arange(chunk_rows)[None, :]
    groups = (jnp.sum(number) + group_chunks - 1) // group_chunks
    targets = jnp.where(slots < used[:, None], place[:, None] + slots, -1)
    return (
        jnp.concatenate([holder, pick(row), place, groups[None]]).astype(jnp.int32),
        targets.astype(jnp.int32).reshape(chunk_count // group_chunks, group_rows),
    )


def last_kernel(
    core, passages, before, queries, block, weights, send, keep, kl,
    own, teacher, scores, total, in_sem,
):
    own_copy = pltpu.make_async_copy(block.at[:, pl.ds(0, width)], own, in_sem.at[0])
    teacher_copy = pltpu.make_async_copy(
        block.at[:, pl.ds(width, passages_all)], teacher, in_sem.at[1]
    )
    own_copy.start()
    teacher_copy.start()
    own_copy.wait()

    def score_only(quarter, carry):
        score_quarter(own, 0, quarter, passages, scores)
        return carry

    lax.fori_loop(0, 4, score_only, 0)
    teacher_copy.wait()
    contract = (((0,), (0,)), ((), ()))

    def together(quarter, carry):
        row_pass(quarter, scores, teacher, weights, kl)
        columns = pl.ds(pl.multiple_of(quarter * 512, 512), 512)
        total[columns, :] = lax.dot_general(
            before[:, columns],
            queries[...],
            contract,
            preferred_element_type=jnp.float32,
        )
        return carry

    lax.fori_loop(0, 4, together, 0)
    even = core[0] == 0

    def reduce(j, carry):
        columns = pl.ds(pl.multiple_of(j * 256, 256), 256)
        grad = lax.dot_general(
            weights[:, columns],
            own[...],
            contract,
            preferred_element_type=jnp.float32,
        )
        grad = (grad + total[columns, :]).astype(jnp.bfloat16)
        for part in range(2):
            upper = grad[part * 128 : part * 128 + 64]
            lower = grad[part * 128 + 64 : part * 128 + 128]
            rows = pl.ds(pl.multiple_of(j * 128 + part * 64, 64), 64)
            keep[rows, :] = jnp.where(even, upper, lower)
            send[rows, :] = jnp.where(even, lower, upper)
        return carry

    lax.fori_loop(0, passages_all // 256, reduce, 0)


def last_block(core, passages, weights, queries, block):
    half = (vmem, (passages_all // 2, width), jnp.bfloat16)
    return call(
        last_kernel,
        "last_block",
        [smem] + [vmem] * 3 + [hbm],
        [
            (vmem, (per_language, passages_all), jnp.bfloat16),
            half,
            half,
            (vmem, (per_language, 128), jnp.float32),
        ],
        [
            pltpu.VMEM((per_language, width), jnp.bfloat16),
            pltpu.VMEM((per_language, passages_all), jnp.bfloat16),
            pltpu.VMEM((per_language, passages_all), jnp.float32),
            pltpu.VMEM((passages_all, width), jnp.float32),
            pltpu.SemaphoreType.DMA((2,)),
        ],
        20,
        6 * 1024**3,
        mib,
    )(core, passages, weights, queries, block)


def query_kernel(places, passages, *refs):
    for number, place in enumerate(places):
        weights, kl = refs[2 * number], refs[2 * number + 1]
        out = refs[2 * len(places) + number]
        rows = pl.ds(place * per_language, per_language)

        def step(half, carry, rows=rows, weights=weights, out=out):
            columns = pl.ds(pl.multiple_of(half * 512, 512), 512)
            grad_columns(rows, columns, weights, passages, out)
            return carry

        lax.fori_loop(0, 2, step, 0)
        out[:, pl.ds(width, extra)] = kl_parts(kl[rows, :])


def query_grads(places, passages, *arrays):
    return call(
        functools.partial(query_kernel, places),
        "query_grads",
        [vmem] * (1 + len(arrays)),
        [(vmem, (per_language, width + extra), jnp.bfloat16)] * len(places),
        [],
        8,
        len(places) * 1024**3,
    )(passages, *arrays)


def pair_kernel(keep, other, out):
    def step(i, carry):
        rows = pl.ds(pl.multiple_of(i * 64, 64), 64)
        out[rows, :] = (
            keep[rows, :].astype(jnp.float32) + other[rows, :].astype(jnp.float32)
        ).astype(jnp.bfloat16)
        return carry

    lax.fori_loop(0, passages_all // 128, step, 0)


def pair_sum(keep, other):
    return call(
        pair_kernel, "pair_sum", [vmem] * 2, [(vmem, keep.shape, jnp.bfloat16)], [], 8, mib
    )(keep, other)[0]


def selection(slot, numbers, select):
    rows = lax.broadcasted_iota(jnp.int32, (per_language, per_device), 0)
    for half, number in enumerate(numbers):
        hit = rows + number * per_language == slot[0:1, :]
        select[half * per_language : (half + 1) * per_language, :] = hit.astype(
            jnp.float32
        ).astype(jnp.bfloat16)


def joined(select, blocks, columns):
    part = None
    for half, block in enumerate(blocks):
        term = lax.dot_general(
            select[half * per_language : (half + 1) * per_language, :],
            block[:, columns],
            (((0,), (0,)), ((), ())),
            preferred_element_type=jnp.float32,
        )
        part = term if part is None else part + term
    return part


def restore_first_kernel(slot, in0, in1, in3, out, select):
    selection(slot, (0, 1, 3), select)
    blocks = (in0, in1, in3)

    def step(j, carry):
        columns = pl.ds(pl.multiple_of(j * 256, 256), 256)
        out[:, columns] = joined(select, blocks, columns).astype(jnp.bfloat16)
        return carry

    lax.fori_loop(0, width // 256, step, 0)
    columns = pl.ds(width, extra)
    out[:, columns] = joined(select, blocks, columns).astype(jnp.bfloat16)


def restore_last_kernel(slot, begun, in2, grads_out, kl, select, grads, out_sem):
    selection(slot, (2,), select)

    def written(j):
        columns = pl.ds(pl.multiple_of(j * 256, 256), 256)
        return pltpu.make_async_copy(grads.at[j], grads_out.at[:, columns], out_sem.at[j])

    def step(j, carry):
        columns = pl.ds(pl.multiple_of(j * 256, 256), 256)
        added = joined(select, (in2,), columns) + begun[:, columns].astype(jnp.float32)
        grads[j] = added.astype(jnp.bfloat16)
        written(j).start()
        return carry

    lax.fori_loop(0, width // 256, step, 0)
    columns = pl.ds(width, extra)
    parts = joined(select, (in2,), columns) + begun[:, columns].astype(jnp.float32)
    column = jnp.sum(parts, axis=1, keepdims=True)
    kl[...] = jnp.transpose(jnp.broadcast_to(column, (per_device, 128)))[:1]
    for j in range(width // 256):
        written(j).wait()


def restore_first(slot, blocks):
    return call(
        restore_first_kernel,
        "restore_first",
        [vmem] * 4,
        [(vmem, (per_device, width + extra), jnp.bfloat16)],
        [pltpu.VMEM((3 * per_language, per_device), jnp.bfloat16)],
        12,
        15 * 1024**3,
    )(slot, *blocks)[0]


def restore_last(slot, begun, block):
    return call(
        restore_last_kernel,
        "restore_last",
        [vmem] * 3,
        [
            (hbm, (per_device, width), jnp.bfloat16),
            (vmem, (1, per_device), jnp.float32),
        ],
        [
            pltpu.VMEM((per_language, per_device), jnp.bfloat16),
            pltpu.VMEM((width // 256, per_device, 256), jnp.bfloat16),
            pltpu.SemaphoreType.DMA((width // 256,)),
        ],
        12,
        1024**3,
    )(slot, begun, block)


def sum_kernel(pieces, out, held, sems):
    copies = [
        pltpu.make_async_copy(pieces.at[pl.ds(4 * i, 4)], held.at[pl.ds(4 * i, 4)], sems.at[i])
        for i in range(4)
    ]
    for copy in copies:
        copy.start()
    total = jnp.zeros((64, width), jnp.float32)
    for i, copy in enumerate(copies):
        copy.wait()
        for j in range(4):
            total = total + held[4 * i + j].astype(jnp.float32)
    out[...] = total.astype(jnp.bfloat16)


def sum_pieces(pieces):
    return call(
        sum_kernel,
        "sum_pieces",
        [hbm],
        [(vmem, (64, width), jnp.bfloat16)],
        [pltpu.VMEM(pieces.shape, jnp.bfloat16), pltpu.SemaphoreType.DMA((4,))],
        8,
        mib,
    )(pieces)[0]


def shift(array, by):
    pairs = [(i, (i + by) % languages) for i in range(languages)]
    return lax.ppermute(array, "x", pairs)


def on_device(queries, bucket_ids, raw_passages, counts, teacher):
    group = ("y", "z", "c")
    here = lax.axis_index("x").astype(jnp.int32).reshape(1)
    core = lax.axis_index("c").astype(jnp.int32).reshape(1)
    all_raw = lax.all_gather(raw_passages[0], group, axis=0, tiled=True)
    ids = bucket_ids[0]
    out1, out3, slot = sort_rows(here, ids, None, queries[0, 0], teacher[0, 0])
    in1, in3 = shift(out1, 1), shift(out3, 3)
    out2, in0, _ = sort_rows(here, ids, slot, queries[0, 0], teacher[0, 0])
    held_counts, in0, out2 = lax.optimization_barrier((counts, in0, out2))
    holder_counts = lax.all_gather(held_counts[0], group, axis=0, tiled=True)
    chunk_list = chunks_of(holder_counts)
    out2, in1, in3, chunk_list = lax.optimization_barrier((out2, in1, in3, chunk_list))
    in2 = shift(out2, 2)
    store, moved = teacher_rows((in0, in1, in3))
    all_raw, store, moved = lax.optimization_barrier((all_raw, store, moved))
    weights, passages, kl, back1 = first_blocks(chunk_list, all_raw, store)
    last_weights, send, keep, last_kl = last_block(core, passages, weights, moved, in2)
    other = lax.ppermute(send, "c", [(0, 1), (1, 0)])
    back3, back2 = query_grads((2, 0), passages, weights, kl, last_weights, last_kl)
    keep, back3, back2 = lax.optimization_barrier((keep, back3, back2))
    home1, home3, home2 = shift(back1, -1), shift(back3, -3), shift(back2, -2)
    paired = pair_sum(keep, other)
    spread = lax.all_to_all(
        paired.reshape(16, 64, width), ("y", "z"), split_axis=0, concat_axis=0, tiled=True
    )
    paired, weights = lax.optimization_barrier((paired, weights))
    (back0,) = query_grads((0,), passages, weights, kl)
    grad_passages = sum_pieces(spread)
    begun = restore_first(slot, (back0, home1, home3))
    grad_queries, kl_rows = restore_last(slot, begun, home2)
    return (grad_queries[None, None], grad_passages[None], kl_rows[None])


def solution(mesh):
    split = Mesh(mesh.devices.reshape(4, 4, 4, 2), ("x", "y", "z", "c"))
    group = ("y", "z", "c")
    in_specs = (
        P("x", group, None, None),
        P("x", group, None),
        P("x", group, None, None),
        P("x", group),
        P("x", group, None, None),
    )
    out_specs = (P("x", group, None, None), P("x", group, None), P("x", group, None))
    return jax.shard_map(
        on_device, mesh=split, in_specs=in_specs, out_specs=out_specs, check_vma=False
    )
```

```python
import functools

import jax
import jax.numpy as jnp
from jax import lax
from jax.experimental import pallas as pl
from jax.experimental.pallas import tpu as pltpu
from jax.sharding import Mesh
from jax.sharding import PartitionSpec as P

student_scale = 0.1
languages = 4
holders = 32
capacity = 192
width = 1024
per_device = 1024
per_language = 256
passages_all = 2048
both = width + passages_all
group_chunks = 8
group_rows = 256
window = 272
extra = 128
chunk_rows = 32
chunk_count = 96
store_rows = 6144
mib = 1024 * 1024


def slots_of(ids, here):
    turned = lax.rem(ids - here + languages, languages)
    kinds = lax.broadcasted_iota(jnp.int32, (8, per_device), 0)
    hot = (turned == kinds).astype(jnp.float32)
    parts = per_device // 128
    stacked = jnp.concatenate([hot[:, i * 128 : (i + 1) * 128] for i in range(parts)], axis=0)
    earlier = lax.broadcasted_iota(jnp.int32, (128, 128), 0)
    later = lax.broadcasted_iota(jnp.int32, (128, 128), 1)
    upper = (earlier <= later).astype(jnp.float32).astype(jnp.bfloat16)
    sums = jnp.dot(stacked.astype(jnp.bfloat16), upper, preferred_element_type=jnp.float32)
    before = jnp.zeros((8, 1), jnp.float32)
    ranks = []
    for i in range(parts):
        segment = sums[i * 8 : (i + 1) * 8]
        ranks.append(segment + before)
        before = before + segment[:, 127:128]
    place = jnp.concatenate(ranks, axis=1) - 1.0 + kinds.astype(jnp.float32) * per_language
    return jnp.sum(hot * place, axis=0, keepdims=True).astype(jnp.int32)


vmem = pl.BlockSpec(memory_space=pltpu.VMEM)
smem = pl.BlockSpec(memory_space=pltpu.SMEM)
hbm = pl.BlockSpec(memory_space=pltpu.HBM)


def call(kernel, name, in_specs, outs, scratch, limit, flops, transcendentals=0):
    return pl.pallas_call(
        kernel,
        in_specs=in_specs,
        out_specs=[spec for spec, _, _ in outs],
        out_shape=[jax.ShapeDtypeStruct(shape, dtype) for _, shape, dtype in outs],
        scratch_shapes=scratch,
        compiler_params=pltpu.CompilerParams(vmem_limit_bytes=limit * mib),
        cost_estimate=pl.CostEstimate(
            flops=flops, bytes_accessed=8 * mib, transcendentals=transcendentals
        ),
        name=name,
    )


def sort_kernel(
    first, here, ids, slot_in, queries, teacher, out_a, out_b, slot,
    select, block, moved_a, moved_b, in_sem, out_sem,
):
    tile = 512
    tiles = both // tile

    def read(j):
        source = queries if j < width // tile else teacher
        column = j * tile if j < width // tile else j * tile - width
        return pltpu.make_async_copy(
            source.at[:, pl.ds(column, tile)], block.at[j], in_sem.at[j]
        )

    def written(j):
        columns = pl.ds(j * tile, tile)
        return [
            pltpu.make_async_copy(moved_a.at[j], out_a.at[:, columns], out_sem.at[2 * j]),
            pltpu.make_async_copy(moved_b.at[j], out_b.at[:, columns], out_sem.at[2 * j + 1]),
        ]

    for j in range(tiles):
        read(j).start()
    if first:
        slots = slots_of(ids[...], here[0])
        slot[...] = jnp.broadcast_to(slots, (8, per_device))
    else:
        slots = slot_in[0:1, :]
        slot[...] = jnp.zeros((8, 128), jnp.int32)
    rows = lax.broadcasted_iota(jnp.int32, (per_language, per_device), 0)
    for half, number in enumerate((1, 3) if first else (2, 0)):
        hit = rows + number * per_language == slots
        select[pl.ds(half * per_language, per_language), :] = hit.astype(jnp.float32).astype(
            jnp.bfloat16
        )
    for j in range(tiles):
        read(j).wait()
        moved = jnp.dot(select[...], block[j], preferred_element_type=jnp.float32)
        moved_a[j] = moved[:per_language].astype(jnp.bfloat16)
        moved_b[j] = moved[per_language:].astype(jnp.bfloat16)
        for copy in written(j):
            copy.start()
    for j in range(tiles):
        for copy in written(j):
            copy.wait()


def sort_rows(here, ids, slot, queries, teacher):
    first = slot is None
    tiles = both // 512
    moved = pltpu.VMEM((tiles, per_language, 512), jnp.bfloat16)
    out = (hbm, (per_language, both), jnp.bfloat16)
    return call(
        functools.partial(sort_kernel, first),
        "sort_first" if first else "sort_rest",
        [smem, vmem, vmem, hbm, hbm],
        [out, out, (vmem, (8, per_device) if first else (8, 128), jnp.int32)],
        [
            pltpu.VMEM((2 * per_language, per_device), jnp.bfloat16),
            pltpu.VMEM((tiles, per_device, 512), jnp.bfloat16),
            moved,
            moved,
            pltpu.SemaphoreType.DMA((tiles,)),
            pltpu.SemaphoreType.DMA((2 * tiles,)),
        ],
        60 if first else 28,
        4 * per_language * per_device * both,
    )(here, ids, ids if first else slot, queries, teacher)


def kl_parts(value):
    high = value.astype(jnp.bfloat16).astype(jnp.float32)
    middle = (value - high).astype(jnp.bfloat16).astype(jnp.float32)
    low = value - high - middle
    lane = lax.broadcasted_iota(jnp.int32, value.shape, 1)
    parts = jnp.where(
        lane == 0, high, jnp.where(lane == 1, middle, jnp.where(lane == 2, low, 0.0))
    )
    return parts.astype(jnp.bfloat16)


def row_pass(quarter, scores, block, weights, kl):
    for i in range(4):
        local = pl.ds(pl.multiple_of(quarter * 64 + i * 16, 16), 16)
        own = scores[local, :]
        taught = block[local, :].astype(jnp.float32)
        top = jnp.max(own, axis=1, keepdims=True)
        taught_top = jnp.max(taught, axis=1, keepdims=True)
        grown = jnp.exp(own - top)
        total = jnp.sum(grown, axis=1, keepdims=True)
        shifted = taught - taught_top
        taught_grown = jnp.exp(shifted)
        taught_total = jnp.sum(taught_grown, axis=1, keepdims=True)
        cross = jnp.sum(taught_grown * (shifted - (own - top)), axis=1, keepdims=True)
        diverge = cross / taught_total - jnp.log(taught_total) + jnp.log(total)
        weights[local, :] = (
            grown * (student_scale / total) - taught_grown * (student_scale / taught_total)
        ).astype(jnp.bfloat16)
        kl[local, :] = jnp.broadcast_to(diverge, (16, 128))


def score_quarter(queries, base, quarter, passages, scores):
    columns = pl.ds(pl.multiple_of(quarter * 512, 512), 512)
    scores[:, columns] = (
        lax.dot_general(
            queries[pl.ds(base, per_language), pl.ds(0, width)],
            passages[columns, :],
            (((1,), (1,)), ((), ())),
            preferred_element_type=jnp.float32,
        )
        * student_scale
    )


def teacher_kernel(in0, in1, in2, store, queries, taught_out, parts, sems):
    rows = 3 * per_language

    def saved(number):
        block = pl.ds(number * per_language, per_language)
        behind = pl.ds(rows + number * per_language, per_language)
        return [
            pltpu.make_async_copy(taught_out.at[block], store.at[block], sems.at[number]),
            pltpu.make_async_copy(
                queries.at[block], store.at[behind, pl.ds(0, width)], sems.at[3 + number]
            ),
            pltpu.make_async_copy(
                parts.at[block], store.at[behind, pl.ds(width, extra)], sems.at[6 + number]
            ),
        ]

    for number, block in enumerate((in0, in1, in2)):

        def rows_of(i, carry, number=number, block=block):
            for part in range(4):
                local = pl.ds(pl.multiple_of(i * 64 + part * 16, 16), 16)
                placed = pl.ds(
                    pl.multiple_of(number * per_language + i * 64 + part * 16, 16), 16
                )
                queries[placed, :] = block[local, pl.ds(0, width)]
                taught = block[local, pl.ds(width, passages_all)].astype(jnp.float32)
                shifted = taught - jnp.max(taught, axis=1, keepdims=True)
                grown = jnp.exp(shifted)
                total = jnp.sum(grown, axis=1, keepdims=True)
                cross = jnp.sum(grown * shifted, axis=1, keepdims=True)
                taught_out[placed, :] = (grown * (student_scale / total)).astype(jnp.bfloat16)
                entropy = jnp.broadcast_to(cross / total - jnp.log(total), (16, 128))
                parts[placed, :] = kl_parts(entropy)
            return carry

        lax.fori_loop(0, 4, rows_of, 0)
        for copy in saved(number):
            copy.start()
    for number in range(3):
        for copy in saved(number):
            copy.wait()


def teacher_rows(blocks):
    rows = 3 * per_language
    return call(
        teacher_kernel,
        "teacher_rows",
        [vmem] * 3,
        [
            (hbm, (store_rows, passages_all), jnp.bfloat16),
            (vmem, (rows, width), jnp.bfloat16),
        ],
        [
            pltpu.VMEM((rows, passages_all), jnp.bfloat16),
            pltpu.VMEM((rows, extra), jnp.bfloat16),
            pltpu.SemaphoreType.DMA((9,)),
        ],
        40,
        mib,
        2 * mib,
    )(*blocks)


def student_pass(base, quarter, scores, taught_ref, parts, weights, kl):
    for i in range(4):
        local = pl.ds(pl.multiple_of(quarter * 64 + i * 16, 16), 16)
        placed = pl.ds(pl.multiple_of(base + quarter * 64 + i * 16, 16), 16)
        own = scores[local, :]
        taught = taught_ref[placed, :].astype(jnp.float32)
        shifted = own - jnp.max(own, axis=1, keepdims=True)
        grown = jnp.exp(shifted)
        total = jnp.sum(grown, axis=1, keepdims=True)
        cross = jnp.sum(taught * shifted, axis=1, keepdims=True)
        entropy = jnp.sum(
            parts[placed, pl.ds(width, extra)].astype(jnp.float32), axis=1, keepdims=True
        )
        diverge = entropy + jnp.log(total) - cross * (1.0 / student_scale)
        weights[placed, :] = (grown * (student_scale / total) - taught).astype(jnp.bfloat16)
        kl[placed, :] = jnp.broadcast_to(diverge, (16, 128))


def grad_columns(rows, columns, weights, passages, out):
    out[:, columns] = jnp.dot(
        weights[rows, :],
        passages[pl.ds(0, passages_all), columns],
        preferred_element_type=jnp.float32,
    ).astype(jnp.bfloat16)


def first_kernel(
    chunk_list, target_of, raw, store,
    weights, passages, kl, grad, raw_v, queries, taught, scores, other_scores, raw_sem, in_sem,
):
    def raw_copy(k):
        rows = pl.ds(pl.multiple_of(chunk_list[chunk_count + k], chunk_rows), chunk_rows)
        return pltpu.make_async_copy(raw.at[chunk_list[k], rows], raw_v.at[k], raw_sem.at[k])

    groups = chunk_list[3 * chunk_count]

    def start_group(g, carry):
        for c in range(group_chunks):
            raw_copy(g * group_chunks + c).start()
        return carry

    lax.fori_loop(0, groups, start_group, 0)
    copies = [
        pltpu.make_async_copy(
            store.at[pl.ds(3 * per_language, 3 * per_language), pl.ds(0, width + extra)],
            queries,
            in_sem.at[0],
        ),
        pltpu.make_async_copy(store.at[pl.ds(0, 3 * per_language)], taught, in_sem.at[1]),
    ]
    for copy in copies:
        copy.start()
    passages[pl.ds(0, 16), :] = jnp.zeros((16, width), jnp.bfloat16)

    def place(g, carry):
        for c in range(group_chunks):
            raw_copy(g * group_chunks + c).wait()
        start = pl.multiple_of((chunk_list[2 * chunk_count + g * group_chunks] // 16) * 16, 16)
        target = lax.broadcasted_iota(jnp.int32, (window, group_rows), 0)
        hit = target == target_of[pl.ds(g, 1), :] - start
        chosen = hit.astype(jnp.float32).astype(jnp.bfloat16)
        chunks = raw_v[pl.ds(g * group_chunks, group_chunks)].reshape(group_rows, width)
        moved = jnp.dot(chosen, chunks, preferred_element_type=jnp.float32).astype(jnp.bfloat16)
        head = passages[pl.ds(start, 16), :]
        passages[pl.ds(start, 16), :] = head + moved[:16]
        passages[pl.ds(start + 16, window - 16), :] = moved[16:]
        return carry

    lax.fori_loop(0, groups, place, 0)
    for copy in copies:
        copy.wait()

    def score_only(quarter, carry):
        score_quarter(queries, 0, quarter, passages, scores)
        return carry

    lax.fori_loop(0, 4, score_only, 0)
    held, free = scores, other_scores
    middle = pl.ds(per_language, per_language)
    for number in range(3):
        base = number * per_language

        def together(quarter, carry, base=base, held=held, free=free, last=number == 2):
            if last:
                columns = pl.ds(pl.multiple_of(quarter * 256, 256), 256)
                grad_columns(middle, columns, weights, passages, grad)
            else:
                score_quarter(queries, base + per_language, quarter, passages, free)
            student_pass(base, quarter, held, taught, queries, weights, kl)
            return carry

        lax.fori_loop(0, 4, together, 0)
        held, free = free, held
    grad[:, pl.ds(width, extra)] = kl_parts(kl[middle, :])


def first_blocks(chunk_list, raw, store):
    rows = 3 * per_language
    scores = pltpu.VMEM((per_language, passages_all), jnp.float32)
    return call(
        first_kernel,
        "first_blocks",
        [smem, vmem, hbm, hbm],
        [
            (vmem, (rows, passages_all), jnp.bfloat16),
            (vmem, (passages_all + window, width), jnp.bfloat16),
            (vmem, (rows, 128), jnp.float32),
            (vmem, (per_language, width + extra), jnp.bfloat16),
        ],
        [
            pltpu.VMEM((chunk_count, chunk_rows, width), jnp.bfloat16),
            pltpu.VMEM((rows, width + extra), jnp.bfloat16),
            pltpu.VMEM((rows, passages_all), jnp.bfloat16),
            scores,
            scores,
            pltpu.SemaphoreType.DMA((chunk_count,)),
            pltpu.SemaphoreType.DMA((2,)),
        ],
        40,
        6 * 1024**3,
        2 * mib,
    )(*chunk_list, raw, store)


def chunks_of(counts):
    number = (counts + chunk_rows - 1) // chunk_rows
    upto = jnp.arange(holders)[None, :] < jnp.arange(holders)[:, None]
    offsets = jnp.sum(jnp.where(upto, counts[None, :], 0), axis=1)
    firsts = jnp.sum(jnp.where(upto, number[None, :], 0), axis=1)
    index = jnp.arange(chunk_count)[:, None]
    mine = (index >= firsts[None, :]) & (index < (firsts + number)[None, :])
    row = (index - firsts[None, :]) * chunk_rows

    def pick(values):
        return jnp.sum(jnp.where(mine, values, 0), axis=1)

    holder = pick(jnp.arange(holders)[None, :] + 0 * row)
    used = pick(jnp.minimum(counts[None, :] - row, chunk_rows))
    place = jnp.where(used > 0, pick(offsets[None, :] + row), passages_all)
    slots = jnp.arange(chunk_rows)[None, :]
    groups = (jnp.sum(number) + group_chunks - 1) // group_chunks
    targets = jnp.where(slots < used[:, None], place[:, None] + slots, -1)
    return (
        jnp.concatenate([holder, pick(row), place, groups[None]]).astype(jnp.int32),
        targets.astype(jnp.int32).reshape(chunk_count // group_chunks, group_rows),
    )


def last_kernel(
    core, passages, before, queries, block, weights, send, keep, kl,
    own, teacher, scores, total, in_sem,
):
    own_copy = pltpu.make_async_copy(block.at[:, pl.ds(0, width)], own, in_sem.at[0])
    teacher_copy = pltpu.make_async_copy(
        block.at[:, pl.ds(width, passages_all)], teacher, in_sem.at[1]
    )
    own_copy.start()
    teacher_copy.start()
    own_copy.wait()

    def score_only(quarter, carry):
        score_quarter(own, 0, quarter, passages, scores)
        return carry

    lax.fori_loop(0, 4, score_only, 0)
    teacher_copy.wait()
    contract = (((0,), (0,)), ((), ()))

    def together(quarter, carry):
        row_pass(quarter, scores, teacher, weights, kl)
        columns = pl.ds(pl.multiple_of(quarter * 512, 512), 512)
        total[columns, :] = lax.dot_general(
            before[:, columns],
            queries[...],
            contract,
            preferred_element_type=jnp.float32,
        )
        return carry

    lax.fori_loop(0, 4, together, 0)
    even = core[0] == 0

    def reduce(j, carry):
        columns = pl.ds(pl.multiple_of(j * 256, 256), 256)
        grad = lax.dot_general(
            weights[:, columns],
            own[...],
            contract,
            preferred_element_type=jnp.float32,
        )
        grad = (grad + total[columns, :]).astype(jnp.bfloat16)
        for part in range(2):
            upper = grad[part * 128 : part * 128 + 64]
            lower = grad[part * 128 + 64 : part * 128 + 128]
            rows = pl.ds(pl.multiple_of(j * 128 + part * 64, 64), 64)
            keep[rows, :] = jnp.where(even, upper, lower)
            send[rows, :] = jnp.where(even, lower, upper)
        return carry

    lax.fori_loop(0, passages_all // 256, reduce, 0)


def last_block(core, passages, weights, queries, block):
    half = (vmem, (passages_all // 2, width), jnp.bfloat16)
    return call(
        last_kernel,
        "last_block",
        [smem] + [vmem] * 3 + [hbm],
        [
            (vmem, (per_language, passages_all), jnp.bfloat16),
            half,
            half,
            (vmem, (per_language, 128), jnp.float32),
        ],
        [
            pltpu.VMEM((per_language, width), jnp.bfloat16),
            pltpu.VMEM((per_language, passages_all), jnp.bfloat16),
            pltpu.VMEM((per_language, passages_all), jnp.float32),
            pltpu.VMEM((passages_all, width), jnp.float32),
            pltpu.SemaphoreType.DMA((2,)),
        ],
        20,
        6 * 1024**3,
        mib,
    )(core, passages, weights, queries, block)


def query_kernel(places, passages, *refs):
    for number, place in enumerate(places):
        weights, kl = refs[2 * number], refs[2 * number + 1]
        out = refs[2 * len(places) + number]
        rows = pl.ds(place * per_language, per_language)

        def step(half, carry, rows=rows, weights=weights, out=out):
            columns = pl.ds(pl.multiple_of(half * 512, 512), 512)
            grad_columns(rows, columns, weights, passages, out)
            return carry

        lax.fori_loop(0, 2, step, 0)
        out[:, pl.ds(width, extra)] = kl_parts(kl[rows, :])


def query_grads(places, passages, *arrays):
    return call(
        functools.partial(query_kernel, places),
        "query_grads",
        [vmem] * (1 + len(arrays)),
        [(vmem, (per_language, width + extra), jnp.bfloat16)] * len(places),
        [],
        8,
        len(places) * 1024**3,
    )(passages, *arrays)


def pair_kernel(keep, other, out):
    def step(i, carry):
        rows = pl.ds(pl.multiple_of(i * 64, 64), 64)
        out[rows, :] = (
            keep[rows, :].astype(jnp.float32) + other[rows, :].astype(jnp.float32)
        ).astype(jnp.bfloat16)
        return carry

    lax.fori_loop(0, passages_all // 128, step, 0)


def pair_sum(keep, other):
    return call(
        pair_kernel, "pair_sum", [vmem] * 2, [(vmem, keep.shape, jnp.bfloat16)], [], 8, mib
    )(keep, other)[0]


def selection(slot, numbers, select):
    rows = lax.broadcasted_iota(jnp.int32, (per_language, per_device), 0)
    for half, number in enumerate(numbers):
        hit = rows + number * per_language == slot[0:1, :]
        select[half * per_language : (half + 1) * per_language, :] = hit.astype(
            jnp.float32
        ).astype(jnp.bfloat16)


def joined(select, blocks, columns):
    part = None
    for half, block in enumerate(blocks):
        term = lax.dot_general(
            select[half * per_language : (half + 1) * per_language, :],
            block[:, columns],
            (((0,), (0,)), ((), ())),
            preferred_element_type=jnp.float32,
        )
        part = term if part is None else part + term
    return part


def restore_first_kernel(slot, in0, in1, in3, out, select):
    selection(slot, (0, 1, 3), select)
    blocks = (in0, in1, in3)

    def step(j, carry):
        columns = pl.ds(pl.multiple_of(j * 256, 256), 256)
        out[:, columns] = joined(select, blocks, columns).astype(jnp.bfloat16)
        return carry

    lax.fori_loop(0, width // 256, step, 0)
    columns = pl.ds(width, extra)
    out[:, columns] = joined(select, blocks, columns).astype(jnp.bfloat16)


def restore_last_kernel(slot, begun, in2, grads_out, kl, select, grads, out_sem):
    selection(slot, (2,), select)

    def written(j):
        columns = pl.ds(pl.multiple_of(j * 256, 256), 256)
        return pltpu.make_async_copy(grads.at[j], grads_out.at[:, columns], out_sem.at[j])

    def step(j, carry):
        columns = pl.ds(pl.multiple_of(j * 256, 256), 256)
        added = joined(select, (in2,), columns) + begun[:, columns].astype(jnp.float32)
        grads[j] = added.astype(jnp.bfloat16)
        written(j).start()
        return carry

    lax.fori_loop(0, width // 256, step, 0)
    columns = pl.ds(width, extra)
    parts = joined(select, (in2,), columns) + begun[:, columns].astype(jnp.float32)
    column = jnp.sum(parts, axis=1, keepdims=True)
    kl[...] = jnp.transpose(jnp.broadcast_to(column, (per_device, 128)))[:1]
    for j in range(width // 256):
        written(j).wait()


def restore_first(slot, blocks):
    return call(
        restore_first_kernel,
        "restore_first",
        [vmem] * 4,
        [(vmem, (per_device, width + extra), jnp.bfloat16)],
        [pltpu.VMEM((3 * per_language, per_device), jnp.bfloat16)],
        12,
        15 * 1024**3,
    )(slot, *blocks)[0]


def restore_last(slot, begun, block):
    return call(
        restore_last_kernel,
        "restore_last",
        [vmem] * 3,
        [
            (hbm, (per_device, width), jnp.bfloat16),
            (vmem, (1, per_device), jnp.float32),
        ],
        [
            pltpu.VMEM((per_language, per_device), jnp.bfloat16),
            pltpu.VMEM((width // 256, per_device, 256), jnp.bfloat16),
            pltpu.SemaphoreType.DMA((width // 256,)),
        ],
        12,
        1024**3,
    )(slot, begun, block)


def sum_kernel(pieces, out, held, sems):
    copies = []
    for i in range(4):
        rows = pl.ds(16 * i, 16)
        copies.append(pltpu.make_async_copy(pieces.at[:, rows], held.at[:, rows], sems.at[i]))
        copies[-1].start()
    for i, copy in enumerate(copies):
        copy.wait()
        total = held[0, 16 * i : 16 * (i + 1), :].astype(jnp.float32)
        for j in range(1, pieces.shape[0]):
            total = total + held[j, 16 * i : 16 * (i + 1), :].astype(jnp.float32)
        out[16 * i : 16 * (i + 1), :] = total.astype(jnp.bfloat16)


def sum_pieces(pieces):
    return call(
        sum_kernel,
        "sum_pieces",
        [hbm],
        [(vmem, (64, width), jnp.bfloat16)],
        [pltpu.VMEM(pieces.shape, jnp.bfloat16), pltpu.SemaphoreType.DMA((4,))],
        8,
        mib,
    )(pieces)[0]


def shift(array, by):
    pairs = [(i, (i + by) % languages) for i in range(languages)]
    return lax.ppermute(array, "x", pairs)


def on_device(queries, bucket_ids, raw_passages, counts, teacher):
    group = ("y", "z", "c")
    here = lax.axis_index("x").astype(jnp.int32).reshape(1)
    core = lax.axis_index("c").astype(jnp.int32).reshape(1)
    all_raw = lax.all_gather(raw_passages[0], group, axis=0, tiled=True)
    ids = bucket_ids[0]
    out1, out3, slot = sort_rows(here, ids, None, queries[0, 0], teacher[0, 0])
    in1, in3 = shift(out1, 1), shift(out3, 3)
    out2, in0, _ = sort_rows(here, ids, slot, queries[0, 0], teacher[0, 0])
    held_counts, in0, out2 = lax.optimization_barrier((counts, in0, out2))
    holder_counts = lax.all_gather(held_counts[0], group, axis=0, tiled=True)
    chunk_list = chunks_of(holder_counts)
    out2, in1, in3, chunk_list = lax.optimization_barrier((out2, in1, in3, chunk_list))
    in2 = shift(out2, 2)
    store, moved = teacher_rows((in0, in1, in3))
    all_raw, store, moved = lax.optimization_barrier((all_raw, store, moved))
    weights, passages, kl, back1 = first_blocks(chunk_list, all_raw, store)
    last_weights, send, keep, last_kl = last_block(core, passages, weights, moved, in2)
    other = lax.ppermute(send, "c", [(0, 1), (1, 0)])
    (back3,) = query_grads((2,), passages, weights, kl)
    keep, back3 = lax.optimization_barrier((keep, back3))
    home1, home3 = shift(back1, -1), shift(back3, -3)
    paired = pair_sum(keep, other)
    spread = lax.all_to_all(
        paired.reshape(16, 64, width), ("y", "z"), split_axis=0, concat_axis=0, tiled=True
    )
    paired, weights, last_weights = lax.optimization_barrier((paired, weights, last_weights))
    back2, back0 = query_grads((0, 0), passages, last_weights, last_kl, weights, kl)
    home2 = shift(back2, -2)
    grad_passages = sum_pieces(spread)
    begun = restore_first(slot, (back0, home1, home3))
    grad_queries, kl_rows = restore_last(slot, begun, home2)
    return (grad_queries[None, None], grad_passages[None], kl_rows[None])


def solution(mesh):
    split = Mesh(mesh.devices.reshape(4, 4, 4, 2), ("x", "y", "z", "c"))
    group = ("y", "z", "c")
    in_specs = (
        P("x", group, None, None),
        P("x", group, None),
        P("x", group, None, None),
        P("x", group),
        P("x", group, None, None),
    )
    out_specs = (P("x", group, None, None), P("x", group, None), P("x", group, None))
    return jax.shard_map(
        on_device, mesh=split, in_specs=in_specs, out_specs=out_specs, check_vma=False
    )
```

```python
import functools

import jax
import jax.numpy as jnp
from jax import lax
from jax.experimental import pallas as pl
from jax.experimental.pallas import tpu as pltpu
from jax.sharding import Mesh
from jax.sharding import PartitionSpec as P

student_scale = 0.1
languages = 4
holders = 32
capacity = 192
width = 1024
per_device = 1024
per_language = 256
passages_all = 2048
both = width + passages_all
group_chunks = 8
group_rows = 256
window = 272
extra = 128
chunk_rows = 32
chunk_count = 96
store_rows = 6144
mib = 1024 * 1024


def slots_of(ids, here):
    turned = lax.rem(ids - here + languages, languages)
    kinds = lax.broadcasted_iota(jnp.int32, (8, per_device), 0)
    hot = (turned == kinds).astype(jnp.float32)
    parts = per_device // 128
    stacked = jnp.concatenate([hot[:, i * 128 : (i + 1) * 128] for i in range(parts)], axis=0)
    earlier = lax.broadcasted_iota(jnp.int32, (128, 128), 0)
    later = lax.broadcasted_iota(jnp.int32, (128, 128), 1)
    upper = (earlier <= later).astype(jnp.float32).astype(jnp.bfloat16)
    sums = jnp.dot(stacked.astype(jnp.bfloat16), upper, preferred_element_type=jnp.float32)
    before = jnp.zeros((8, 1), jnp.float32)
    ranks = []
    for i in range(parts):
        segment = sums[i * 8 : (i + 1) * 8]
        ranks.append(segment + before)
        before = before + segment[:, 127:128]
    place = jnp.concatenate(ranks, axis=1) - 1.0 + kinds.astype(jnp.float32) * per_language
    return jnp.sum(hot * place, axis=0, keepdims=True).astype(jnp.int32)


vmem = pl.BlockSpec(memory_space=pltpu.VMEM)
smem = pl.BlockSpec(memory_space=pltpu.SMEM)
hbm = pl.BlockSpec(memory_space=pltpu.HBM)


def call(kernel, name, in_specs, outs, scratch, limit, flops, transcendentals=0):
    return pl.pallas_call(
        kernel,
        in_specs=in_specs,
        out_specs=[spec for spec, _, _ in outs],
        out_shape=[jax.ShapeDtypeStruct(shape, dtype) for _, shape, dtype in outs],
        scratch_shapes=scratch,
        compiler_params=pltpu.CompilerParams(vmem_limit_bytes=limit * mib),
        cost_estimate=pl.CostEstimate(
            flops=flops, bytes_accessed=8 * mib, transcendentals=transcendentals
        ),
        name=name,
    )


def sort_kernel(
    first, here, ids, slot_in, queries, teacher, out_a, out_b, slot,
    select, block, moved_a, moved_b, in_sem, out_sem,
):
    tile = 512
    tiles = both // tile

    def read(j):
        source = queries if j < width // tile else teacher
        column = j * tile if j < width // tile else j * tile - width
        return pltpu.make_async_copy(
            source.at[:, pl.ds(column, tile)], block.at[j], in_sem.at[j]
        )

    def written(j):
        columns = pl.ds(j * tile, tile)
        return [
            pltpu.make_async_copy(moved_a.at[j], out_a.at[:, columns], out_sem.at[2 * j]),
            pltpu.make_async_copy(moved_b.at[j], out_b.at[:, columns], out_sem.at[2 * j + 1]),
        ]

    for j in range(tiles):
        read(j).start()
    if first:
        slots = slots_of(ids[...], here[0])
        slot[...] = jnp.broadcast_to(slots, (8, per_device))
    else:
        slots = slot_in[0:1, :]
        slot[...] = jnp.zeros((8, 128), jnp.int32)
    rows = lax.broadcasted_iota(jnp.int32, (per_language, per_device), 0)
    for half, number in enumerate((1, 3) if first else (2, 0)):
        hit = rows + number * per_language == slots
        select[pl.ds(half * per_language, per_language), :] = hit.astype(jnp.float32).astype(
            jnp.bfloat16
        )
    for j in range(tiles):
        read(j).wait()
        moved = jnp.dot(select[...], block[j], preferred_element_type=jnp.float32)
        moved_a[j] = moved[:per_language].astype(jnp.bfloat16)
        moved_b[j] = moved[per_language:].astype(jnp.bfloat16)
        for copy in written(j):
            copy.start()
    for j in range(tiles):
        for copy in written(j):
            copy.wait()


def sort_rows(here, ids, slot, queries, teacher):
    first = slot is None
    tiles = both // 512
    moved = pltpu.VMEM((tiles, per_language, 512), jnp.bfloat16)
    out = (hbm, (per_language, both), jnp.bfloat16)
    return call(
        functools.partial(sort_kernel, first),
        "sort_first" if first else "sort_rest",
        [smem, vmem, vmem, hbm, hbm],
        [out, out, (vmem, (8, per_device) if first else (8, 128), jnp.int32)],
        [
            pltpu.VMEM((2 * per_language, per_device), jnp.bfloat16),
            pltpu.VMEM((tiles, per_device, 512), jnp.bfloat16),
            moved,
            moved,
            pltpu.SemaphoreType.DMA((tiles,)),
            pltpu.SemaphoreType.DMA((2 * tiles,)),
        ],
        60 if first else 28,
        4 * per_language * per_device * both,
    )(here, ids, ids if first else slot, queries, teacher)


def kl_parts(value):
    high = value.astype(jnp.bfloat16).astype(jnp.float32)
    middle = (value - high).astype(jnp.bfloat16).astype(jnp.float32)
    low = value - high - middle
    lane = lax.broadcasted_iota(jnp.int32, value.shape, 1)
    parts = jnp.where(
        lane == 0, high, jnp.where(lane == 1, middle, jnp.where(lane == 2, low, 0.0))
    )
    return parts.astype(jnp.bfloat16)


def row_pass(quarter, scores, block, weights, kl):
    for i in range(4):
        local = pl.ds(pl.multiple_of(quarter * 64 + i * 16, 16), 16)
        own = scores[local, :]
        taught = block[local, :].astype(jnp.float32)
        top = jnp.max(own, axis=1, keepdims=True)
        taught_top = jnp.max(taught, axis=1, keepdims=True)
        grown = jnp.exp(own - top)
        total = jnp.sum(grown, axis=1, keepdims=True)
        shifted = taught - taught_top
        taught_grown = jnp.exp(shifted)
        taught_total = jnp.sum(taught_grown, axis=1, keepdims=True)
        cross = jnp.sum(taught_grown * (shifted - (own - top)), axis=1, keepdims=True)
        diverge = cross / taught_total - jnp.log(taught_total) + jnp.log(total)
        weights[local, :] = (
            grown * (student_scale / total) - taught_grown * (student_scale / taught_total)
        ).astype(jnp.bfloat16)
        kl[local, :] = jnp.broadcast_to(diverge, (16, 128))


def score_quarter(queries, base, quarter, passages, scores):
    columns = pl.ds(pl.multiple_of(quarter * 512, 512), 512)
    scores[:, columns] = (
        lax.dot_general(
            queries[pl.ds(base, per_language), pl.ds(0, width)],
            passages[columns, :],
            (((1,), (1,)), ((), ())),
            preferred_element_type=jnp.float32,
        )
        * student_scale
    )


def teacher_kernel(in0, in1, in2, store, queries, taught_out, parts, sems):
    rows = 3 * per_language

    def saved(number):
        block = pl.ds(number * per_language, per_language)
        behind = pl.ds(rows + number * per_language, per_language)
        return [
            pltpu.make_async_copy(taught_out.at[block], store.at[block], sems.at[number]),
            pltpu.make_async_copy(
                queries.at[block], store.at[behind, pl.ds(0, width)], sems.at[3 + number]
            ),
            pltpu.make_async_copy(
                parts.at[block], store.at[behind, pl.ds(width, extra)], sems.at[6 + number]
            ),
        ]

    for number, block in enumerate((in0, in1, in2)):

        def rows_of(i, carry, number=number, block=block):
            for part in range(4):
                local = pl.ds(pl.multiple_of(i * 64 + part * 16, 16), 16)
                placed = pl.ds(
                    pl.multiple_of(number * per_language + i * 64 + part * 16, 16), 16
                )
                queries[placed, :] = block[local, pl.ds(0, width)]
                taught = block[local, pl.ds(width, passages_all)].astype(jnp.float32)
                shifted = taught - jnp.max(taught, axis=1, keepdims=True)
                grown = jnp.exp(shifted)
                total = jnp.sum(grown, axis=1, keepdims=True)
                cross = jnp.sum(grown * shifted, axis=1, keepdims=True)
                taught_out[placed, :] = (grown * (student_scale / total)).astype(jnp.bfloat16)
                entropy = jnp.broadcast_to(cross / total - jnp.log(total), (16, 128))
                parts[placed, :] = kl_parts(entropy)
            return carry

        lax.fori_loop(0, 4, rows_of, 0)
        for copy in saved(number):
            copy.start()
    for number in range(3):
        for copy in saved(number):
            copy.wait()


def teacher_rows(blocks):
    rows = 3 * per_language
    return call(
        teacher_kernel,
        "teacher_rows",
        [vmem] * 3,
        [
            (hbm, (store_rows, passages_all), jnp.bfloat16),
            (vmem, (rows, width), jnp.bfloat16),
        ],
        [
            pltpu.VMEM((rows, passages_all), jnp.bfloat16),
            pltpu.VMEM((rows, extra), jnp.bfloat16),
            pltpu.SemaphoreType.DMA((9,)),
        ],
        40,
        mib,
        2 * mib,
    )(*blocks)


def student_pass(base, quarter, scores, taught_ref, parts, weights, kl):
    for i in range(4):
        local = pl.ds(pl.multiple_of(quarter * 64 + i * 16, 16), 16)
        placed = pl.ds(pl.multiple_of(base + quarter * 64 + i * 16, 16), 16)
        own = scores[local, :]
        taught = taught_ref[placed, :].astype(jnp.float32)
        shifted = own - jnp.max(own, axis=1, keepdims=True)
        grown = jnp.exp(shifted)
        total = jnp.sum(grown, axis=1, keepdims=True)
        cross = jnp.sum(taught * shifted, axis=1, keepdims=True)
        entropy = jnp.sum(
            parts[placed, pl.ds(width, extra)].astype(jnp.float32), axis=1, keepdims=True
        )
        diverge = entropy + jnp.log(total) - cross * (1.0 / student_scale)
        weights[placed, :] = (grown * (student_scale / total) - taught).astype(jnp.bfloat16)
        kl[placed, :] = jnp.broadcast_to(diverge, (16, 128))


def grad_columns(rows, columns, weights, passages, out):
    out[:, columns] = jnp.dot(
        weights[rows, :],
        passages[pl.ds(0, passages_all), columns],
        preferred_element_type=jnp.float32,
    ).astype(jnp.bfloat16)


def first_kernel(
    chunk_list, target_of, raw, store,
    weights, passages, kl, grad, raw_v, queries, taught, scores, other_scores, raw_sem, in_sem,
):
    def raw_copy(k):
        rows = pl.ds(pl.multiple_of(chunk_list[chunk_count + k], chunk_rows), chunk_rows)
        return pltpu.make_async_copy(raw.at[chunk_list[k], rows], raw_v.at[k], raw_sem.at[k])

    groups = chunk_list[3 * chunk_count]

    def start_group(g, carry):
        for c in range(2 * group_chunks):
            raw_copy(2 * g * group_chunks + c).start()
        return carry

    lax.fori_loop(0, groups, start_group, 0)
    copies = [
        pltpu.make_async_copy(
            store.at[pl.ds(3 * per_language, 3 * per_language), pl.ds(0, width + extra)],
            queries,
            in_sem.at[0],
        ),
        pltpu.make_async_copy(store.at[pl.ds(0, 3 * per_language)], taught, in_sem.at[1]),
    ]
    for copy in copies:
        copy.start()
    passages[pl.ds(0, 16), :] = jnp.zeros((16, width), jnp.bfloat16)

    def place(pair, carry):
        ready = []
        for g in (2 * pair, 2 * pair + 1):
            for c in range(group_chunks):
                raw_copy(g * group_chunks + c).wait()
        for g in (2 * pair, 2 * pair + 1):
            first = chunk_list[2 * chunk_count + g * group_chunks]
            start = pl.multiple_of((first // 16) * 16, 16)
            target = lax.broadcasted_iota(jnp.int32, (window, group_rows), 0)
            hit = target == target_of[pl.ds(g, 1), :] - start
            chosen = hit.astype(jnp.float32).astype(jnp.bfloat16)
            chunks = raw_v[pl.ds(g * group_chunks, group_chunks)].reshape(group_rows, width)
            moved = jnp.dot(chosen, chunks, preferred_element_type=jnp.float32)
            ready.append((start, moved.astype(jnp.bfloat16)))
        for start, moved in ready:
            head = passages[pl.ds(start, 16), :]
            passages[pl.ds(start, 16), :] = head + moved[:16]
            passages[pl.ds(start + 16, window - 16), :] = moved[16:]
        return carry

    lax.fori_loop(0, groups, place, 0)
    for copy in copies:
        copy.wait()

    def score_only(quarter, carry):
        score_quarter(queries, 0, quarter, passages, scores)
        return carry

    lax.fori_loop(0, 4, score_only, 0)
    held, free = scores, other_scores
    middle = pl.ds(per_language, per_language)
    for number in range(3):
        base = number * per_language

        def together(quarter, carry, base=base, held=held, free=free, last=number == 2):
            if last:
                columns = pl.ds(pl.multiple_of(quarter * 256, 256), 256)
                grad_columns(middle, columns, weights, passages, grad)
            else:
                score_quarter(queries, base + per_language, quarter, passages, free)
            student_pass(base, quarter, held, taught, queries, weights, kl)
            return carry

        lax.fori_loop(0, 4, together, 0)
        held, free = free, held
    grad[:, pl.ds(width, extra)] = kl_parts(kl[middle, :])


def first_blocks(chunk_list, raw, store):
    rows = 3 * per_language
    scores = pltpu.VMEM((per_language, passages_all), jnp.float32)
    return call(
        first_kernel,
        "first_blocks",
        [smem, vmem, hbm, hbm],
        [
            (vmem, (rows, passages_all), jnp.bfloat16),
            (vmem, (passages_all + window, width), jnp.bfloat16),
            (vmem, (rows, 128), jnp.float32),
            (vmem, (per_language, width + extra), jnp.bfloat16),
        ],
        [
            pltpu.VMEM((chunk_count, chunk_rows, width), jnp.bfloat16),
            pltpu.VMEM((rows, width + extra), jnp.bfloat16),
            pltpu.VMEM((rows, passages_all), jnp.bfloat16),
            scores,
            scores,
            pltpu.SemaphoreType.DMA((chunk_count,)),
            pltpu.SemaphoreType.DMA((2,)),
        ],
        40,
        6 * 1024**3,
        2 * mib,
    )(*chunk_list, raw, store)


def chunks_of(counts):
    number = (counts + chunk_rows - 1) // chunk_rows
    upto = jnp.arange(holders)[None, :] < jnp.arange(holders)[:, None]
    offsets = jnp.sum(jnp.where(upto, counts[None, :], 0), axis=1)
    firsts = jnp.sum(jnp.where(upto, number[None, :], 0), axis=1)
    index = jnp.arange(chunk_count)[:, None]
    mine = (index >= firsts[None, :]) & (index < (firsts + number)[None, :])
    row = (index - firsts[None, :]) * chunk_rows

    def pick(values):
        return jnp.sum(jnp.where(mine, values, 0), axis=1)

    holder = pick(jnp.arange(holders)[None, :] + 0 * row)
    used = pick(jnp.minimum(counts[None, :] - row, chunk_rows))
    place = jnp.where(used > 0, pick(offsets[None, :] + row), passages_all)
    slots = jnp.arange(chunk_rows)[None, :]
    groups = (jnp.sum(number) + 2 * group_chunks - 1) // (2 * group_chunks)
    targets = jnp.where(slots < used[:, None], place[:, None] + slots, -1)
    return (
        jnp.concatenate([holder, pick(row), place, groups[None]]).astype(jnp.int32),
        targets.astype(jnp.int32).reshape(chunk_count // group_chunks, group_rows),
    )


def last_kernel(
    core, passages, before, queries, block, weights, send, keep, kl,
    own, teacher, scores, total, in_sem,
):
    own_copy = pltpu.make_async_copy(block.at[:, pl.ds(0, width)], own, in_sem.at[0])
    teacher_copy = pltpu.make_async_copy(
        block.at[:, pl.ds(width, passages_all)], teacher, in_sem.at[1]
    )
    own_copy.start()
    teacher_copy.start()
    own_copy.wait()

    def score_only(quarter, carry):
        score_quarter(own, 0, quarter, passages, scores)
        return carry

    lax.fori_loop(0, 4, score_only, 0)
    teacher_copy.wait()
    contract = (((0,), (0,)), ((), ()))

    def together(quarter, carry):
        row_pass(quarter, scores, teacher, weights, kl)
        columns = pl.ds(pl.multiple_of(quarter * 512, 512), 512)
        total[columns, :] = lax.dot_general(
            before[:, columns],
            queries[...],
            contract,
            preferred_element_type=jnp.float32,
        )
        return carry

    lax.fori_loop(0, 4, together, 0)
    even = core[0] == 0

    def reduce(j, carry):
        columns = pl.ds(pl.multiple_of(j * 256, 256), 256)
        grad = lax.dot_general(
            weights[:, columns],
            own[...],
            contract,
            preferred_element_type=jnp.float32,
        )
        grad = (grad + total[columns, :]).astype(jnp.bfloat16)
        for part in range(2):
            upper = grad[part * 128 : part * 128 + 64]
            lower = grad[part * 128 + 64 : part * 128 + 128]
            rows = pl.ds(pl.multiple_of(j * 128 + part * 64, 64), 64)
            keep[rows, :] = jnp.where(even, upper, lower)
            send[rows, :] = jnp.where(even, lower, upper)
        return carry

    lax.fori_loop(0, passages_all // 256, reduce, 0)


def last_block(core, passages, weights, queries, block):
    half = (vmem, (passages_all // 2, width), jnp.bfloat16)
    return call(
        last_kernel,
        "last_block",
        [smem] + [vmem] * 3 + [hbm],
        [
            (vmem, (per_language, passages_all), jnp.bfloat16),
            half,
            half,
            (vmem, (per_language, 128), jnp.float32),
        ],
        [
            pltpu.VMEM((per_language, width), jnp.bfloat16),
            pltpu.VMEM((per_language, passages_all), jnp.bfloat16),
            pltpu.VMEM((per_language, passages_all), jnp.float32),
            pltpu.VMEM((passages_all, width), jnp.float32),
            pltpu.SemaphoreType.DMA((2,)),
        ],
        20,
        6 * 1024**3,
        mib,
    )(core, passages, weights, queries, block)


def query_kernel(places, passages, *refs):
    for number, place in enumerate(places):
        weights, kl = refs[2 * number], refs[2 * number + 1]
        out = refs[2 * len(places) + number]
        rows = pl.ds(place * per_language, per_language)

        def step(half, carry, rows=rows, weights=weights, out=out):
            columns = pl.ds(pl.multiple_of(half * 512, 512), 512)
            grad_columns(rows, columns, weights, passages, out)
            return carry

        lax.fori_loop(0, 2, step, 0)
        out[:, pl.ds(width, extra)] = kl_parts(kl[rows, :])


def query_grads(places, passages, *arrays):
    return call(
        functools.partial(query_kernel, places),
        "query_grads",
        [vmem] * (1 + len(arrays)),
        [(vmem, (per_language, width + extra), jnp.bfloat16)] * len(places),
        [],
        8,
        len(places) * 1024**3,
    )(passages, *arrays)


def pair_kernel(keep, other, out):
    def step(i, carry):
        rows = pl.ds(pl.multiple_of(i * 64, 64), 64)
        out[rows, :] = (
            keep[rows, :].astype(jnp.float32) + other[rows, :].astype(jnp.float32)
        ).astype(jnp.bfloat16)
        return carry

    lax.fori_loop(0, passages_all // 128, step, 0)


def pair_sum(keep, other):
    return call(
        pair_kernel, "pair_sum", [vmem] * 2, [(vmem, keep.shape, jnp.bfloat16)], [], 8, mib
    )(keep, other)[0]


def selection(slot, numbers, select):
    rows = lax.broadcasted_iota(jnp.int32, (per_language, per_device), 0)
    for half, number in enumerate(numbers):
        hit = rows + number * per_language == slot[0:1, :]
        select[half * per_language : (half + 1) * per_language, :] = hit.astype(
            jnp.float32
        ).astype(jnp.bfloat16)


def joined(select, blocks, columns):
    part = None
    for half, block in enumerate(blocks):
        term = lax.dot_general(
            select[half * per_language : (half + 1) * per_language, :],
            block[:, columns],
            (((0,), (0,)), ((), ())),
            preferred_element_type=jnp.float32,
        )
        part = term if part is None else part + term
    return part


def restore_first_kernel(slot, in0, in1, in3, out, select):
    selection(slot, (0, 1, 3), select)
    blocks = (in0, in1, in3)

    def step(j, carry):
        columns = pl.ds(pl.multiple_of(j * 256, 256), 256)
        out[:, columns] = joined(select, blocks, columns).astype(jnp.bfloat16)
        return carry

    lax.fori_loop(0, width // 256, step, 0)
    columns = pl.ds(width, extra)
    out[:, columns] = joined(select, blocks, columns).astype(jnp.bfloat16)


def restore_last_kernel(slot, begun, in2, grads_out, kl, select, grads, out_sem):
    selection(slot, (2,), select)

    def written(j):
        columns = pl.ds(pl.multiple_of(j * 256, 256), 256)
        return pltpu.make_async_copy(grads.at[j], grads_out.at[:, columns], out_sem.at[j])

    def step(j, carry):
        columns = pl.ds(pl.multiple_of(j * 256, 256), 256)
        added = joined(select, (in2,), columns) + begun[:, columns].astype(jnp.float32)
        grads[j] = added.astype(jnp.bfloat16)
        written(j).start()
        return carry

    lax.fori_loop(0, width // 256, step, 0)
    columns = pl.ds(width, extra)
    parts = joined(select, (in2,), columns) + begun[:, columns].astype(jnp.float32)
    column = jnp.sum(parts, axis=1, keepdims=True)
    kl[...] = jnp.transpose(jnp.broadcast_to(column, (per_device, 128)))[:1]
    for j in range(width // 256):
        written(j).wait()


def restore_first(slot, blocks):
    return call(
        restore_first_kernel,
        "restore_first",
        [vmem] * 4,
        [(vmem, (per_device, width + extra), jnp.bfloat16)],
        [pltpu.VMEM((3 * per_language, per_device), jnp.bfloat16)],
        12,
        15 * 1024**3,
    )(slot, *blocks)[0]


def restore_last(slot, begun, block):
    return call(
        restore_last_kernel,
        "restore_last",
        [vmem] * 3,
        [
            (hbm, (per_device, width), jnp.bfloat16),
            (vmem, (1, per_device), jnp.float32),
        ],
        [
            pltpu.VMEM((per_language, per_device), jnp.bfloat16),
            pltpu.VMEM((width // 256, per_device, 256), jnp.bfloat16),
            pltpu.SemaphoreType.DMA((width // 256,)),
        ],
        12,
        1024**3,
    )(slot, begun, block)


def sum_kernel(pieces, out, held, sems):
    def read(i, j):
        rows, some = pl.ds(16 * i, 16), pl.ds(4 * j, 4)
        return pltpu.make_async_copy(
            pieces.at[some, rows], held.at[some, rows], sems.at[4 * i + j]
        )

    for i in range(4):
        for j in range(4):
            read(i, j).start()
    for i in range(4):
        for j in range(4):
            read(i, j).wait()
        total = held[0, 16 * i : 16 * (i + 1), :].astype(jnp.float32)
        for j in range(1, pieces.shape[0]):
            total = total + held[j, 16 * i : 16 * (i + 1), :].astype(jnp.float32)
        out[16 * i : 16 * (i + 1), :] = total.astype(jnp.bfloat16)


def sum_pieces(pieces):
    return call(
        sum_kernel,
        "sum_pieces",
        [hbm],
        [(vmem, (64, width), jnp.bfloat16)],
        [pltpu.VMEM(pieces.shape, jnp.bfloat16), pltpu.SemaphoreType.DMA((16,))],
        8,
        mib,
    )(pieces)[0]


def shift(array, by):
    pairs = [(i, (i + by) % languages) for i in range(languages)]
    return lax.ppermute(array, "x", pairs)


def on_device(queries, bucket_ids, raw_passages, counts, teacher):
    group = ("y", "z", "c")
    here = lax.axis_index("x").astype(jnp.int32).reshape(1)
    core = lax.axis_index("c").astype(jnp.int32).reshape(1)
    all_raw = lax.all_gather(raw_passages[0], group, axis=0, tiled=True)
    ids = bucket_ids[0]
    out1, out3, slot = sort_rows(here, ids, None, queries[0, 0], teacher[0, 0])
    in1, in3 = shift(out1, 1), shift(out3, 3)
    out2, in0, _ = sort_rows(here, ids, slot, queries[0, 0], teacher[0, 0])
    held_counts, in0, out2 = lax.optimization_barrier((counts, in0, out2))
    holder_counts = lax.all_gather(held_counts[0], group, axis=0, tiled=True)
    chunk_list = chunks_of(holder_counts)
    out2, in1, in3, chunk_list = lax.optimization_barrier((out2, in1, in3, chunk_list))
    in2 = shift(out2, 2)
    store, moved = teacher_rows((in0, in1, in3))
    all_raw, store, moved = lax.optimization_barrier((all_raw, store, moved))
    weights, passages, kl, back1 = first_blocks(chunk_list, all_raw, store)
    last_weights, send, keep, last_kl = last_block(core, passages, weights, moved, in2)
    other = lax.ppermute(send, "c", [(0, 1), (1, 0)])
    (back3,) = query_grads((2,), passages, weights, kl)
    keep, back3 = lax.optimization_barrier((keep, back3))
    home1, home3 = shift(back1, -1), shift(back3, -3)
    paired = pair_sum(keep, other)
    spread = lax.all_to_all(
        paired.reshape(16, 64, width), ("y", "z"), split_axis=0, concat_axis=0, tiled=True
    )
    paired, weights, last_weights = lax.optimization_barrier((paired, weights, last_weights))
    back2, back0 = query_grads((0, 0), passages, last_weights, last_kl, weights, kl)
    home2 = shift(back2, -2)
    grad_passages = sum_pieces(spread)
    begun = restore_first(slot, (back0, home1, home3))
    grad_queries, kl_rows = restore_last(slot, begun, home2)
    return (grad_queries[None, None], grad_passages[None], kl_rows[None])


def solution(mesh):
    split = Mesh(mesh.devices.reshape(4, 4, 4, 2), ("x", "y", "z", "c"))
    group = ("y", "z", "c")
    in_specs = (
        P("x", group, None, None),
        P("x", group, None),
        P("x", group, None, None),
        P("x", group),
        P("x", group, None, None),
    )
    out_specs = (P("x", group, None, None), P("x", group, None), P("x", group, None))
    return jax.shard_map(
        on_device, mesh=split, in_specs=in_specs, out_specs=out_specs, check_vma=False
    )
```

```python
import functools

import jax
import jax.numpy as jnp
from jax import lax
from jax.experimental import pallas as pl
from jax.experimental.pallas import tpu as pltpu
from jax.sharding import Mesh
from jax.sharding import PartitionSpec as P

student_scale = 0.1
languages = 4
holders = 32
capacity = 192
width = 1024
per_device = 1024
per_language = 256
passages_all = 2048
both = width + passages_all
group_chunks = 8
group_rows = 256
window = 272
extra = 128
chunk_rows = 32
chunk_count = 96
store_rows = 6144
mib = 1024 * 1024


def slots_of(ids, here):
    turned = lax.rem(ids - here + languages, languages)
    kinds = lax.broadcasted_iota(jnp.int32, (8, per_device), 0)
    hot = (turned == kinds).astype(jnp.float32)
    parts = per_device // 128
    stacked = jnp.concatenate([hot[:, i * 128 : (i + 1) * 128] for i in range(parts)], axis=0)
    earlier = lax.broadcasted_iota(jnp.int32, (128, 128), 0)
    later = lax.broadcasted_iota(jnp.int32, (128, 128), 1)
    upper = (earlier <= later).astype(jnp.float32).astype(jnp.bfloat16)
    sums = jnp.dot(stacked.astype(jnp.bfloat16), upper, preferred_element_type=jnp.float32)
    before = jnp.zeros((8, 1), jnp.float32)
    ranks = []
    for i in range(parts):
        segment = sums[i * 8 : (i + 1) * 8]
        ranks.append(segment + before)
        before = before + segment[:, 127:128]
    place = jnp.concatenate(ranks, axis=1) - 1.0 + kinds.astype(jnp.float32) * per_language
    return jnp.sum(hot * place, axis=0, keepdims=True).astype(jnp.int32)


vmem = pl.BlockSpec(memory_space=pltpu.VMEM)
smem = pl.BlockSpec(memory_space=pltpu.SMEM)
hbm = pl.BlockSpec(memory_space=pltpu.HBM)


def call(kernel, name, in_specs, outs, scratch, limit, flops, transcendentals=0):
    return pl.pallas_call(
        kernel,
        in_specs=in_specs,
        out_specs=[spec for spec, _, _ in outs],
        out_shape=[jax.ShapeDtypeStruct(shape, dtype) for _, shape, dtype in outs],
        scratch_shapes=scratch,
        compiler_params=pltpu.CompilerParams(vmem_limit_bytes=limit * mib),
        cost_estimate=pl.CostEstimate(
            flops=flops, bytes_accessed=8 * mib, transcendentals=transcendentals
        ),
        name=name,
    )


def sort_kernel(
    first, here, ids, slot_in, queries, teacher, out_a, out_b, slot,
    select, block, moved_a, moved_b, in_sem, out_sem,
):
    tile = 512
    tiles = both // tile

    def read(j):
        source = queries if j < width // tile else teacher
        column = j * tile if j < width // tile else j * tile - width
        return pltpu.make_async_copy(
            source.at[:, pl.ds(column, tile)], block.at[j], in_sem.at[j]
        )

    def written(j):
        columns = pl.ds(j * tile, tile)
        return [
            pltpu.make_async_copy(moved_a.at[j], out_a.at[:, columns], out_sem.at[2 * j]),
            pltpu.make_async_copy(moved_b.at[j], out_b.at[:, columns], out_sem.at[2 * j + 1]),
        ]

    for j in range(tiles):
        read(j).start()
    if first:
        slots = slots_of(ids[...], here[0])
        slot[...] = jnp.broadcast_to(slots, (8, per_device))
    else:
        slots = slot_in[0:1, :]
        slot[...] = jnp.zeros((8, 128), jnp.int32)
    rows = lax.broadcasted_iota(jnp.int32, (per_language, per_device), 0)
    for half, number in enumerate((1, 3) if first else (2, 0)):
        hit = rows + number * per_language == slots
        select[pl.ds(half * per_language, per_language), :] = hit.astype(jnp.float32).astype(
            jnp.bfloat16
        )
    for j in range(tiles):
        read(j).wait()
        moved = jnp.dot(select[...], block[j], preferred_element_type=jnp.float32)
        moved_a[j] = moved[:per_language].astype(jnp.bfloat16)
        moved_b[j] = moved[per_language:].astype(jnp.bfloat16)
        for copy in written(j):
            copy.start()
    for j in range(tiles):
        for copy in written(j):
            copy.wait()


def sort_rows(here, ids, slot, queries, teacher):
    first = slot is None
    tiles = both // 512
    moved = pltpu.VMEM((tiles, per_language, 512), jnp.bfloat16)
    out = (hbm, (per_language, both), jnp.bfloat16)
    return call(
        functools.partial(sort_kernel, first),
        "sort_first" if first else "sort_rest",
        [smem, vmem, vmem, hbm, hbm],
        [out, out, (vmem, (8, per_device) if first else (8, 128), jnp.int32)],
        [
            pltpu.VMEM((2 * per_language, per_device), jnp.bfloat16),
            pltpu.VMEM((tiles, per_device, 512), jnp.bfloat16),
            moved,
            moved,
            pltpu.SemaphoreType.DMA((tiles,)),
            pltpu.SemaphoreType.DMA((2 * tiles,)),
        ],
        60 if first else 28,
        4 * per_language * per_device * both,
    )(here, ids, ids if first else slot, queries, teacher)


def kl_parts(value):
    high = value.astype(jnp.bfloat16).astype(jnp.float32)
    middle = (value - high).astype(jnp.bfloat16).astype(jnp.float32)
    low = value - high - middle
    lane = lax.broadcasted_iota(jnp.int32, value.shape, 1)
    parts = jnp.where(
        lane == 0, high, jnp.where(lane == 1, middle, jnp.where(lane == 2, low, 0.0))
    )
    return parts.astype(jnp.bfloat16)


def row_pass(quarter, scores, block, weights, kl):
    for i in range(4):
        local = pl.ds(pl.multiple_of(quarter * 64 + i * 16, 16), 16)
        own = scores[local, :]
        taught = block[local, :].astype(jnp.float32)
        top = jnp.max(own, axis=1, keepdims=True)
        taught_top = jnp.max(taught, axis=1, keepdims=True)
        grown = jnp.exp(own - top)
        total = jnp.sum(grown, axis=1, keepdims=True)
        shifted = taught - taught_top
        taught_grown = jnp.exp(shifted)
        taught_total = jnp.sum(taught_grown, axis=1, keepdims=True)
        cross = jnp.sum(taught_grown * (shifted - (own - top)), axis=1, keepdims=True)
        diverge = cross / taught_total - jnp.log(taught_total) + jnp.log(total)
        weights[local, :] = (
            grown * (student_scale / total) - taught_grown * (student_scale / taught_total)
        ).astype(jnp.bfloat16)
        kl[local, :] = jnp.broadcast_to(diverge, (16, 128))


def score_quarter(queries, base, quarter, passages, scores):
    columns = pl.ds(pl.multiple_of(quarter * 512, 512), 512)
    scores[:, columns] = (
        lax.dot_general(
            queries[pl.ds(base, per_language), pl.ds(0, width)],
            passages[columns, :],
            (((1,), (1,)), ((), ())),
            preferred_element_type=jnp.float32,
        )
        * student_scale
    )


def teacher_kernel(in0, in1, in2, store, queries, taught_out, parts, sems):
    rows = 3 * per_language

    def saved(number):
        block = pl.ds(number * per_language, per_language)
        behind = pl.ds(rows + number * per_language, per_language)
        return [
            pltpu.make_async_copy(taught_out.at[block], store.at[block], sems.at[number]),
            pltpu.make_async_copy(
                queries.at[block], store.at[behind, pl.ds(0, width)], sems.at[3 + number]
            ),
            pltpu.make_async_copy(
                parts.at[block], store.at[behind, pl.ds(width, extra)], sems.at[6 + number]
            ),
        ]

    for number, block in enumerate((in0, in1, in2)):

        def rows_of(i, carry, number=number, block=block):
            for part in range(4):
                local = pl.ds(pl.multiple_of(i * 64 + part * 16, 16), 16)
                placed = pl.ds(
                    pl.multiple_of(number * per_language + i * 64 + part * 16, 16), 16
                )
                queries[placed, :] = block[local, pl.ds(0, width)]
                taught = block[local, pl.ds(width, passages_all)].astype(jnp.float32)
                shifted = taught - jnp.max(taught, axis=1, keepdims=True)
                grown = jnp.exp(shifted)
                total = jnp.sum(grown, axis=1, keepdims=True)
                cross = jnp.sum(grown * shifted, axis=1, keepdims=True)
                taught_out[placed, :] = (grown * (student_scale / total)).astype(jnp.bfloat16)
                entropy = jnp.broadcast_to(cross / total - jnp.log(total), (16, 128))
                parts[placed, :] = kl_parts(entropy)
            return carry

        lax.fori_loop(0, 4, rows_of, 0)
        for copy in saved(number):
            copy.start()
    for number in range(3):
        for copy in saved(number):
            copy.wait()


def teacher_rows(blocks):
    rows = 3 * per_language
    return call(
        teacher_kernel,
        "teacher_rows",
        [vmem] * 3,
        [
            (hbm, (store_rows, passages_all), jnp.bfloat16),
            (vmem, (rows, width), jnp.bfloat16),
        ],
        [
            pltpu.VMEM((rows, passages_all), jnp.bfloat16),
            pltpu.VMEM((rows, extra), jnp.bfloat16),
            pltpu.SemaphoreType.DMA((9,)),
        ],
        40,
        mib,
        2 * mib,
    )(*blocks)


def student_pass(base, quarter, scores, taught_ref, parts, weights, kl):
    for i in range(4):
        local = pl.ds(pl.multiple_of(quarter * 64 + i * 16, 16), 16)
        placed = pl.ds(pl.multiple_of(base + quarter * 64 + i * 16, 16), 16)
        own = scores[local, :]
        taught = taught_ref[placed, :].astype(jnp.float32)
        shifted = own - jnp.max(own, axis=1, keepdims=True)
        grown = jnp.exp(shifted)
        total = jnp.sum(grown, axis=1, keepdims=True)
        cross = jnp.sum(taught * shifted, axis=1, keepdims=True)
        entropy = jnp.sum(
            parts[placed, pl.ds(width, extra)].astype(jnp.float32), axis=1, keepdims=True
        )
        diverge = entropy + jnp.log(total) - cross * (1.0 / student_scale)
        weights[placed, :] = (grown * (student_scale / total) - taught).astype(jnp.bfloat16)
        kl[placed, :] = jnp.broadcast_to(diverge, (16, 128))


def grad_columns(rows, columns, weights, passages, out):
    out[:, columns] = jnp.dot(
        weights[rows, :],
        passages[pl.ds(0, passages_all), columns],
        preferred_element_type=jnp.float32,
    ).astype(jnp.bfloat16)


def first_kernel(
    chunk_list, target_of, raw, store,
    weights, passages, kl, grad, raw_v, queries, taught, scores, other_scores, raw_sem, in_sem,
):
    def raw_copy(k):
        rows = pl.ds(pl.multiple_of(chunk_list[chunk_count + k], chunk_rows), chunk_rows)
        return pltpu.make_async_copy(raw.at[chunk_list[k], rows], raw_v.at[k], raw_sem.at[k])

    groups = chunk_list[3 * chunk_count]

    def start_group(g, carry):
        for c in range(group_chunks):
            raw_copy(g * group_chunks + c).start()
        return carry

    lax.fori_loop(0, groups, start_group, 0)
    copies = [
        pltpu.make_async_copy(
            store.at[pl.ds(3 * per_language, 3 * per_language), pl.ds(0, width + extra)],
            queries,
            in_sem.at[0],
        ),
        pltpu.make_async_copy(store.at[pl.ds(0, 3 * per_language)], taught, in_sem.at[1]),
    ]
    for copy in copies:
        copy.start()
    passages[pl.ds(0, 16), :] = jnp.zeros((16, width), jnp.bfloat16)

    def place(g, carry):
        for c in range(group_chunks):
            raw_copy(g * group_chunks + c).wait()
        start = pl.multiple_of((chunk_list[2 * chunk_count + g * group_chunks] // 16) * 16, 16)
        target = lax.broadcasted_iota(jnp.int32, (window, group_rows), 0)
        hit = target == target_of[pl.ds(g, 1), :] - start
        chosen = hit.astype(jnp.float32).astype(jnp.bfloat16)
        chunks = raw_v[pl.ds(g * group_chunks, group_chunks)].reshape(group_rows, width)
        moved = jnp.dot(chosen, chunks, preferred_element_type=jnp.float32).astype(jnp.bfloat16)
        head = passages[pl.ds(start, 16), :]
        passages[pl.ds(start, 16), :] = head + moved[:16]
        passages[pl.ds(start + 16, window - 16), :] = moved[16:]
        return carry

    lax.fori_loop(0, groups, place, 0)
    for copy in copies:
        copy.wait()

    def score_only(quarter, carry):
        score_quarter(queries, 0, quarter, passages, scores)
        return carry

    lax.fori_loop(0, 4, score_only, 0)
    held, free = scores, other_scores
    middle = pl.ds(per_language, per_language)
    for number in range(3):
        base = number * per_language

        def together(quarter, carry, base=base, held=held, free=free, last=number == 2):
            if last:
                columns = pl.ds(pl.multiple_of(quarter * 256, 256), 256)
                grad_columns(middle, columns, weights, passages, grad)
            else:
                score_quarter(queries, base + per_language, quarter, passages, free)
            student_pass(base, quarter, held, taught, queries, weights, kl)
            return carry

        lax.fori_loop(0, 4, together, 0)
        held, free = free, held
    grad[:, pl.ds(width, extra)] = kl_parts(kl[middle, :])


def first_blocks(chunk_list, raw, store):
    rows = 3 * per_language
    scores = pltpu.VMEM((per_language, passages_all), jnp.float32)
    return call(
        first_kernel,
        "first_blocks",
        [smem, vmem, hbm, hbm],
        [
            (vmem, (rows, passages_all), jnp.bfloat16),
            (vmem, (passages_all + window, width), jnp.bfloat16),
            (vmem, (rows, 128), jnp.float32),
            (vmem, (per_language, width + extra), jnp.bfloat16),
        ],
        [
            pltpu.VMEM((chunk_count, chunk_rows, width), jnp.bfloat16),
            pltpu.VMEM((rows, width + extra), jnp.bfloat16),
            pltpu.VMEM((rows, passages_all), jnp.bfloat16),
            scores,
            scores,
            pltpu.SemaphoreType.DMA((chunk_count,)),
            pltpu.SemaphoreType.DMA((2,)),
        ],
        40,
        6 * 1024**3,
        2 * mib,
    )(*chunk_list, raw, store)


def chunks_of(counts):
    number = (counts + chunk_rows - 1) // chunk_rows
    upto = jnp.arange(holders)[None, :] < jnp.arange(holders)[:, None]
    offsets = jnp.sum(jnp.where(upto, counts[None, :], 0), axis=1)
    firsts = jnp.sum(jnp.where(upto, number[None, :], 0), axis=1)
    index = jnp.arange(chunk_count)[:, None]
    mine = (index >= firsts[None, :]) & (index < (firsts + number)[None, :])
    row = (index - firsts[None, :]) * chunk_rows

    def pick(values):
        return jnp.sum(jnp.where(mine, values, 0), axis=1)

    holder = pick(jnp.arange(holders)[None, :] + 0 * row)
    used = pick(jnp.minimum(counts[None, :] - row, chunk_rows))
    place = jnp.where(used > 0, pick(offsets[None, :] + row), passages_all)
    slots = jnp.arange(chunk_rows)[None, :]
    groups = (jnp.sum(number) + group_chunks - 1) // group_chunks
    targets = jnp.where(slots < used[:, None], place[:, None] + slots, -1)
    return (
        jnp.concatenate([holder, pick(row), place, groups[None]]).astype(jnp.int32),
        targets.astype(jnp.int32).reshape(chunk_count // group_chunks, group_rows),
    )


def last_kernel(
    core, passages, before, queries, block, weights, send, keep, kl,
    own, teacher, scores, total, in_sem,
):
    own_copy = pltpu.make_async_copy(block.at[:, pl.ds(0, width)], own, in_sem.at[0])
    teacher_copy = pltpu.make_async_copy(
        block.at[:, pl.ds(width, passages_all)], teacher, in_sem.at[1]
    )
    own_copy.start()
    teacher_copy.start()
    own_copy.wait()

    def score_only(quarter, carry):
        score_quarter(own, 0, quarter, passages, scores)
        return carry

    lax.fori_loop(0, 4, score_only, 0)
    teacher_copy.wait()
    contract = (((0,), (0,)), ((), ()))

    def together(quarter, carry):
        row_pass(quarter, scores, teacher, weights, kl)
        columns = pl.ds(pl.multiple_of(quarter * 512, 512), 512)
        total[columns, :] = lax.dot_general(
            before[:, columns],
            queries[...],
            contract,
            preferred_element_type=jnp.float32,
        )
        return carry

    lax.fori_loop(0, 4, together, 0)
    even = core[0] == 0

    def reduce(j, carry):
        columns = pl.ds(pl.multiple_of(j * 256, 256), 256)
        grad = lax.dot_general(
            weights[:, columns],
            own[...],
            contract,
            preferred_element_type=jnp.float32,
        )
        grad = (grad + total[columns, :]).astype(jnp.bfloat16)
        for part in range(2):
            upper = grad[part * 128 : part * 128 + 64]
            lower = grad[part * 128 + 64 : part * 128 + 128]
            rows = pl.ds(pl.multiple_of(j * 128 + part * 64, 64), 64)
            keep[rows, :] = jnp.where(even, upper, lower)
            send[rows, :] = jnp.where(even, lower, upper)
        return carry

    lax.fori_loop(0, passages_all // 256, reduce, 0)


def last_block(core, passages, weights, queries, block):
    half = (vmem, (passages_all // 2, width), jnp.bfloat16)
    return call(
        last_kernel,
        "last_block",
        [smem] + [vmem] * 3 + [hbm],
        [
            (vmem, (per_language, passages_all), jnp.bfloat16),
            half,
            half,
            (vmem, (per_language, 128), jnp.float32),
        ],
        [
            pltpu.VMEM((per_language, width), jnp.bfloat16),
            pltpu.VMEM((per_language, passages_all), jnp.bfloat16),
            pltpu.VMEM((per_language, passages_all), jnp.float32),
            pltpu.VMEM((passages_all, width), jnp.float32),
            pltpu.SemaphoreType.DMA((2,)),
        ],
        20,
        6 * 1024**3,
        mib,
    )(core, passages, weights, queries, block)


def query_kernel(places, passages, *refs):
    for number, place in enumerate(places):
        weights, kl = refs[2 * number], refs[2 * number + 1]
        out = refs[2 * len(places) + number]
        rows = pl.ds(place * per_language, per_language)

        def step(half, carry, rows=rows, weights=weights, out=out):
            columns = pl.ds(pl.multiple_of(half * 512, 512), 512)
            grad_columns(rows, columns, weights, passages, out)
            return carry

        lax.fori_loop(0, 2, step, 0)
        out[:, pl.ds(width, extra)] = kl_parts(kl[rows, :])


def query_grads(places, passages, *arrays):
    return call(
        functools.partial(query_kernel, places),
        "query_grads",
        [vmem] * (1 + len(arrays)),
        [(vmem, (per_language, width + extra), jnp.bfloat16)] * len(places),
        [],
        8,
        len(places) * 1024**3,
    )(passages, *arrays)


def pair_kernel(keep, other, out):
    def step(i, carry):
        rows = pl.ds(pl.multiple_of(i * 64, 64), 64)
        out[rows, :] = (
            keep[rows, :].astype(jnp.float32) + other[rows, :].astype(jnp.float32)
        ).astype(jnp.bfloat16)
        return carry

    lax.fori_loop(0, passages_all // 128, step, 0)


def pair_sum(keep, other):
    return call(
        pair_kernel, "pair_sum", [vmem] * 2, [(vmem, keep.shape, jnp.bfloat16)], [], 8, mib
    )(keep, other)[0]


def selection(slot, numbers, select):
    rows = lax.broadcasted_iota(jnp.int32, (per_language, per_device), 0)
    for half, number in enumerate(numbers):
        hit = rows + number * per_language == slot[0:1, :]
        select[half * per_language : (half + 1) * per_language, :] = hit.astype(
            jnp.float32
        ).astype(jnp.bfloat16)


def joined(select, blocks, columns):
    part = None
    for half, block in enumerate(blocks):
        term = lax.dot_general(
            select[half * per_language : (half + 1) * per_language, :],
            block[:, columns],
            (((0,), (0,)), ((), ())),
            preferred_element_type=jnp.float32,
        )
        part = term if part is None else part + term
    return part


def restore_first_kernel(slot, in0, in1, in3, out, select):
    selection(slot, (0, 1, 3), select)
    blocks = (in0, in1, in3)

    def step(j, carry):
        columns = pl.ds(pl.multiple_of(j * 256, 256), 256)
        out[:, columns] = joined(select, blocks, columns).astype(jnp.bfloat16)
        return carry

    lax.fori_loop(0, width // 256, step, 0)
    columns = pl.ds(width, extra)
    out[:, columns] = joined(select, blocks, columns).astype(jnp.bfloat16)


def restore_last_kernel(slot, begun, in2, grads_out, kl, select, grads, out_sem):
    selection(slot, (2,), select)

    def written(j):
        columns = pl.ds(pl.multiple_of(j * 256, 256), 256)
        return pltpu.make_async_copy(grads.at[j], grads_out.at[:, columns], out_sem.at[j])

    def step(j, carry):
        columns = pl.ds(pl.multiple_of(j * 256, 256), 256)
        added = joined(select, (in2,), columns) + begun[:, columns].astype(jnp.float32)
        grads[j] = added.astype(jnp.bfloat16)
        written(j).start()
        return carry

    lax.fori_loop(0, width // 256, step, 0)
    columns = pl.ds(width, extra)
    parts = joined(select, (in2,), columns) + begun[:, columns].astype(jnp.float32)
    column = jnp.sum(parts, axis=1, keepdims=True)
    kl[...] = jnp.transpose(jnp.broadcast_to(column, (per_device, 128)))[:1]
    for j in range(width // 256):
        written(j).wait()


def restore_first(slot, blocks):
    return call(
        restore_first_kernel,
        "restore_first",
        [vmem] * 4,
        [(vmem, (per_device, width + extra), jnp.bfloat16)],
        [pltpu.VMEM((3 * per_language, per_device), jnp.bfloat16)],
        12,
        15 * 1024**3,
    )(slot, *blocks)[0]


def restore_last(slot, begun, block):
    return call(
        restore_last_kernel,
        "restore_last",
        [vmem] * 3,
        [
            (hbm, (per_device, width), jnp.bfloat16),
            (vmem, (1, per_device), jnp.float32),
        ],
        [
            pltpu.VMEM((per_language, per_device), jnp.bfloat16),
            pltpu.VMEM((width // 256, per_device, 256), jnp.bfloat16),
            pltpu.SemaphoreType.DMA((width // 256,)),
        ],
        12,
        1024**3,
    )(slot, begun, block)


def sum_kernel(pieces, out):
    for i in range(4):
        rows = slice(16 * i, 16 * (i + 1))
        total = pieces[0, rows, :].astype(jnp.float32)
        for j in range(1, pieces.shape[0]):
            total = total + pieces[j, rows, :].astype(jnp.float32)
        out[rows, :] = total.astype(jnp.bfloat16)


def sum_pieces(pieces):
    return call(
        sum_kernel, "sum_pieces", [vmem], [(vmem, (64, width), jnp.bfloat16)], [], 8, mib
    )(pieces)[0]


def shift(array, by):
    pairs = [(i, (i + by) % languages) for i in range(languages)]
    return lax.ppermute(array, "x", pairs)


def on_device(queries, bucket_ids, raw_passages, counts, teacher):
    group = ("y", "z", "c")
    here = lax.axis_index("x").astype(jnp.int32).reshape(1)
    core = lax.axis_index("c").astype(jnp.int32).reshape(1)
    all_raw = lax.all_gather(raw_passages[0], group, axis=0, tiled=True)
    ids = bucket_ids[0]
    out1, out3, slot = sort_rows(here, ids, None, queries[0, 0], teacher[0, 0])
    in1, in3 = shift(out1, 1), shift(out3, 3)
    out2, in0, _ = sort_rows(here, ids, slot, queries[0, 0], teacher[0, 0])
    held_counts, in0, out2 = lax.optimization_barrier((counts, in0, out2))
    holder_counts = lax.all_gather(held_counts[0], group, axis=0, tiled=True)
    chunk_list = chunks_of(holder_counts)
    out2, in1, in3, chunk_list = lax.optimization_barrier((out2, in1, in3, chunk_list))
    in2 = shift(out2, 2)
    store, moved = teacher_rows((in0, in1, in3))
    all_raw, store, moved = lax.optimization_barrier((all_raw, store, moved))
    weights, passages, kl, back1 = first_blocks(chunk_list, all_raw, store)
    last_weights, send, keep, last_kl = last_block(core, passages, weights, moved, in2)
    other = lax.ppermute(send, "c", [(0, 1), (1, 0)])
    (back3,) = query_grads((2,), passages, weights, kl)
    keep, back3 = lax.optimization_barrier((keep, back3))
    home1, home3 = shift(back1, -1), shift(back3, -3)
    paired = pair_sum(keep, other)
    spread = lax.all_to_all(
        paired.reshape(16, 64, width), ("y", "z"), split_axis=0, concat_axis=0, tiled=True
    )
    paired, weights, last_weights = lax.optimization_barrier((paired, weights, last_weights))
    back2, back0 = query_grads((0, 0), passages, last_weights, last_kl, weights, kl)
    home2 = shift(back2, -2)
    grad_passages = sum_pieces(spread)
    begun = restore_first(slot, (back0, home1, home3))
    grad_queries, kl_rows = restore_last(slot, begun, home2)
    return (grad_queries[None, None], grad_passages[None], kl_rows[None])


def solution(mesh):
    split = Mesh(mesh.devices.reshape(4, 4, 4, 2), ("x", "y", "z", "c"))
    group = ("y", "z", "c")
    in_specs = (
        P("x", group, None, None),
        P("x", group, None),
        P("x", group, None, None),
        P("x", group),
        P("x", group, None, None),
    )
    out_specs = (P("x", group, None, None), P("x", group, None), P("x", group, None))
    return jax.shard_map(
        on_device, mesh=split, in_specs=in_specs, out_specs=out_specs, check_vma=False
    )
```
